32 devices in a mesh: dp: 8 (over z, y), tensor: 4 (over x, core).
Axes of the slice: x: 2, y: 2, z: 4, core: 2. Of those that a mesh axis runs over, the one named last changes fastest.
Arguments:
- dense: bfloat16 [1536, 2048], P('dp'), may hold values from -8 to 8
- bottom_weight: bfloat16 [2048, 16384], P(None, 'tensor'), may hold values from -0.125 to 0.125
- bottom_bias: float32 [16384], P('tensor'), may hold values from -3 to 3
- cross_blocks: bfloat16 [40, 512, 512], P('tensor', 'dp'), may hold values from -0.25 to 0.25
- cross_bias: float32 [16384], P('tensor'), may hold values from -3 to 3
- cotangent: bfloat16 [1536, 16384], P('dp', 'tensor'), may hold values from -6 to 6
- in_blocks: int32 [4, 10], replicated, may hold values from 0 to 31, as said below
- out_blocks: int32 [4, 10], replicated, may hold values from 0 to 31, as said below
- live_slots: int32 [4], replicated, may hold values from 2 to 10, as said below
Outputs:
- cross_out: bfloat16 [1536, 16384], P('dp', 'tensor')
- grad_bottom: float32 [2048, 16384], P('dp', 'tensor')
- grad_bias_bottom: float32 [16384], P('tensor')
- grad_blocks: float32 [40, 512, 512], P('tensor', 'dp')
- grad_bias: float32 [16384], P('tensor')
The draws below stay inside these ranges and needn't reach their ends.
Inputs may be any that keep to these rules, and one draw needn't show every extreme that they name: `in_blocks`: among the live slots of one tensor device, at most 3 have input blocks held by any one tensor device (blocks s * 16384 / (512 * 4) onward for device s), and this most is reached in every draw. `out_blocks`: among the live slots of one tensor device, at most 3 have output blocks held by any one tensor device, and this most is reached in every draw. `live_slots`: some tensor device has all 10 slots live.
All inputs are finite; a program needn't handle non-finite values.
Results may differ from the reference program's by a relative error of at most 0.014.
Values may be sent and summed in bfloat16 or wider, within the bound.
No kernel may reach another device: no remote copies, remote signals or barrier semaphores. Data moves between devices by JAX's collectives and lax.ppermute only.
A program may use at most 128 MiB of HBM per device.

```python
import jax
import jax.numpy as jnp
from jax import lax

DENSE = 2048
WIDTH = 16384
BLK = 512
B_DEV = 192
SLOTS = 10
SLOTS_ALL = 40
BATCH = 1536
N_DP = 8
N_TENSOR = 4


def slot_tables(key):
    per_device = WIDTH // BLK // N_TENSOR
    subkeys = jax.random.split(jax.random.fold_in(key, 7), 6)
    perm_out = jax.vmap(lambda subkey: jax.random.permutation(subkey, N_TENSOR))(jax.random.split(subkeys[0], N_TENSOR))
    perm_in = jax.vmap(lambda subkey: jax.random.permutation(subkey, N_TENSOR))(jax.random.split(subkeys[1], N_TENSOR))
    position = jnp.arange(SLOTS)
    owner_out = perm_out[:, position % N_TENSOR]
    offsets = jax.random.randint(subkeys[2], (N_TENSOR, 1), 0, per_device)
    local_out = (offsets + position[None, :] // N_TENSOR) % per_device
    owner_in = perm_in[:, position % N_TENSOR]
    local_in = jax.random.randint(subkeys[3], (N_TENSOR, SLOTS), 0, per_device)
    counts = jax.random.randint(subkeys[4], (N_TENSOR,), 2, SLOTS + 1)
    busiest = jax.random.randint(subkeys[5], (), 0, N_TENSOR)
    counts = jnp.where(jnp.arange(N_TENSOR) == busiest, SLOTS, counts)
    inputs = (owner_in * per_device + local_in).astype(jnp.int32)
    outputs = (owner_out * per_device + local_out).astype(jnp.int32)
    return (inputs, outputs, counts.astype(jnp.int32))


def draw_in_blocks(key, part):
    return slot_tables(key)[0]


def draw_out_blocks(key, part):
    return slot_tables(key)[1]


def draw_live_slots(key, part):
    return slot_tables(key)[2]


def spiked(array, rng, source, target, shards_of, factor):
    def block_of(dim):
        return (jnp.arange(array.shape[dim]) // (array.shape[dim] // shards_of)).reshape((-1,) + (1,) * (array.ndim - 1 - dim))

    near = jax.random.permutation(rng, shards_of)[block_of(target)]
    far = (block_of(target) + shards_of // 2) % shards_of
    return jnp.where((block_of(source) == near) | (block_of(source) == far), factor * array, array)


def steps_of(rng, shape, pieces, low, largest):
    factor_of, own = 1.0, jax.random.fold_in(rng, 6)
    for dim, parts in pieces:
        steps = jnp.exp(jax.random.uniform(jax.random.fold_in(own, dim), (parts,), jnp.float32, low / len(pieces), largest / len(pieces)))
        factor_of = factor_of * jnp.repeat(steps, shape[dim] // parts).reshape([-1 if axis == dim else 1 for axis in range(len(shape))])
    return factor_of


def bell_draw(stream_key, shape, spread, limit, cuts=(), kind=jnp.bfloat16):
    entries = jax.random.normal(stream_key, shape, jnp.float32) * spread
    if len(cuts) > 0:
        entries = steps_of(stream_key, shape, cuts, -0.22, 0.18) * entries
    return jnp.clip(entries, min=-limit, max=limit).astype(kind)


def gaussian_with(stream_key, extent, deviation, bound, pieces, heavy, dtype=jnp.bfloat16):
    values = deviation * jax.random.normal(stream_key, extent, jnp.float32)
    if pieces:
        values = values * steps_of(stream_key, extent, pieces, -0.22, 0.18)
    return jnp.clip(spiked(values, jax.random.fold_in(stream_key, 3), *heavy), -bound, bound).astype(dtype)


def setup_inputs(seed: int = 0) -> dict:
    splits = jax.random.split(jax.random.key(seed), 10)
    dense = gaussian_with(splits[0], (BATCH, DENSE), 1.0, 8.0, ((0, 8),), (0, 1, 8, 2.0))
    bottom_weight = bell_draw(splits[1], (DENSE, WIDTH), DENSE ** -0.5, 0.125, ((1, 4),))
    bottom_bias = bell_draw(splits[2], (WIDTH,), 0.5, 3.0, ((0, 4),), jnp.float32)
    cross_blocks = bell_draw(splits[3], (SLOTS_ALL, BLK, BLK), BLK ** -0.5, 0.25, ((0, 4), (1, 8)))
    cross_bias = bell_draw(splits[4], (WIDTH,), 0.5, 3.0, ((0, 4),), jnp.float32)
    cotangent = bell_draw(splits[5], (BATCH, WIDTH), 1.0, 6.0, ((0, 8), (1, 4)))
    in_blocks = draw_in_blocks(jax.random.fold_in(splits[9], 71), 0)
    out_blocks = draw_out_blocks(jax.random.fold_in(splits[9], 71), 0)
    live_slots = draw_live_slots(jax.random.fold_in(splits[9], 71), 0)
    return {"dense": dense, "bottom_weight": bottom_weight, "bottom_bias": bottom_bias, "cross_blocks": cross_blocks, "cross_bias": cross_bias, "cotangent": cotangent, "in_blocks": in_blocks, "out_blocks": out_blocks, "live_slots": live_slots}


def reference(dense, bottom_weight, bottom_bias, cross_blocks, cross_bias, cotangent, in_blocks, out_blocks, live_slots):
    preact = jnp.dot(dense, bottom_weight, preferred_element_type=jnp.float32) + bottom_bias
    start = jax.nn.silu(preact).astype(jnp.bfloat16)
    start_wide = start.astype(jnp.float32)
    inputs_all = in_blocks.reshape(-1).astype(jnp.int32)
    outputs_all = out_blocks.reshape(-1).astype(jnp.int32)
    alive = (jnp.arange(SLOTS)[None, :] < live_slots[:, None]).reshape(-1).astype(jnp.float32)

    def forward_slot(mixed, item):
        column, target, switch, weight_block = item
        taken = lax.dynamic_slice_in_dim(start, column * BLK, BLK, 1)
        product = jnp.dot(taken, weight_block, preferred_element_type=jnp.float32).astype(jnp.bfloat16)
        product = lax.optimization_barrier(product)
        product = product.astype(jnp.float32) * switch
        current = lax.dynamic_slice_in_dim(mixed, target * BLK, BLK, 1)
        mixed = lax.dynamic_update_slice_in_dim(mixed, current + product, target * BLK, 1)
        return mixed, None

    mixed, unused = lax.scan(forward_slot, jnp.zeros((BATCH, WIDTH), jnp.float32), (inputs_all, outputs_all, alive, cross_blocks))
    mixed = mixed + cross_bias
    cross_out = (start_wide * mixed + start_wide).astype(jnp.bfloat16)
    cot_wide = cotangent.astype(jnp.float32)
    grad_mixed = cot_wide * start_wide
    grad_mixed_low = grad_mixed.astype(jnp.bfloat16)
    grad_bias = jnp.sum(grad_mixed, axis=0)

    def backward_slot(grad_start, item):
        column, target, switch, weight_block = item
        taken = lax.dynamic_slice_in_dim(start, column * BLK, BLK, 1)
        upstream = lax.dynamic_slice_in_dim(grad_mixed_low, target * BLK, BLK, 1)
        back = jnp.dot(upstream, weight_block.T, preferred_element_type=jnp.float32).astype(jnp.bfloat16)
        back = lax.optimization_barrier(back)
        back = back.astype(jnp.float32) * switch
        current = lax.dynamic_slice_in_dim(grad_start, column * BLK, BLK, 1)
        grad_start = lax.dynamic_update_slice_in_dim(grad_start, current + back, column * BLK, 1)
        taken_groups = taken.astype(jnp.float32).reshape(N_DP, B_DEV, BLK)
        upstream_groups = upstream.astype(jnp.float32).reshape(N_DP, B_DEV, BLK)
        partial_grads = jnp.einsum("nbi,nbj->nij", taken_groups, upstream_groups, precision=lax.Precision.HIGHEST).astype(jnp.bfloat16)
        partial_grads = lax.optimization_barrier(partial_grads)
        block_grad = jnp.sum(partial_grads.astype(jnp.float32), axis=0) * switch
        return grad_start, block_grad

    grad_start, grad_blocks = lax.scan(backward_slot, jnp.zeros((BATCH, WIDTH), jnp.float32), (inputs_all, outputs_all, alive, cross_blocks))
    grad_start = grad_start + cot_wide * mixed + cot_wide
    sigma = jax.nn.sigmoid(preact)
    grad_pre = grad_start * sigma * (1.0 + preact * (1.0 - sigma))
    grad_pre_low = grad_pre.astype(jnp.bfloat16)
    grad_bias_bottom = jnp.sum(grad_pre, axis=0)

    def bottom_group(total, item):
        dense_group, grad_group = item
        partial_grad = jnp.dot(dense_group.T, grad_group, preferred_element_type=jnp.float32).astype(jnp.bfloat16)
        partial_grad = lax.optimization_barrier(partial_grad)
        return total + partial_grad.astype(jnp.float32), None

    grad_bottom, unused = lax.scan(bottom_group, jnp.zeros((DENSE, WIDTH), jnp.float32), (dense.reshape(N_DP, B_DEV, DENSE), grad_pre_low.reshape(N_DP, B_DEV, WIDTH)))
    return cross_out, grad_bottom, grad_bias_bottom, grad_blocks, grad_bias
```

```python
import functools

import jax
import jax.numpy as jnp
import numpy as np
from jax import lax
from jax.experimental import pallas as pl
from jax.experimental.pallas import tpu as pltpu
from jax.sharding import Mesh, PartitionSpec as P

BLK = 512
SLOTS = 10
BF = jnp.bfloat16
F32 = jnp.float32
ANY = pl.BlockSpec(memory_space=pl.ANY)
VMEM = pl.BlockSpec(memory_space=pltpu.VMEM)
LIMIT = 56 * 1024 * 1024


def params(semantics=None):
    return pltpu.CompilerParams(vmem_limit_bytes=LIMIT, dimension_semantics=semantics)


def dot(a, b, dims):
    return lax.dot_general(a, b, (dims, ((), ())), preferred_element_type=F32)


def ring_order(n):
    return list(range(0, n, 2)) + list(range(n - 1 - (n % 2), 0, -2))


def ring_hop(n):
    order = ring_order(n)
    return [(order[p], order[(p + 1) % n]) for p in range(n)]


def ring_from(axis, n, step):
    order = ring_order(n)
    me = lax.axis_index(axis)
    behind = [0] * n
    for p in range(n):
        behind[order[p]] = order[(p - step) % n]
    result = jnp.int32(behind[0])
    for i in range(1, n):
        result = jnp.where(me == i, behind[i], result)
    return result


def ring_gather(value, axis, n):
    pieces = [value]
    for _ in range(n - 1):
        pieces.append(lax.ppermute(pieces[-1], axis, ring_hop(n)))
    return pieces


def local_of(block, per_device):
    return lax.div(block, jnp.int32(per_device))


def owner_walk(me, ref, live, groups, per_device, visit):
    total = jnp.int32(0)
    for kk in range(groups):
        source = me ^ kk
        alive = live[source]
        rank = jnp.int32(0)
        for k in range(SLOTS):
            hit = (k < alive) & (local_of(ref[source, k], per_device) == me)

            @pl.when(hit)
            def _(source=source, k=k, total=total, rank=rank, kk=kk):
                visit(kk, source, k, total, rank)

            step = hit.astype(jnp.int32)
            total = total + step
            rank = rank + step
    return total


def tensor_index():
    return lax.axis_index("x") * lax.axis_size("core") + lax.axis_index("core")


def pack_kernel(groups, per_device, inb, outb, live, w, packed, count):
    me = tensor_index()
    for g in range(groups):
        count[g] = 0
    alive = live[me]

    def body(k, carry):
        to = me ^ local_of(outb[me, k], per_device)

        @pl.when(k < alive)
        def _():
            packed[to, count[to]] = w[k]
            count[to] = count[to] + 1

        return carry

    lax.fori_loop(0, SLOTS, body, 0)


def compact_kernel(groups, per_device, inb, outb, live, *refs):
    pieces, out = refs[:groups], refs[groups]
    me = tensor_index()

    def visit(kk, source, k, total, rank):
        out[total] = pieces[kk][rank]

    owner_walk(me, outb, live, groups, per_device, visit)


def expand_kernel(groups, per_device, inb, outb, live, grads, packed):
    me = tensor_index()

    def visit(kk, source, k, total, rank):
        packed[kk, rank] = grads[total]

    owner_walk(me, outb, live, groups, per_device, visit)


def return_kernel(groups, per_device, inb, outb, live, *refs):
    pieces, out, count = refs[:groups], refs[groups], refs[groups + 1]
    me = tensor_index()
    for g in range(groups):
        count[g] = 0
    alive = live[me]

    def body(k, carry):
        to = me ^ local_of(outb[me, k], per_device)

        @pl.when(k < alive)
        def _():
            for g in range(groups):

                @pl.when(to == g)
                def _(g=g):
                    out[k] = pieces[g][count[g]].astype(F32)

            count[to] = count[to] + 1

        @pl.when(k >= alive)
        def _():
            out[k] = jnp.zeros(out.shape[1:], F32)

        return carry

    lax.fori_loop(0, SLOTS, body, 0)


def bottom_kernel(dense, weight, bias, cot, start, low, slope, bias_sum):
    pre = jnp.dot(dense[...], weight[...], preferred_element_type=F32) + bias[...]
    sigma = 1.0 / (1.0 + jnp.exp(-pre))
    begin = (pre * sigma).astype(BF)
    start[0] = begin
    grad = cot[...].astype(F32) * begin.astype(F32)
    low[0] = grad.astype(BF)
    slope[0] = sigma * (1.0 + pre * (1.0 - sigma))
    bias_sum[...] = jnp.sum(grad, axis=0, keepdims=True)


def fetch_inputs(groups, per_device, inb, outb, live, pieces, sbuf, tin, tout, sem):
    me = tensor_index()

    def visit(kk, source, k, total, rank):
        block = inb[source, k]
        owner = local_of(block, per_device)
        tin[total] = block + ((me ^ owner) - owner) * per_device
        tout[total] = outb[source, k] - me * per_device

    total = owner_walk(me, outb, live, groups, per_device, visit)

    def issue(j, carry):
        which = local_of(tin[j], per_device)
        col = tin[j] - which * per_device
        for g in range(groups):

            @pl.when(which == g)
            def _(g=g):
                pltpu.make_async_copy(pieces[g].at[col], sbuf.at[j], sem.at[j]).start()

        return carry

    lax.fori_loop(0, total, issue, 0)
    return total


def wait_input(pieces, sbuf, sem, j):
    pltpu.make_async_copy(pieces[0].at[0], sbuf.at[j], sem.at[j]).wait()


def block_grad_kernel(groups, per_device, ny, inb, outb, live, *refs):
    pieces = refs[:groups]
    low, out, sbuf, tmp, tin, tout, sem = refs[groups:]
    total = fetch_inputs(groups, per_device, inb, outb, live, pieces, sbuf, tin, tout, sem)
    rows = out.shape[2]

    def body(j, carry):
        wait_input(pieces, sbuf, sem, j)
        tmp[...] = dot(sbuf[j], low[tout[j]], ((0,), (0,))).astype(BF)
        for d in range(out.shape[0]):
            out[d, j] = tmp[d * rows : (d + 1) * rows, :]
        return carry

    lax.fori_loop(0, total, body, 0)


def cross_kernel(groups, per_device, nx, nz, ny, inb, outb, live, *refs):
    pieces = refs[:groups]
    low, start, cot, bias = refs[groups : groups + 4]
    shards = refs[groups + 4 : groups + 4 + nz * ny]
    cross, base, back_same, back_other = refs[groups + 4 + nz * ny : groups + 8 + nz * ny]
    wbuf, sbuf, mixed, acc, tin, tout, sem, wsem = refs[groups + 8 + nz * ny :]
    rows = shards[0].shape[1]
    copies = []
    for sz in range(nz):
        for sy in range(ny):
            d = ring_from("z", nz, sz) * ny + ring_from("y", ny, sy)
            place = pl.ds(pl.multiple_of(d * rows, rows), rows)
            copies.append(
                pltpu.make_async_copy(
                    shards[sz * ny + sy], wbuf.at[:, place, :], wsem.at[sz * ny + sy]
                )
            )
    for copy in copies:
        copy.start()
    total = fetch_inputs(groups, per_device, inb, outb, live, pieces, sbuf, tin, tout, sem)

    def clear(i, carry):
        acc[i] = jnp.zeros(acc.shape[1:], F32)
        return carry

    lax.fori_loop(0, acc.shape[0], clear, 0)

    def begin(b, carry):
        mixed[b] = jnp.broadcast_to(bias[b], mixed.shape[1:])
        return carry

    lax.fori_loop(0, per_device, begin, 0)
    for copy in copies:
        copy.wait()

    def body(j, carry):
        wait_input(pieces, sbuf, sem, j)
        part = dot(sbuf[j], wbuf[j], ((1,), (0,))).astype(BF).astype(F32)
        mixed[tout[j]] = mixed[tout[j]] + part
        back = dot(low[tout[j]], wbuf[j], ((1,), (1,))).astype(BF).astype(F32)
        acc[tin[j]] = acc[tin[j]] + back
        return carry

    lax.fori_loop(0, total, body, 0)
    for b in range(per_device):
        wide = start[b].astype(F32)
        mix = mixed[b]
        c = cot[:, b * BLK : (b + 1) * BLK].astype(F32)
        cross[:, b * BLK : (b + 1) * BLK] = (wide * mix + wide).astype(BF)
        base[b] = c * mix + c + acc[b]

    mx, core = lax.axis_index("x"), lax.axis_index("core")
    for sx in range(nx):
        rel = (mx ^ ring_from("x", nx, sx)) * 2

        def spill(b, carry, sx=sx, rel=rel):
            if sx > 0:
                back_same[sx - 1, b] = acc[rel * per_device + b].astype(BF)
            back_other[sx, b] = acc[(rel + 1) * per_device + b].astype(BF)
            return carry

        lax.fori_loop(0, per_device, spill, 0)


def pre_kernel(base, here, far, slope, low, bias_sum):
    grad = base[0] + here[0].astype(F32) + far[0].astype(F32)
    grad = grad * slope[0]
    low[0] = grad.astype(BF)
    bias_sum[...] = jnp.sum(grad, axis=0, keepdims=True)


def weight_grad_kernel(nz, ny, rows, *refs):
    grads, dense = refs[:nz], refs[nz : 2 * nz]
    own, send = refs[2 * nz :]
    for sy in range(ny):
        y = ring_from("y", ny, sy)
        cols = pl.ds(pl.multiple_of(y * rows, rows), rows)
        total = None
        for s in range(nz):
            term = dot(dense[s][:, cols], grads[s][0], ((0,), (0,)))
            total = term if total is None else total + term
        if sy == 0:
            own[...] = total
        else:
            send[sy - 1] = total.astype(BF)


def final_kernel(chunks, width, *refs):
    own, far, out = refs[:chunks], refs[chunks : 2 * chunks], refs[2 * chunks]
    for c in range(chunks):
        out[:, c * width : (c + 1) * width] = own[c][...] + far[c][...].astype(F32)


def on_device(sizes, *args):
    dense, bottom_weight, bottom_bias, cross_blocks, cross_bias, cotangent, inb, outb, live = args
    nz, ny, nx = sizes
    groups = nx * 2
    row_count, depth = dense.shape
    local_width = bottom_weight.shape[1]
    per_device = local_width // BLK
    capacity = -(-SLOTS // groups)
    width = groups * capacity
    rows = cross_blocks.shape[1]
    n_dp = nz * ny
    out_rows = depth // n_dp
    smem = pltpu.SMEM
    tables = (inb, outb, live)
    sds = jax.ShapeDtypeStruct

    def table_call(kernel, n_in, out_shape, scratch=(), in_specs=None, out_specs=None):
        single = not isinstance(out_shape, (tuple, list))
        return pl.pallas_call(
            kernel,
            out_shape=out_shape,
            grid_spec=pltpu.PrefetchScalarGridSpec(
                num_scalar_prefetch=3,
                grid=(),
                in_specs=in_specs or [VMEM] * n_in,
                out_specs=out_specs or (VMEM if single else [VMEM] * len(out_shape)),
                scratch_shapes=list(scratch),
            ),
            compiler_params=params(),
        )

    def swap(value, kk):
        return lax.ppermute(value, ("x", "core"), [(i, i ^ kk) for i in range(groups)])

    packed = table_call(
        functools.partial(pack_kernel, groups, per_device),
        1,
        sds((groups, capacity, rows, BLK), BF),
        [pltpu.SMEM((groups,), jnp.int32)],
    )(*tables, cross_blocks)
    moved = [packed[0]] + [swap(packed[kk], kk) for kk in range(1, groups)]
    shard = table_call(
        functools.partial(compact_kernel, groups, per_device),
        groups,
        sds((width, rows, BLK), BF),
    )(*tables, *moved)

    block = lambda dtype: pl.BlockSpec((1, row_count, BLK), lambda i: (i, 0, 0))
    line = pl.BlockSpec((1, BLK), lambda i: (0, i))
    wide = sds((per_device, row_count, BLK), F32)
    narrow = sds((per_device, row_count, BLK), BF)
    start, low, slope, bias_mixed = pl.pallas_call(
        bottom_kernel,
        grid=(per_device,),
        in_specs=[
            pl.BlockSpec((row_count, depth), lambda i: (0, 0)),
            pl.BlockSpec((depth, BLK), lambda i: (0, i)),
            line,
            pl.BlockSpec((row_count, BLK), lambda i: (0, i)),
        ],
        out_specs=[block(BF), block(BF), block(F32), line],
        out_shape=[narrow, narrow, wide, sds((1, local_width), F32)],
        compiler_params=params(("arbitrary",)),
    )(dense, bottom_weight, bottom_bias.reshape(1, -1), cotangent)

    if nx == 2:
        far = lax.ppermute(start, "x", [(0, 1), (1, 0)])
        flip = [(0, 1), (1, 0)]
        pieces = [start, lax.ppermute(start, "core", flip), far, lax.ppermute(far, "core", flip)]
    else:
        pieces = [start] + [swap(start, kk) for kk in range(1, groups)]

    shards = []
    for piece in ring_gather(shard, "z", nz):
        shards += ring_gather(piece, "y", ny)

    tabs = [smem((width,), jnp.int32), smem((width,), jnp.int32), pltpu.SemaphoreType.DMA((width,))]
    sbuf = pltpu.VMEM((width, row_count, BLK), BF)
    block_grads = table_call(
        functools.partial(block_grad_kernel, groups, per_device, ny),
        groups + 1,
        sds((n_dp, width, rows, BLK), BF),
        [sbuf, pltpu.VMEM((BLK, BLK), BF)] + tabs,
        in_specs=[ANY] * groups + [VMEM],
    )(*tables, *pieces, low)
    summed = lax.psum_scatter(block_grads, ("z", "y"), scatter_dimension=0, tiled=True)
    summed = summed.reshape(width, rows, BLK)
    returned = table_call(
        functools.partial(expand_kernel, groups, per_device),
        1,
        sds((groups, capacity, rows, BLK), BF),
    )(*tables, summed)
    returned = [returned[0]] + [swap(returned[kk], kk) for kk in range(1, groups)]
    grad_blocks = table_call(
        functools.partial(return_kernel, groups, per_device),
        groups,
        sds((SLOTS, rows, BLK), F32),
        [pltpu.SMEM((groups,), jnp.int32)],
    )(*tables, *returned)

    cross_out, base, back_same, back_other = table_call(
        functools.partial(cross_kernel, groups, per_device, nx, nz, ny),
        groups + 4 + n_dp,
        [
            sds((row_count, local_width), BF),
            wide,
            sds((nx - 1, per_device, row_count, BLK), BF),
            sds((nx, per_device, row_count, BLK), BF),
        ],
        [
            pltpu.VMEM((width, BLK, BLK), BF),
            sbuf,
            pltpu.VMEM((per_device, row_count, BLK), F32),
            pltpu.VMEM((groups * per_device, row_count, BLK), F32),
        ]
        + tabs
        + [pltpu.SemaphoreType.DMA((n_dp,))],
        in_specs=[ANY] * groups + [VMEM] * 4 + [ANY] * n_dp,
    )(*tables, *pieces, low, start, cotangent, cross_bias.reshape(per_device, 1, BLK), *shards)
    across = lax.ppermute(back_other, "core", [(0, 1), (1, 0)])

    plane = ny * out_rows
    order = ring_order(nz)
    dense_parts = []
    for s in range(nz):
        ahead = ring_from("z", nz, -s)
        cut = lax.dynamic_slice_in_dim(dense, ahead * plane, plane, 1)
        if s > 0:
            cut = lax.ppermute(cut, "z", [(order[p], order[(p + s) % nz]) for p in range(nz)])
        dense_parts.append(cut)

    chunks = 2 if per_device % 2 == 0 else 1
    span = per_device // chunks
    owns, fars, sums = [], [], []
    for c in range(chunks):
        sl = slice(c * span, (c + 1) * span)
        carried = None
        for sx in range(1, nx):
            term = back_same[sx - 1, sl].astype(F32) + across[sx, sl].astype(F32)
            if carried is not None:
                term = term + carried.astype(F32)
            carried = lax.ppermute(term.astype(BF), "x", ring_hop(nx))
        first = c * span
        shifted = pl.BlockSpec((1, row_count, BLK), lambda i: (i + first, 0, 0))
        plain = pl.BlockSpec((1, row_count, BLK), lambda i: (i, 0, 0))
        grad_low, sum_c = pl.pallas_call(
            pre_kernel,
            grid=(span,),
            in_specs=[shifted, shifted, plain, shifted],
            out_specs=[plain, line],
            out_shape=[sds((span, row_count, BLK), BF), sds((1, span * BLK), F32)],
            compiler_params=params(("arbitrary",)),
        )(base, across[0], carried, slope)
        sums.append(sum_c)
        gathered = ring_gather(grad_low, "z", nz)
        own, send = pl.pallas_call(
            functools.partial(weight_grad_kernel, nz, ny, out_rows),
            grid=(span,),
            in_specs=[plain] * nz + [pl.BlockSpec((row_count, plane), lambda i: (0, 0))] * nz,
            out_specs=[
                pl.BlockSpec((out_rows, BLK), lambda i: (0, i)),
                pl.BlockSpec((ny - 1, out_rows, BLK), lambda i: (0, 0, i)),
            ],
            out_shape=[
                sds((out_rows, span * BLK), F32),
                sds((ny - 1, out_rows, span * BLK), BF),
            ],
            compiler_params=params(("arbitrary",)),
        )(*gathered, *dense_parts)
        carried = None
        for sy in range(1, ny):
            term = send[sy - 1]
            if carried is not None:
                term = (term.astype(F32) + carried.astype(F32)).astype(BF)
            carried = lax.ppermute(term, "y", ring_hop(ny))
        owns.append(own)
        fars.append(carried)
    grad_bottom = pl.pallas_call(
        functools.partial(final_kernel, chunks, span * BLK),
        in_specs=[VMEM] * (2 * chunks),
        out_specs=VMEM,
        out_shape=sds((out_rows, local_width), F32),
        compiler_params=params(),
    )(*owns, *fars)

    bias = jnp.concatenate([bias_mixed] + sums, axis=1)
    for piece in ring_gather(bias, "z", nz)[1:]:
        bias = bias + piece
    for piece in ring_gather(bias, "y", ny)[1:]:
        bias = bias + piece
    bias = bias.reshape(2, local_width)
    return cross_out, grad_bottom, bias[1], grad_blocks, bias[0]


def solution(mesh):
    n_dp, groups = mesh.devices.shape
    nx = groups // 2
    ny = nx if n_dp % nx == 0 else 1
    nz = n_dp // ny
    fine = Mesh(mesh.devices.reshape(nz, ny, nx, 2), ("z", "y", "x", "core"))
    dp, tensor = ("z", "y"), ("x", "core")
    return jax.shard_map(
        functools.partial(on_device, (nz, ny, nx)),
        mesh=fine,
        in_specs=(
            P(dp, None),
            P(None, tensor),
            P(tensor),
            P(tensor, dp, None),
            P(tensor),
            P(dp, tensor),
            P(),
            P(),
            P(),
        ),
        out_specs=(
            P(dp, tensor),
            P(dp, tensor),
            P(tensor),
            P(tensor, dp, None),
            P(tensor),
        ),
        check_vma=False,
    )
```

```python
import functools

import jax
import jax.numpy as jnp
import numpy as np
from jax import lax
from jax.experimental import pallas as pl
from jax.experimental.pallas import tpu as pltpu
from jax.sharding import Mesh, PartitionSpec as P

BLK = 512
SLOTS = 10
EXTRA = 16
BF = jnp.bfloat16
F32 = jnp.float32
ANY = pl.BlockSpec(memory_space=pl.ANY)
VMEM = pl.BlockSpec(memory_space=pltpu.VMEM)
LIMIT = 56 * 1024 * 1024


def params(semantics=None):
    return pltpu.CompilerParams(vmem_limit_bytes=LIMIT, dimension_semantics=semantics)


def dot(a, b, dims):
    return lax.dot_general(a, b, (dims, ((), ())), preferred_element_type=F32)


def ring_order(n):
    return list(range(0, n, 2)) + list(range(n - 1 - (n % 2), 0, -2))


def ring_hop(n):
    order = ring_order(n)
    return [(order[p], order[(p + 1) % n]) for p in range(n)]


def ring_from(axis, n, step):
    order = ring_order(n)
    me = lax.axis_index(axis)
    behind = [0] * n
    for p in range(n):
        behind[order[p]] = order[(p - step) % n]
    result = jnp.int32(behind[0])
    for i in range(1, n):
        result = jnp.where(me == i, behind[i], result)
    return result


def tie(*values):
    return lax.optimization_barrier(tuple(values))


def ring_gather(value, axis, n):
    pieces = [value]
    for _ in range(n - 1):
        pieces.append(lax.ppermute(pieces[-1], axis, ring_hop(n)))
    return pieces


def local_of(block, per_device):
    return lax.div(block, jnp.int32(per_device))


def owner_walk(me, ref, live, groups, per_device, visit):
    total = jnp.int32(0)
    for kk in range(groups):
        source = me ^ kk
        alive = live[source]
        rank = jnp.int32(0)
        for k in range(SLOTS):
            hit = (k < alive) & (local_of(ref[source, k], per_device) == me)

            @pl.when(hit)
            def _(source=source, k=k, total=total, rank=rank, kk=kk):
                visit(kk, source, k, total, rank)

            step = hit.astype(jnp.int32)
            total = total + step
            rank = rank + step
    return total


def tensor_index():
    return lax.axis_index("x") * lax.axis_size("core") + lax.axis_index("core")


def pack_kernel(groups, per_device, inb, outb, live, w, *refs):
    packed, count = refs[:groups], refs[groups]
    me = tensor_index()
    for g in range(groups):
        count[g] = 0
    alive = live[me]

    def body(k, carry):
        to = me ^ local_of(outb[me, k], per_device)

        @pl.when(k < alive)
        def _():
            for g in range(groups):

                @pl.when(to == g)
                def _(g=g):
                    packed[g][count[g]] = w[k]

            count[to] = count[to] + 1

        return carry

    lax.fori_loop(0, SLOTS, body, 0)


def compact_kernel(groups, per_device, inb, outb, live, *refs):
    pieces, out = refs[:groups], refs[groups]
    me = tensor_index()

    def visit(kk, source, k, total, rank):
        out[total] = pieces[kk][rank]

    owner_walk(me, outb, live, groups, per_device, visit)


def expand_kernel(groups, per_device, inb, outb, live, grads, *packed):
    me = tensor_index()

    def visit(kk, source, k, total, rank):
        packed[kk][rank] = grads[total]

    owner_walk(me, outb, live, groups, per_device, visit)


def return_kernel(groups, per_device, inb, outb, live, *refs):
    pieces, out, count = refs[:groups], refs[groups], refs[groups + 1]
    me = tensor_index()
    for g in range(groups):
        count[g] = 0
    alive = live[me]

    def body(k, carry):
        to = me ^ local_of(outb[me, k], per_device)

        @pl.when(k < alive)
        def _():
            for g in range(groups):

                @pl.when(to == g)
                def _(g=g):
                    out[k] = pieces[g][count[g]].astype(F32)

            count[to] = count[to] + 1

        @pl.when(k >= alive)
        def _():
            out[k] = jnp.zeros(out.shape[1:], F32)

        return carry

    lax.fori_loop(0, SLOTS, body, 0)


def bottom_kernel(dense, weight, bias, cot, start, low, slope, bias_sum):
    pre = jnp.dot(dense[...], weight[...], preferred_element_type=F32) + bias[...]
    sigma = 1.0 / (1.0 + jnp.exp(-pre))
    begin = (pre * sigma).astype(BF)
    start[0] = begin
    grad = cot[...].astype(F32) * begin.astype(F32)
    low[0] = grad.astype(BF)
    slope[0] = sigma * (1.0 + pre * (1.0 - sigma))
    bias_sum[...] = jnp.sum(grad, axis=0, keepdims=True)


def fetch_inputs(groups, per_device, inb, outb, live, pieces, sbuf, tin, tout, sem):
    me = tensor_index()

    def visit(kk, source, k, total, rank):
        block = inb[source, k]
        owner = local_of(block, per_device)
        tin[total] = block + ((me ^ owner) - owner) * per_device
        tout[total] = outb[source, k] - me * per_device

    total = owner_walk(me, outb, live, groups, per_device, visit)

    def issue(j, carry):
        which = local_of(tin[j], per_device)
        col = tin[j] - which * per_device
        for g in range(groups):

            @pl.when(which == g)
            def _(g=g):
                pltpu.make_async_copy(pieces[g].at[col], sbuf.at[j], sem.at[j]).start()

        return carry

    lax.fori_loop(0, total, issue, 0)
    return total


def wait_input(pieces, sbuf, sem, j):
    pltpu.make_async_copy(pieces[0].at[0], sbuf.at[j], sem.at[j]).wait()


def block_grad_kernel(groups, per_device, ny, inb, outb, live, *refs):
    pieces = refs[:groups]
    low, out, sbuf, tmp, tin, tout, sem = refs[groups:]
    total = fetch_inputs(groups, per_device, inb, outb, live, pieces, sbuf, tin, tout, sem)
    rows = out.shape[2]

    def body(j, carry):
        wait_input(pieces, sbuf, sem, j)
        tmp[...] = dot(sbuf[j], low[tout[j]], ((0,), (0,))).astype(BF)
        for d in range(out.shape[0]):
            out[d, j] = tmp[d * rows : (d + 1) * rows, :]
        return carry

    lax.fori_loop(0, total, body, 0)


def cross_kernel(groups, per_device, nx, nz, ny, inb, outb, live, *refs):
    pieces = refs[:groups]
    low, start, cot, bias = refs[groups : groups + 4]
    shards = refs[groups + 4 : groups + 4 + nz * ny]
    cross, base, back_same, back_other = refs[groups + 4 + nz * ny : groups + 8 + nz * ny]
    wbuf, sbuf, mixed, acc, tin, tout, sem, wsem = refs[groups + 8 + nz * ny :]
    rows = shards[0].shape[1]
    copies = []
    for sz in range(nz):
        for sy in range(ny):
            d = ring_from("z", nz, sz) * ny + ring_from("y", ny, sy)
            place = pl.ds(pl.multiple_of(d * rows, rows), rows)
            copies.append(
                pltpu.make_async_copy(
                    shards[sz * ny + sy], wbuf.at[:, place, :], wsem.at[sz * ny + sy]
                )
            )
    for copy in copies:
        copy.start()
    total = fetch_inputs(groups, per_device, inb, outb, live, pieces, sbuf, tin, tout, sem)

    def clear(i, carry):
        acc[i] = jnp.zeros(acc.shape[1:], F32)
        return carry

    lax.fori_loop(0, acc.shape[0], clear, 0)

    def begin(b, carry):
        mixed[b] = jnp.broadcast_to(bias[b], mixed.shape[1:])
        return carry

    lax.fori_loop(0, per_device, begin, 0)
    for copy in copies:
        copy.wait()

    def body(j, carry):
        wait_input(pieces, sbuf, sem, j)
        part = dot(sbuf[j], wbuf[j], ((1,), (0,))).astype(BF).astype(F32)
        mixed[tout[j]] = mixed[tout[j]] + part
        back = dot(low[tout[j]], wbuf[j], ((1,), (1,))).astype(BF).astype(F32)
        acc[tin[j]] = acc[tin[j]] + back
        return carry

    lax.fori_loop(0, total, body, 0)
    for b in range(per_device):
        wide = start[b].astype(F32)
        mix = mixed[b]
        c = cot[:, b * BLK : (b + 1) * BLK].astype(F32)
        cross[:, b * BLK : (b + 1) * BLK] = (wide * mix + wide).astype(BF)
        base[b] = c * mix + c + acc[b]

    mx, core = lax.axis_index("x"), lax.axis_index("core")
    for sx in range(nx):
        rel = (mx ^ ring_from("x", nx, sx)) * 2

        def spill(b, carry, sx=sx, rel=rel):
            if sx > 0:
                back_same[sx - 1, b] = acc[rel * per_device + b].astype(BF)
            back_other[sx, b] = acc[(rel + 1) * per_device + b].astype(BF)
            return carry

        lax.fori_loop(0, per_device, spill, 0)


def pre_kernel(base, here, far, slope, low):
    grad = base[0] + here[0].astype(F32) + far[0].astype(F32)
    grad = grad * slope[0]
    low[0] = grad.astype(BF)


def weight_grad_kernel(nz, ny, rows, *refs):
    grads, dense = refs[:nz], refs[nz : 2 * nz]
    own, send = refs[2 * nz :]
    column = grads[0][0].astype(F32)
    for s in range(1, nz):
        column = column + grads[s][0].astype(F32)
    column = jnp.sum(column, axis=0, keepdims=True)
    high = column.astype(BF).astype(F32)
    place = lax.broadcasted_iota(jnp.int32, (EXTRA, BLK), 0)
    own[rows:, :] = jnp.where(place == 0, column, 0.0)
    extra = jnp.where(place == 0, high, jnp.where(place == 1, column - high, 0.0)).astype(BF)
    for sy in range(ny):
        y = ring_from("y", ny, sy)
        cols = pl.ds(pl.multiple_of(y * rows, rows), rows)
        total = None
        for s in range(nz):
            term = dot(dense[s][:, cols], grads[s][0], ((0,), (0,)))
            total = term if total is None else total + term
        if sy == 0:
            own[:rows, :] = total
        else:
            send[sy - 1, :rows, :] = total.astype(BF)
            send[sy - 1, rows:, :] = extra


def final_kernel(chunks, width, rows, *refs):
    own, far, (out, bias) = refs[:chunks], refs[chunks : 2 * chunks], refs[2 * chunks :]
    for c in range(chunks):
        cols = slice(c * width, (c + 1) * width)
        out[:, cols] = own[c][:rows, :] + far[c][:rows, :].astype(F32)
        low = jnp.sum(far[c][rows:, :].astype(F32), axis=0, keepdims=True)
        bias[:, cols] = own[c][rows : rows + 1, :] + low


def on_device(sizes, *args):
    dense, bottom_weight, bottom_bias, cross_blocks, cross_bias, cotangent, inb, outb, live = args
    nz, ny, nx = sizes
    groups = nx * 2
    row_count, depth = dense.shape
    local_width = bottom_weight.shape[1]
    per_device = local_width // BLK
    capacity = -(-SLOTS // groups)
    width = groups * capacity
    rows = cross_blocks.shape[1]
    n_dp = nz * ny
    out_rows = depth // n_dp
    smem = pltpu.SMEM
    tables = (inb, outb, live)
    sds = jax.ShapeDtypeStruct

    def table_call(kernel, n_in, out_shape, scratch=(), in_specs=None, out_specs=None):
        single = not isinstance(out_shape, (tuple, list))
        return pl.pallas_call(
            kernel,
            out_shape=out_shape,
            grid_spec=pltpu.PrefetchScalarGridSpec(
                num_scalar_prefetch=3,
                grid=(),
                in_specs=in_specs or [VMEM] * n_in,
                out_specs=out_specs or (VMEM if single else [VMEM] * len(out_shape)),
                scratch_shapes=list(scratch),
            ),
            compiler_params=params(),
        )

    def swap(value, kk):
        return lax.ppermute(value, ("x", "core"), [(i, i ^ kk) for i in range(groups)])

    packed = table_call(
        functools.partial(pack_kernel, groups, per_device),
        1,
        [sds((capacity, rows, BLK), BF)] * groups,
        [pltpu.SMEM((groups,), jnp.int32)],
    )(*tables, cross_blocks)
    dense_tied, _ = tie(dense, packed[0])
    moved = [packed[0]] + [swap(packed[kk], kk) for kk in range(1, groups)]
    shard = table_call(
        functools.partial(compact_kernel, groups, per_device),
        groups,
        sds((width, rows, BLK), BF),
    )(*tables, *moved)

    block = lambda dtype: pl.BlockSpec((1, row_count, BLK), lambda i: (i, 0, 0))
    line = pl.BlockSpec((1, BLK), lambda i: (0, i))
    wide = sds((per_device, row_count, BLK), F32)
    narrow = sds((per_device, row_count, BLK), BF)
    start, low, slope, bias_mixed = pl.pallas_call(
        bottom_kernel,
        grid=(per_device,),
        in_specs=[
            pl.BlockSpec((row_count, depth), lambda i: (0, 0)),
            pl.BlockSpec((depth, BLK), lambda i: (0, i)),
            line,
            pl.BlockSpec((row_count, BLK), lambda i: (0, i)),
        ],
        out_specs=[block(BF), block(BF), block(F32), line],
        out_shape=[narrow, narrow, wide, sds((1, local_width), F32)],
        compiler_params=params(("arbitrary",)),
    )(dense_tied, bottom_weight, bottom_bias.reshape(1, -1), cotangent)

    if nx == 2:
        far = lax.ppermute(start, "x", [(0, 1), (1, 0)])
        flip = [(0, 1), (1, 0)]
        pieces = [start, lax.ppermute(start, "core", flip), far, lax.ppermute(far, "core", flip)]
    else:
        pieces = [start] + [swap(start, kk) for kk in range(1, groups)]

    plane = ny * out_rows
    order = ring_order(nz)
    dense_parts = []
    for s in range(nz):
        ahead = ring_from("z", nz, -s)
        cut = lax.dynamic_slice_in_dim(dense, ahead * plane, plane, 1)
        if s > 0:
            cut = lax.ppermute(cut, "z", [(order[p], order[(p + s) % nz]) for p in range(nz)])
        dense_parts.append(cut)

    bias = bias_mixed
    for piece in ring_gather(bias, "z", nz)[1:]:
        bias = bias + piece
    for piece in ring_gather(bias, "y", ny)[1:]:
        bias = bias + piece

    shards = []
    for piece in ring_gather(shard, "z", nz):
        if shards:
            piece, shards[-1] = tie(piece, shards[-1])
        shards += ring_gather(piece, "y", ny)

    low_late, _ = tie(low, shards[-1])
    tabs = [smem((width,), jnp.int32), smem((width,), jnp.int32), pltpu.SemaphoreType.DMA((width,))]
    sbuf = pltpu.VMEM((width, row_count, BLK), BF)
    block_grads = table_call(
        functools.partial(block_grad_kernel, groups, per_device, ny),
        groups + 1,
        sds((n_dp, width, rows, BLK), BF),
        [sbuf, pltpu.VMEM((BLK, BLK), BF)] + tabs,
        in_specs=[ANY] * groups + [VMEM],
    )(*tables, *pieces, low_late)
    summed = lax.psum_scatter(block_grads, ("z", "y"), scatter_dimension=0, tiled=True)
    summed = summed.reshape(width, rows, BLK)
    returned = table_call(
        functools.partial(expand_kernel, groups, per_device),
        1,
        [sds((capacity, rows, BLK), BF)] * groups,
    )(*tables, summed)
    returned = [returned[0]] + [swap(returned[kk], kk) for kk in range(1, groups)]
    grad_blocks = table_call(
        functools.partial(return_kernel, groups, per_device),
        groups,
        sds((SLOTS, rows, BLK), F32),
        [pltpu.SMEM((groups,), jnp.int32)],
    )(*tables, *returned)

    cotangent, *_ = tie(cotangent, bias, *dense_parts)
    cross_out, base, back_same, back_other = table_call(
        functools.partial(cross_kernel, groups, per_device, nx, nz, ny),
        groups + 4 + n_dp,
        [
            sds((row_count, local_width), BF),
            wide,
            sds((nx - 1, per_device, row_count, BLK), BF),
            sds((nx, per_device, row_count, BLK), BF),
        ],
        [
            pltpu.VMEM((width, BLK, BLK), BF),
            sbuf,
            pltpu.VMEM((per_device, row_count, BLK), F32),
            pltpu.VMEM((groups * per_device, row_count, BLK), F32),
        ]
        + tabs
        + [pltpu.SemaphoreType.DMA((n_dp,))],
        in_specs=[ANY] * groups + [VMEM] * 4 + [ANY] * n_dp,
    )(*tables, *pieces, low, start, cotangent, cross_bias.reshape(per_device, 1, BLK), *shards)
    across = lax.ppermute(back_other, "core", [(0, 1), (1, 0)])

    chunks = 2 if per_device % 2 == 0 else 1
    span = per_device // chunks
    owns, fars = [], []
    for c in range(chunks):
        sl = slice(c * span, (c + 1) * span)
        carried = None
        for sx in range(1, nx):
            term = back_same[sx - 1, sl].astype(F32) + across[sx, sl].astype(F32)
            if carried is not None:
                term = term + carried.astype(F32)
            carried = lax.ppermute(term.astype(BF), "x", ring_hop(nx))
        first = c * span
        shifted = pl.BlockSpec((1, row_count, BLK), lambda i: (i + first, 0, 0))
        plain = pl.BlockSpec((1, row_count, BLK), lambda i: (i, 0, 0))
        grad_low = pl.pallas_call(
            pre_kernel,
            grid=(span,),
            in_specs=[shifted, shifted, plain, shifted],
            out_specs=plain,
            out_shape=sds((span, row_count, BLK), BF),
            compiler_params=params(("arbitrary",)),
        )(base, across[0], carried, slope)
        gathered = ring_gather(grad_low, "z", nz)
        own, send = pl.pallas_call(
            functools.partial(weight_grad_kernel, nz, ny, out_rows),
            grid=(span,),
            in_specs=[plain] * nz + [pl.BlockSpec((row_count, plane), lambda i: (0, 0))] * nz,
            out_specs=[
                pl.BlockSpec((out_rows + EXTRA, BLK), lambda i: (0, i)),
                pl.BlockSpec((ny - 1, out_rows + EXTRA, BLK), lambda i: (0, 0, i)),
            ],
            out_shape=[
                sds((out_rows + EXTRA, span * BLK), F32),
                sds((ny - 1, out_rows + EXTRA, span * BLK), BF),
            ],
            compiler_params=params(("arbitrary",)),
        )(*gathered, *dense_parts)
        carried = None
        for sy in range(1, ny):
            term = send[sy - 1]
            if carried is not None:
                term = (term.astype(F32) + carried.astype(F32)).astype(BF)
            carried = lax.ppermute(term, "y", ring_hop(ny))
        owns.append(own)
        fars.append(carried)
    grad_bottom, bias_pre = pl.pallas_call(
        functools.partial(final_kernel, chunks, span * BLK, out_rows),
        in_specs=[VMEM] * (2 * chunks),
        out_specs=[VMEM, VMEM],
        out_shape=[sds((out_rows, local_width), F32), sds((1, local_width), F32)],
        compiler_params=params(),
    )(*owns, *fars)

    return cross_out, grad_bottom, bias_pre.reshape(-1), grad_blocks, bias.reshape(-1)


def solution(mesh):
    n_dp, groups = mesh.devices.shape
    nx = groups // 2
    ny = nx if n_dp % nx == 0 else 1
    nz = n_dp // ny
    fine = Mesh(mesh.devices.reshape(nz, ny, nx, 2), ("z", "y", "x", "core"))
    dp, tensor = ("z", "y"), ("x", "core")
    return jax.shard_map(
        functools.partial(on_device, (nz, ny, nx)),
        mesh=fine,
        in_specs=(
            P(dp, None),
            P(None, tensor),
            P(tensor),
            P(tensor, dp, None),
            P(tensor),
            P(dp, tensor),
            P(),
            P(),
            P(),
        ),
        out_specs=(
            P(dp, tensor),
            P(dp, tensor),
            P(tensor),
            P(tensor, dp, None),
            P(tensor),
        ),
        check_vma=False,
    )
```

```python
import functools

import jax
import jax.numpy as jnp
import numpy as np
from jax import lax
from jax.experimental import pallas as pl
from jax.experimental.pallas import tpu as pltpu
from jax.sharding import Mesh, PartitionSpec as P

BLK = 512
SLOTS = 10
EXTRA = 16
BF = jnp.bfloat16
F32 = jnp.float32
ANY = pl.BlockSpec(memory_space=pl.ANY)
VMEM = pl.BlockSpec(memory_space=pltpu.VMEM)
LIMIT = 56 * 1024 * 1024


def params(semantics=None):
    return pltpu.CompilerParams(vmem_limit_bytes=LIMIT, dimension_semantics=semantics)


def dot(a, b, dims):
    return lax.dot_general(a, b, (dims, ((), ())), preferred_element_type=F32)


def ring_order(n):
    return list(range(0, n, 2)) + list(range(n - 1 - (n % 2), 0, -2))


def ring_hop(n):
    order = ring_order(n)
    return [(order[p], order[(p + 1) % n]) for p in range(n)]


def ring_from(axis, n, step):
    order = ring_order(n)
    me = lax.axis_index(axis)
    behind = [0] * n
    for p in range(n):
        behind[order[p]] = order[(p - step) % n]
    result = jnp.int32(behind[0])
    for i in range(1, n):
        result = jnp.where(me == i, behind[i], result)
    return result


def tie(*values):
    return lax.optimization_barrier(tuple(values))


def ring_gather(value, axis, n):
    pieces = [value]
    for _ in range(n - 1):
        pieces.append(lax.ppermute(pieces[-1], axis, ring_hop(n)))
    return pieces


def ring_sum(terms, axis, n):
    carried = None
    for s in range(1, n):
        term = terms[s]
        if carried is not None:
            term = (term.astype(F32) + carried.astype(F32)).astype(BF)
        carried = lax.ppermute(term, axis, ring_hop(n))
    return (terms[0].astype(F32) + carried.astype(F32)).astype(BF)


def local_of(block, per_device):
    return lax.div(block, jnp.int32(per_device))


def owner_walk(me, ref, live, groups, per_device, visit):
    total = jnp.int32(0)
    for kk in range(groups):
        source = me ^ kk
        alive = live[source]
        rank = jnp.int32(0)
        for k in range(SLOTS):
            hit = (k < alive) & (local_of(ref[source, k], per_device) == me)

            @pl.when(hit)
            def _(source=source, k=k, total=total, rank=rank, kk=kk):
                visit(kk, source, k, total, rank)

            step = hit.astype(jnp.int32)
            total = total + step
            rank = rank + step
    return total


def tensor_index():
    return lax.axis_index("x") * lax.axis_size("core") + lax.axis_index("core")


def pack_kernel(groups, per_device, inb, outb, live, w, *refs):
    packed, most, count = refs[:groups], refs[groups], refs[groups + 1]
    me = tensor_index()
    for g in range(groups):
        count[g] = 0
    for t in range(groups):
        alive = live[t]

        def tally(k, carry, t=t, alive=alive):
            @pl.when(k < alive)
            def _():
                owner = local_of(outb[t, k], per_device)
                count[owner] = count[owner] + 1

            return carry

        lax.fori_loop(0, SLOTS, tally, 0)
    largest = count[0]
    for g in range(1, groups):
        largest = jnp.maximum(largest, count[g])
    most[0] = largest
    for g in range(groups):
        count[g] = 0
    alive = live[me]

    def body(k, carry):
        to = me ^ local_of(outb[me, k], per_device)

        @pl.when(k < alive)
        def _():
            for g in range(groups):

                @pl.when(to == g)
                def _(g=g):
                    packed[g][count[g]] = w[k]

            count[to] = count[to] + 1

        return carry

    lax.fori_loop(0, SLOTS, body, 0)


def compact_kernel(groups, per_device, inb, outb, live, *refs):
    pieces, out = refs[:groups], refs[groups]
    me = tensor_index()

    def visit(kk, source, k, total, rank):
        out[total] = pieces[kk][rank]

    owner_walk(me, outb, live, groups, per_device, visit)


def expand_kernel(groups, per_device, half, inb, outb, live, first, second, *packed):
    me = tensor_index()

    def visit(kk, source, k, total, rank):
        @pl.when(total < half)
        def _():
            packed[kk][rank] = first[total]

        @pl.when(total >= half)
        def _():
            packed[kk][rank] = second[total - half]

    owner_walk(me, outb, live, groups, per_device, visit)


def return_kernel(groups, per_device, inb, outb, live, *refs):
    pieces, out, count = refs[:groups], refs[groups], refs[groups + 1]
    me = tensor_index()
    for g in range(groups):
        count[g] = 0
    alive = live[me]

    def body(k, carry):
        to = me ^ local_of(outb[me, k], per_device)

        @pl.when(k < alive)
        def _():
            for g in range(groups):

                @pl.when(to == g)
                def _(g=g):
                    out[k] = pieces[g][count[g]].astype(F32)

            count[to] = count[to] + 1

        @pl.when(k >= alive)
        def _():
            out[k] = jnp.zeros(out.shape[1:], F32)

        return carry

    lax.fori_loop(0, SLOTS, body, 0)


def bottom_kernel(dense, weight, bias, cot, start, low, slope, bias_sum):
    pre = jnp.dot(dense[...], weight[...], preferred_element_type=F32) + bias[...]
    sigma = 1.0 / (1.0 + jnp.exp(-pre))
    begin = (pre * sigma).astype(BF)
    start[0] = begin
    grad = cot[...].astype(F32) * begin.astype(F32)
    low[0] = grad.astype(BF)
    slope[0] = sigma * (1.0 + pre * (1.0 - sigma))
    bias_sum[...] = jnp.sum(grad, axis=0, keepdims=True)


def list_slots(groups, per_device, inb, outb, live, tin, tout):
    me = tensor_index()

    def visit(kk, source, k, total, rank):
        block = inb[source, k]
        owner = local_of(block, per_device)
        tin[total] = block + ((me ^ owner) - owner) * per_device
        tout[total] = outb[source, k] - me * per_device

    return owner_walk(me, outb, live, groups, per_device, visit)


def fetch_inputs(groups, per_device, inb, outb, live, pieces, sbuf, tin, tout, sem):
    total = list_slots(groups, per_device, inb, outb, live, tin, tout)

    def issue(j, carry):
        which = local_of(tin[j], per_device)
        col = tin[j] - which * per_device
        for g in range(groups):

            @pl.when(which == g)
            def _(g=g):
                pltpu.make_async_copy(pieces[g].at[col], sbuf.at[j], sem.at[j]).start()

        return carry

    lax.fori_loop(0, total, issue, 0)
    return total


def wait_input(pieces, sbuf, sem, j):
    pltpu.make_async_copy(pieces[0].at[0], sbuf.at[j], sem.at[j]).wait()


def block_grad_kernel(groups, per_device, half, nz, ny, inb, outb, live, *refs):
    pieces = refs[:groups]
    low, first, second = refs[groups], refs[groups + 1 : groups + 1 + nz], refs[groups + 1 + nz : groups + 1 + nz + ny]
    sbuf, tmp, tin, tout, sem = refs[groups + 1 + nz + ny :]
    total = fetch_inputs(groups, per_device, inb, outb, live, pieces, sbuf, tin, tout, sem)
    rows = first[0].shape[2]

    def body(j, carry):
        wait_input(pieces, sbuf, sem, j)
        tmp[...] = dot(sbuf[j], low[tout[j]], ((0,), (0,))).astype(BF)
        for sz in range(nz):
            for sy in range(ny):
                d = ring_from("z", nz, sz) * ny + ring_from("y", ny, sy)
                part = tmp[pl.ds(pl.multiple_of(d * rows, rows), rows), :]

                @pl.when(j < half)
                def _(sz=sz, sy=sy, part=part):
                    first[sz][sy, j] = part

                @pl.when(j >= half)
                def _(sz=sz, sy=sy, part=part):
                    second[sy][sz, j - half] = part

        return carry

    lax.fori_loop(0, total, body, 0)


def load_shards(nz, ny, shards, wbuf, wsem):
    rows = shards[0].shape[1]
    copies = []
    for sz in range(nz):
        for sy in range(ny):
            d = ring_from("z", nz, sz) * ny + ring_from("y", ny, sy)
            place = pl.ds(pl.multiple_of(d * rows, rows), rows)
            i = sz * ny + sy
            copies.append(pltpu.make_async_copy(shards[i], wbuf.at[:, place, :], wsem.at[i]))
    for copy in copies:
        copy.start()
    return copies


def back_kernel(groups, per_device, nx, nz, ny, inb, outb, live, *refs):
    low, shards = refs[0], refs[1 : 1 + nz * ny]
    back_same, back_other, wbuf, acc, tin, tout, wsem = refs[1 + nz * ny :]
    copies = load_shards(nz, ny, shards, wbuf, wsem)
    total = list_slots(groups, per_device, inb, outb, live, tin, tout)

    def clear(i, carry):
        acc[i] = jnp.zeros(acc.shape[1:], F32)
        return carry

    lax.fori_loop(0, acc.shape[0], clear, 0)
    for copy in copies:
        copy.wait()

    def body(j, carry):
        back = dot(low[tout[j]], wbuf[j], ((1,), (1,))).astype(BF).astype(F32)
        acc[tin[j]] = acc[tin[j]] + back
        return carry

    lax.fori_loop(0, total, body, 0)

    mx = lax.axis_index("x")
    for sx in range(nx):
        rel = (mx ^ ring_from("x", nx, sx)) * 2

        def spill(b, carry, sx=sx, rel=rel):
            back_same[sx, b] = acc[rel * per_device + b].astype(BF)
            back_other[sx, b] = acc[(rel + 1) * per_device + b].astype(BF)
            return carry

        lax.fori_loop(0, per_device, spill, 0)


def forward_kernel(groups, per_device, nz, ny, inb, outb, live, *refs):
    pieces = refs[:groups]
    start, cot, bias = refs[groups : groups + 3]
    shards = refs[groups + 3 : groups + 3 + nz * ny]
    cross, base, wbuf, sbuf, tin, tout, sem, wsem = refs[groups + 3 + nz * ny :]
    copies = load_shards(nz, ny, shards, wbuf, wsem)
    total = fetch_inputs(groups, per_device, inb, outb, live, pieces, sbuf, tin, tout, sem)

    def begin(b, carry):
        base[b] = jnp.broadcast_to(bias[b], base.shape[1:])
        return carry

    lax.fori_loop(0, per_device, begin, 0)
    for copy in copies:
        copy.wait()

    def body(j, carry):
        wait_input(pieces, sbuf, sem, j)
        part = dot(sbuf[j], wbuf[j], ((1,), (0,))).astype(BF).astype(F32)
        base[tout[j]] = base[tout[j]] + part
        return carry

    lax.fori_loop(0, total, body, 0)
    for b in range(per_device):
        wide = start[b].astype(F32)
        mix = base[b]
        c = cot[:, b * BLK : (b + 1) * BLK].astype(F32)
        cross[:, b * BLK : (b + 1) * BLK] = (wide * mix + wide).astype(BF)
        base[b] = c * mix + c


def pre_kernel(base, own, here, far, slope, low):
    grad = base[0] + own[0, 0].astype(F32) + here[0, 0].astype(F32) + far[0].astype(F32)
    grad = grad * slope[0]
    low[0] = grad.astype(BF)


def weight_grad_kernel(nz, ny, rows, *refs):
    grads, dense = refs[:nz], refs[nz : 2 * nz]
    own, send = refs[2 * nz :]
    column = grads[0][0].astype(F32)
    for s in range(1, nz):
        column = column + grads[s][0].astype(F32)
    column = jnp.sum(column, axis=0, keepdims=True)
    high = column.astype(BF).astype(F32)
    place = lax.broadcasted_iota(jnp.int32, (EXTRA, BLK), 0)
    own[rows:, :] = jnp.where(place == 0, column, 0.0)
    extra = jnp.where(place == 0, high, jnp.where(place == 1, column - high, 0.0)).astype(BF)
    for sy in range(ny):
        y = ring_from("y", ny, sy)
        cols = pl.ds(pl.multiple_of(y * rows, rows), rows)
        total = None
        for s in range(nz):
            term = dot(dense[s][:, cols], grads[s][0], ((0,), (0,)))
            total = term if total is None else total + term
        if sy == 0:
            own[:rows, :] = total
        else:
            send[sy - 1, :rows, :] = total.astype(BF)
            send[sy - 1, rows:, :] = extra


def final_kernel(rows, parts, *refs):
    own, far = refs[:parts], refs[parts : 2 * parts]
    out, bias = refs[-2:]
    size = out.shape[1] // parts
    for c in range(parts):
        cols = slice(c * size, (c + 1) * size)
        out[:, cols] = own[c][:rows, :] + far[c][0, :rows, :].astype(F32)
        low = jnp.sum(far[c][0, rows:, :].astype(F32), axis=0, keepdims=True)
        bias[:, cols] = own[c][rows : rows + 1, :] + low


def on_device(sizes, *args):
    dense, bottom_weight, bottom_bias, cross_blocks, cross_bias, cotangent, inb, outb, live = args
    nz, ny, nx = sizes
    groups = nx * 2
    row_count, depth = dense.shape
    local_width = bottom_weight.shape[1]
    per_device = local_width // BLK
    capacity = -(-SLOTS // groups)
    rows = cross_blocks.shape[1]
    n_dp = nz * ny
    out_rows = depth // n_dp
    plane = ny * out_rows
    smem = pltpu.SMEM
    tables = (inb, outb, live)
    sds = jax.ShapeDtypeStruct
    flip = [(0, 1), (1, 0)]

    def table_call(kernel, n_in, out_shape, scratch=(), in_specs=None, out_specs=None):
        single = not isinstance(out_shape, (tuple, list))
        return pl.pallas_call(
            kernel,
            out_shape=out_shape,
            grid_spec=pltpu.PrefetchScalarGridSpec(
                num_scalar_prefetch=3,
                grid=(),
                in_specs=in_specs or [VMEM] * n_in,
                out_specs=out_specs or (VMEM if single else [VMEM] * len(out_shape)),
                scratch_shapes=list(scratch),
            ),
            compiler_params=params(),
        )

    def swap(value, kk):
        return lax.ppermute(value, ("x", "core"), [(i, i ^ kk) for i in range(groups)])

    *packed, most = table_call(
        functools.partial(pack_kernel, groups, per_device),
        1,
        [sds((capacity, rows, BLK), BF)] * groups + [sds((1,), jnp.int32)],
        [smem((groups,), jnp.int32)],
        out_specs=[VMEM] * groups + [pl.BlockSpec(memory_space=smem)],
    )(*tables, cross_blocks)
    dense_tied, _ = tie(dense, packed[0])
    moved = [packed[0]] + [swap(packed[kk], kk) for kk in range(1, groups)]

    block = lambda dtype: pl.BlockSpec((1, row_count, BLK), lambda i: (i, 0, 0))
    line = pl.BlockSpec((1, BLK), lambda i: (0, i))
    wide = sds((per_device, row_count, BLK), F32)
    narrow = sds((per_device, row_count, BLK), BF)
    start, low, slope, bias_mixed = pl.pallas_call(
        bottom_kernel,
        grid=(per_device,),
        in_specs=[
            pl.BlockSpec((row_count, depth), lambda i: (0, 0)),
            pl.BlockSpec((depth, BLK), lambda i: (0, i)),
            line,
            pl.BlockSpec((row_count, BLK), lambda i: (0, i)),
        ],
        out_specs=[block(BF), block(BF), block(F32), line],
        out_shape=[narrow, narrow, wide, sds((1, local_width), F32)],
        compiler_params=params(("arbitrary",)),
    )(dense_tied, bottom_weight, bottom_bias.reshape(1, -1), cotangent)

    order = ring_order(nz)
    dense_parts = []
    for s in range(nz):
        ahead = ring_from("z", nz, -s)
        cut = lax.dynamic_slice_in_dim(dense, ahead * plane, plane, 1)
        if s > 0:
            cut = lax.ppermute(cut, "z", [(order[p], order[(p + s) % nz]) for p in range(nz)])
        dense_parts.append(cut)

    def rest(width, *operands):
        start, low, slope, bias_mixed, cotangent, cross_bias = operands[:6]
        tables = operands[6:9]
        moved = operands[9 : 9 + groups]
        dense_parts = operands[9 + groups :]
        half = width // 2
        shard = table_call(
            functools.partial(compact_kernel, groups, per_device),
            groups,
            sds((width, rows, BLK), BF),
        )(*tables, *moved)

        if nx == 2:
            far = lax.ppermute(start, "x", flip)
            pieces = [start, lax.ppermute(start, "core", flip), far, lax.ppermute(far, "core", flip)]
        else:
            pieces = [start] + [swap(start, kk) for kk in range(1, groups)]

        shards = []
        for piece in ring_gather(shard, "z", nz):
            if shards:
                piece, shards[-1] = tie(piece, shards[-1])
            shards += ring_gather(piece, "y", ny)

        tabs = [smem((width,), jnp.int32), smem((width,), jnp.int32)]
        sem = pltpu.SemaphoreType.DMA((width,))
        sbuf = pltpu.VMEM((width, row_count, BLK), BF)
        wbuf = pltpu.VMEM((width, BLK, BLK), BF)
        wsem = pltpu.SemaphoreType.DMA((n_dp,))
        parts = table_call(
            functools.partial(block_grad_kernel, groups, per_device, half, nz, ny),
            groups + 1,
            [sds((ny, half, rows, BLK), BF)] * nz + [sds((nz, width - half, rows, BLK), BF)] * ny,
            [sbuf, pltpu.VMEM((BLK, BLK), BF)] + tabs + [sem],
            in_specs=[ANY] * groups + [VMEM],
        )(*tables, *pieces, low)
        z_first, y_first = list(parts[:nz]), list(parts[nz:])
        z_first[1], y_first[1], shards[-1] = tie(z_first[1], y_first[1], shards[-1])
        first = ring_sum(ring_sum(z_first, "z", nz), "y", ny)
        second = ring_sum(ring_sum(y_first, "y", ny), "z", nz)

        back = sds((nx, per_device, row_count, BLK), BF)
        back_same, back_other = table_call(
            functools.partial(back_kernel, groups, per_device, nx, nz, ny),
            1 + n_dp,
            [back, back],
            [wbuf, pltpu.VMEM((groups * per_device, row_count, BLK), F32)] + tabs + [wsem],
            in_specs=[VMEM] + [ANY] * n_dp,
        )(*tables, low, *shards)
        across = lax.ppermute(back_other, "core", flip)

        start_late, _ = tie(start, back_other)
        cross_out, base = table_call(
            functools.partial(forward_kernel, groups, per_device, nz, ny),
            groups + 3 + n_dp,
            [sds((row_count, local_width), BF), wide],
            [wbuf, sbuf] + tabs + [sem, wsem],
            in_specs=[ANY] * groups + [VMEM] * 3 + [ANY] * n_dp,
        )(*tables, *pieces, start_late, cotangent, cross_bias.reshape(per_device, 1, BLK), *shards)

        chunks = 4 if per_device % 4 == 0 else 1
        span = per_device // chunks
        plain = pl.BlockSpec((1, row_count, BLK), lambda i: (i, 0, 0))
        owns, fars, ends = [], [], []
        for c in range(chunks):
            first_block = c * span
            sl = slice(first_block, first_block + span)
            carried = None
            for sx in range(1, nx):
                term = back_same[sx, sl].astype(F32) + across[sx, sl].astype(F32)
                if carried is not None:
                    term = term + carried.astype(F32)
                carried = lax.ppermute(term.astype(BF), "x", ring_hop(nx))
            shifted = pl.BlockSpec((1, row_count, BLK), lambda i, f=first_block: (i + f, 0, 0))
            own_spec = pl.BlockSpec((1, 1, row_count, BLK), lambda i, f=first_block: (0, i + f, 0, 0))
            grad_low = pl.pallas_call(
                pre_kernel,
                grid=(span,),
                in_specs=[shifted, own_spec, own_spec, plain, shifted],
                out_specs=plain,
                out_shape=sds((span, row_count, BLK), BF),
                compiler_params=params(("arbitrary",)),
            )(base, back_same, across, carried, slope)
            if c >= 2:
                grad_low, ends[c - 2][-1] = tie(grad_low, ends[c - 2][-1])
            gathered = ring_gather(grad_low, "z", nz)
            ends.append(gathered)
        for c in range(chunks):
            own, send = pl.pallas_call(
                functools.partial(weight_grad_kernel, nz, ny, out_rows),
                grid=(span,),
                in_specs=[plain] * nz + [pl.BlockSpec((row_count, plane), lambda i: (0, 0))] * nz,
                out_specs=[
                    pl.BlockSpec((out_rows + EXTRA, BLK), lambda i: (0, i)),
                    pl.BlockSpec((ny - 1, out_rows + EXTRA, BLK), lambda i: (0, 0, i)),
                ],
                out_shape=[
                    sds((out_rows + EXTRA, span * BLK), F32),
                    sds((ny - 1, out_rows + EXTRA, span * BLK), BF),
                ],
                compiler_params=params(("arbitrary",)),
            )(*ends[c], *dense_parts)
            carried = None
            for sy in range(1, ny):
                term = send[sy - 1 : sy]
                if carried is not None:
                    term = (term.astype(F32) + carried.astype(F32)).astype(BF)
                carried = lax.ppermute(term, "y", ring_hop(ny))
            owns.append(own)
            fars.append(carried)

        size = span * BLK
        outs = [sds((out_rows, local_width), F32), sds((1, local_width), F32)]
        done = None
        groups_of = [range(chunks)] if chunks == 1 else [range(chunks // 2), range(chunks // 2, chunks)]
        for place, group in enumerate(groups_of):
            parts_in = [owns[c] for c in group] + [fars[c] for c in group]
            total = len(group) * size
            done = pl.pallas_call(
                functools.partial(final_kernel, out_rows, len(group)),
                grid=(1,),
                in_specs=[pl.BlockSpec(p.shape, lambda i, n=p.ndim: (0,) * n) for p in parts_in]
                + ([ANY, ANY] if done else []),
                out_specs=[
                    pl.BlockSpec((out_rows, total), lambda i, place=place: (0, place)),
                    pl.BlockSpec((1, total), lambda i, place=place: (0, place)),
                ],
                out_shape=outs,
                input_output_aliases={len(parts_in): 0, len(parts_in) + 1: 1} if done else {},
                compiler_params=params(("arbitrary",)),
            )(*parts_in, *(done or ()))
        grad_bottom, bias_pre = done

        returned = table_call(
            functools.partial(expand_kernel, groups, per_device, half),
            2,
            [sds((capacity, rows, BLK), BF)] * groups,
        )(*tables, first, second)
        returned = [returned[0]] + [swap(returned[kk], kk) for kk in range(1, groups)]
        grad_blocks = table_call(
            functools.partial(return_kernel, groups, per_device),
            groups,
            sds((SLOTS, rows, BLK), F32),
            [smem((groups,), jnp.int32)],
        )(*tables, *returned)

        bias = bias_mixed
        for piece in ring_gather(bias, "y", ny)[1:]:
            bias = bias + piece
        bias, _ = tie(bias, ends[-1][-1])
        for piece in ring_gather(bias, "z", nz)[1:]:
            bias = bias + piece
        return cross_out, grad_bottom, bias_pre.reshape(-1), grad_blocks, bias.reshape(-1)

    most_slots = groups * capacity
    widths = sorted({-(-most_slots * 2 // 3), -(-most_slots * 5 // 6), most_slots})
    which = sum((most[0] > w).astype(jnp.int32) for w in widths[:-1])
    return lax.switch(
        which,
        [functools.partial(rest, w) for w in widths],
        start,
        low,
        slope,
        bias_mixed,
        cotangent,
        cross_bias,
        *tables,
        *moved,
        *dense_parts,
    )


def solution(mesh):
    n_dp, groups = mesh.devices.shape
    nx = groups // 2
    ny = nx if n_dp % nx == 0 else 1
    nz = n_dp // ny
    fine = Mesh(mesh.devices.reshape(nz, ny, nx, 2), ("z", "y", "x", "core"))
    dp, tensor = ("z", "y"), ("x", "core")
    return jax.shard_map(
        functools.partial(on_device, (nz, ny, nx)),
        mesh=fine,
        in_specs=(
            P(dp, None),
            P(None, tensor),
            P(tensor),
            P(tensor, dp, None),
            P(tensor),
            P(dp, tensor),
            P(),
            P(),
            P(),
        ),
        out_specs=(
            P(dp, tensor),
            P(dp, tensor),
            P(tensor),
            P(tensor, dp, None),
            P(tensor),
        ),
        check_vma=False,
    )
```

```python
import functools

import jax
import jax.numpy as jnp
import numpy as np
from jax import lax
from jax.experimental import pallas as pl
from jax.experimental.pallas import tpu as pltpu
from jax.sharding import Mesh, PartitionSpec as P

BLK = 512
SLOTS = 10
EXTRA = 16
BF = jnp.bfloat16
F32 = jnp.float32
ANY = pl.BlockSpec(memory_space=pl.ANY)
VMEM = pl.BlockSpec(memory_space=pltpu.VMEM)
LIMIT = 56 * 1024 * 1024


def params(semantics=None):
    return pltpu.CompilerParams(vmem_limit_bytes=LIMIT, dimension_semantics=semantics)


def dot(a, b, dims):
    return lax.dot_general(a, b, (dims, ((), ())), preferred_element_type=F32)


def ring_order(n):
    return list(range(0, n, 2)) + list(range(n - 1 - (n % 2), 0, -2))


def ring_hop(n):
    order = ring_order(n)
    return [(order[p], order[(p + 1) % n]) for p in range(n)]


def ring_from(axis, n, step):
    order = ring_order(n)
    me = lax.axis_index(axis)
    behind = [0] * n
    for p in range(n):
        behind[order[p]] = order[(p - step) % n]
    result = jnp.int32(behind[0])
    for i in range(1, n):
        result = jnp.where(me == i, behind[i], result)
    return result


def after(value, *others):
    return lax.optimization_barrier((value,) + others)[0]


def ring_gather(value, axis, n):
    pieces = [value]
    for _ in range(n - 1):
        pieces.append(lax.ppermute(pieces[-1], axis, ring_hop(n)))
    return pieces


def ring_sum(terms, axis, n):
    carried = None
    for s in range(1, n):
        term = terms[s]
        if carried is not None:
            term = (term.astype(F32) + carried.astype(F32)).astype(BF)
        carried = lax.ppermute(term, axis, ring_hop(n))
    return (terms[0].astype(F32) + carried.astype(F32)).astype(BF)


def local_of(block, per_device):
    return lax.div(block, jnp.int32(per_device))


def owner_walk(me, ref, live, groups, per_device, visit):
    total = jnp.int32(0)
    for kk in range(groups):
        source = me ^ kk
        alive = live[source]
        rank = jnp.int32(0)
        for k in range(SLOTS):
            hit = (k < alive) & (local_of(ref[source, k], per_device) == me)

            @pl.when(hit)
            def _(source=source, k=k, total=total, rank=rank, kk=kk):
                visit(kk, source, k, total, rank)

            step = hit.astype(jnp.int32)
            total = total + step
            rank = rank + step
    return total


def tensor_index():
    return lax.axis_index("x") * lax.axis_size("core") + lax.axis_index("core")


def pack_kernel(groups, per_device, inb, outb, live, w, *refs):
    packed, most, count = refs[:groups], refs[groups], refs[groups + 1]
    me = tensor_index()
    for g in range(groups):
        count[g] = 0
    for t in range(groups):
        alive = live[t]

        def tally(k, carry, t=t, alive=alive):
            @pl.when(k < alive)
            def _():
                owner = local_of(outb[t, k], per_device)
                count[owner] = count[owner] + 1

            return carry

        lax.fori_loop(0, SLOTS, tally, 0)
    largest = count[0]
    for g in range(1, groups):
        largest = jnp.maximum(largest, count[g])
    most[0] = largest
    for g in range(groups):
        count[g] = 0
    alive = live[me]

    def body(k, carry):
        to = me ^ local_of(outb[me, k], per_device)

        @pl.when(k < alive)
        def _():
            for g in range(groups):

                @pl.when(to == g)
                def _(g=g):
                    packed[g][count[g]] = w[k]

            count[to] = count[to] + 1

        return carry

    lax.fori_loop(0, SLOTS, body, 0)


def compact_kernel(groups, per_device, inb, outb, live, *refs):
    pieces, out = refs[:groups], refs[groups]
    me = tensor_index()

    def visit(kk, source, k, total, rank):
        out[total] = pieces[kk][rank]

    owner_walk(me, outb, live, groups, per_device, visit)


def expand_kernel(groups, per_device, half, inb, outb, live, first, second, *packed):
    me = tensor_index()

    def visit(kk, source, k, total, rank):
        @pl.when(total < half)
        def _():
            packed[kk][rank] = first[total]

        @pl.when(total >= half)
        def _():
            packed[kk][rank] = second[total - half]

    owner_walk(me, outb, live, groups, per_device, visit)


def return_kernel(groups, per_device, inb, outb, live, *refs):
    pieces, out, count = refs[:groups], refs[groups], refs[groups + 1]
    me = tensor_index()
    for g in range(groups):
        count[g] = 0
    alive = live[me]

    def body(k, carry):
        to = me ^ local_of(outb[me, k], per_device)

        @pl.when(k < alive)
        def _():
            for g in range(groups):

                @pl.when(to == g)
                def _(g=g):
                    out[k] = pieces[g][count[g]].astype(F32)

            count[to] = count[to] + 1

        @pl.when(k >= alive)
        def _():
            out[k] = jnp.zeros(out.shape[1:], F32)

        return carry

    lax.fori_loop(0, SLOTS, body, 0)


def bottom_kernel(dense, weight, bias, cot, start, low, slope, bias_sum):
    pre = jnp.dot(dense[...], weight[...], preferred_element_type=F32) + bias[...]
    sigma = 1.0 / (1.0 + jnp.exp(-pre))
    begin = (pre * sigma).astype(BF)
    start[0] = begin
    grad = cot[...].astype(F32) * begin.astype(F32)
    low[0] = grad.astype(BF)
    slope[0] = sigma * (1.0 + pre * (1.0 - sigma))
    bias_sum[...] = jnp.sum(grad, axis=0, keepdims=True)


def list_slots(groups, per_device, inb, outb, live, tin, tout):
    me = tensor_index()

    def visit(kk, source, k, total, rank):
        block = inb[source, k]
        owner = local_of(block, per_device)
        tin[total] = block + ((me ^ owner) - owner) * per_device
        tout[total] = outb[source, k] - me * per_device

    return owner_walk(me, outb, live, groups, per_device, visit)


def fetch_inputs(groups, per_device, inb, outb, live, pieces, sbuf, tin, tout, sem):
    total = list_slots(groups, per_device, inb, outb, live, tin, tout)

    def issue(j, carry):
        which = local_of(tin[j], per_device)
        col = tin[j] - which * per_device
        for g in range(groups):

            @pl.when(which == g)
            def _(g=g):
                pltpu.make_async_copy(pieces[g].at[col], sbuf.at[j], sem.at[j]).start()

        return carry

    lax.fori_loop(0, total, issue, 0)
    return total


def wait_input(pieces, sbuf, sem, j):
    pltpu.make_async_copy(pieces[0].at[0], sbuf.at[j], sem.at[j]).wait()


def block_grad_kernel(groups, per_device, half, nz, ny, inb, outb, live, *refs):
    pieces = refs[:groups]
    low, first, second = refs[groups], refs[groups + 1 : groups + 1 + nz], refs[groups + 1 + nz : groups + 1 + nz + ny]
    sbuf, tmp, tin, tout, sem = refs[groups + 1 + nz + ny :]
    total = fetch_inputs(groups, per_device, inb, outb, live, pieces, sbuf, tin, tout, sem)
    rows = first[0].shape[2]

    def body(j, carry):
        wait_input(pieces, sbuf, sem, j)
        tmp[...] = dot(sbuf[j], low[tout[j]], ((0,), (0,))).astype(BF)
        for sz in range(nz):
            for sy in range(ny):
                d = ring_from("z", nz, sz) * ny + ring_from("y", ny, sy)
                part = tmp[pl.ds(pl.multiple_of(d * rows, rows), rows), :]

                @pl.when(j < half)
                def _(sz=sz, sy=sy, part=part):
                    first[sz][sy, j] = part

                @pl.when(j >= half)
                def _(sz=sz, sy=sy, part=part):
                    second[sy][sz, j - half] = part

        return carry

    lax.fori_loop(0, total, body, 0)


def load_shards(nz, ny, shards, wbuf, wsem):
    rows = shards[0].shape[1]
    copies = []
    for sz in range(nz):
        for sy in range(ny):
            d = ring_from("z", nz, sz) * ny + ring_from("y", ny, sy)
            place = pl.ds(pl.multiple_of(d * rows, rows), rows)
            i = sz * ny + sy
            copies.append(pltpu.make_async_copy(shards[i], wbuf.at[:, place, :], wsem.at[i]))
    for copy in copies:
        copy.start()
    return copies


def back_kernel(groups, per_device, nx, nz, ny, inb, outb, live, *refs):
    low, shards = refs[0], refs[1 : 1 + nz * ny]
    back_same, back_other, wbuf, acc, tin, tout, wsem = refs[1 + nz * ny :]
    copies = load_shards(nz, ny, shards, wbuf, wsem)
    total = list_slots(groups, per_device, inb, outb, live, tin, tout)

    def clear(i, carry):
        acc[i] = jnp.zeros(acc.shape[1:], F32)
        return carry

    lax.fori_loop(0, acc.shape[0], clear, 0)
    for copy in copies:
        copy.wait()

    def body(j, carry):
        back = dot(low[tout[j]], wbuf[j], ((1,), (1,))).astype(BF).astype(F32)
        acc[tin[j]] = acc[tin[j]] + back
        return carry

    lax.fori_loop(0, total, body, 0)

    mx = lax.axis_index("x")
    for sx in range(nx):
        rel = (mx ^ ring_from("x", nx, sx)) * 2

        def spill(b, carry, sx=sx, rel=rel):
            back_same[sx, b] = acc[rel * per_device + b].astype(BF)
            back_other[sx, b] = acc[(rel + 1) * per_device + b].astype(BF)
            return carry

        lax.fori_loop(0, per_device, spill, 0)


def forward_kernel(groups, per_device, nz, ny, inb, outb, live, *refs):
    pieces = refs[:groups]
    start, cot, bias = refs[groups : groups + 3]
    shards = refs[groups + 3 : groups + 3 + nz * ny]
    cross, base, wbuf, sbuf, tin, tout, sem, wsem = refs[groups + 3 + nz * ny :]
    copies = load_shards(nz, ny, shards, wbuf, wsem)
    total = fetch_inputs(groups, per_device, inb, outb, live, pieces, sbuf, tin, tout, sem)

    def begin(b, carry):
        base[b] = jnp.broadcast_to(bias[b], base.shape[1:])
        return carry

    lax.fori_loop(0, per_device, begin, 0)
    for copy in copies:
        copy.wait()

    def body(j, carry):
        wait_input(pieces, sbuf, sem, j)
        part = dot(sbuf[j], wbuf[j], ((1,), (0,))).astype(BF).astype(F32)
        base[tout[j]] = base[tout[j]] + part
        return carry

    lax.fori_loop(0, total, body, 0)
    for b in range(per_device):
        wide = start[b].astype(F32)
        mix = base[b]
        c = cot[:, b * BLK : (b + 1) * BLK].astype(F32)
        cross[:, b * BLK : (b + 1) * BLK] = (wide * mix + wide).astype(BF)
        base[b] = c * mix + c


def pre_kernel(base, own, here, far, slope, low):
    grad = base[0] + own[0, 0].astype(F32) + here[0, 0].astype(F32) + far[0].astype(F32)
    grad = grad * slope[0]
    low[0] = grad.astype(BF)


def weight_grad_kernel(nz, ny, rows, *refs):
    grads, dense = refs[:nz], refs[nz : 2 * nz]
    own, send = refs[2 * nz :]
    column = grads[0][0].astype(F32)
    for s in range(1, nz):
        column = column + grads[s][0].astype(F32)
    column = jnp.sum(column, axis=0, keepdims=True)
    high = column.astype(BF).astype(F32)
    place = lax.broadcasted_iota(jnp.int32, (EXTRA, BLK), 0)
    own[rows:, :] = jnp.where(place == 0, column, 0.0)
    extra = jnp.where(place == 0, high, jnp.where(place == 1, column - high, 0.0)).astype(BF)
    for sy in range(ny):
        y = ring_from("y", ny, sy)
        cols = pl.ds(pl.multiple_of(y * rows, rows), rows)
        total = None
        for s in range(nz):
            term = dot(dense[s][:, cols], grads[s][0], ((0,), (0,)))
            total = term if total is None else total + term
        if sy == 0:
            own[:rows, :] = total
        else:
            send[sy - 1, :rows, :] = total.astype(BF)
            send[sy - 1, rows:, :] = extra


def final_kernel(rows, parts, *refs):
    own, far = refs[:parts], refs[parts : 2 * parts]
    out, bias = refs[-2:]
    size = out.shape[1] // parts
    for c in range(parts):
        cols = slice(c * size, (c + 1) * size)
        out[:, cols] = own[c][:rows, :] + far[c][0, :rows, :].astype(F32)
        low = jnp.sum(far[c][0, rows:, :].astype(F32), axis=0, keepdims=True)
        bias[:, cols] = own[c][rows : rows + 1, :] + low


def on_device(sizes, *args):
    dense, bottom_weight, bottom_bias, cross_blocks, cross_bias, cotangent, inb, outb, live = args
    nz, ny, nx = sizes
    groups = nx * 2
    row_count, depth = dense.shape
    local_width = bottom_weight.shape[1]
    per_device = local_width // BLK
    capacity = -(-SLOTS // groups)
    rows = cross_blocks.shape[1]
    n_dp = nz * ny
    out_rows = depth // n_dp
    plane = ny * out_rows
    smem = pltpu.SMEM
    tables = (inb, outb, live)
    sds = jax.ShapeDtypeStruct
    flip = [(0, 1), (1, 0)]

    def table_call(kernel, n_in, out_shape, scratch=(), in_specs=None, out_specs=None):
        single = not isinstance(out_shape, (tuple, list))
        return pl.pallas_call(
            kernel,
            out_shape=out_shape,
            grid_spec=pltpu.PrefetchScalarGridSpec(
                num_scalar_prefetch=3,
                grid=(),
                in_specs=in_specs or [VMEM] * n_in,
                out_specs=out_specs or (VMEM if single else [VMEM] * len(out_shape)),
                scratch_shapes=list(scratch),
            ),
            compiler_params=params(),
        )

    def swap(value, kk):
        return lax.ppermute(value, ("x", "core"), [(i, i ^ kk) for i in range(groups)])

    *packed, most = table_call(
        functools.partial(pack_kernel, groups, per_device),
        1,
        [sds((capacity, rows, BLK), BF)] * groups + [sds((1,), jnp.int32)],
        [smem((groups,), jnp.int32)],
        out_specs=[VMEM] * groups + [pl.BlockSpec(memory_space=smem)],
    )(*tables, cross_blocks)
    moved = [packed[0]] + [swap(packed[kk], kk) for kk in range(1, groups)]

    order = ring_order(nz)

    dense_tied = after(dense, packed[0])
    block = lambda dtype: pl.BlockSpec((1, row_count, BLK), lambda i: (i, 0, 0))
    line = pl.BlockSpec((1, BLK), lambda i: (0, i))
    wide = sds((per_device, row_count, BLK), F32)
    narrow = sds((per_device, row_count, BLK), BF)
    start, low, slope, bias_mixed = pl.pallas_call(
        bottom_kernel,
        grid=(per_device,),
        in_specs=[
            pl.BlockSpec((row_count, depth), lambda i: (0, 0)),
            pl.BlockSpec((depth, BLK), lambda i: (0, i)),
            line,
            pl.BlockSpec((row_count, BLK), lambda i: (0, i)),
        ],
        out_specs=[block(BF), block(BF), block(F32), line],
        out_shape=[narrow, narrow, wide, sds((1, local_width), F32)],
        compiler_params=params(("arbitrary",)),
    )(dense_tied, bottom_weight, bottom_bias.reshape(1, -1), cotangent)

    def rest(width, *operands):
        dense, start, low, slope, bias_mixed, cotangent, cross_bias = operands[:7]
        tables = operands[7:10]
        moved = operands[10:]
        half = width // 2
        shard = table_call(
            functools.partial(compact_kernel, groups, per_device),
            groups,
            sds((width, rows, BLK), BF),
        )(*tables, *moved)

        if nx == 2:
            far = lax.ppermute(start, "x", flip)
            pieces = [start, lax.ppermute(start, "core", flip), far, lax.ppermute(far, "core", flip)]
        else:
            pieces = [start] + [swap(start, kk) for kk in range(1, groups)]

        shards, z_pieces = [], []
        for i in range(nz):
            if i == 0:
                piece = shard
            else:
                source = z_pieces[-1]
                if i > 2:
                    source = after(source, shards[(i - 2) * ny - 1])
                piece = lax.ppermute(source, "z", ring_hop(nz))
            z_pieces.append(piece)
            shards += ring_gather(after(piece, shards[-1]) if i >= 2 else piece, "y", ny)

        dense_late = after(dense, z_pieces[-1])
        bias_late = after(bias_mixed, z_pieces[-1])
        dense_parts, bias = [], bias_late
        for s in range(nz):
            ahead = ring_from("z", nz, -s)
            cut = lax.dynamic_slice_in_dim(dense_late, ahead * plane, plane, 1)
            if s > 0:
                hop = [(order[p], order[(p + s) % nz]) for p in range(nz)]
                cut = lax.ppermute(cut, "z", hop)
                bias = bias + lax.ppermute(bias_late, "z", hop)
            dense_parts.append(cut)
        for piece in ring_gather(bias, "y", ny)[1:]:
            bias = bias + piece

        tabs = [smem((width,), jnp.int32), smem((width,), jnp.int32)]
        sem = pltpu.SemaphoreType.DMA((width,))
        sbuf = pltpu.VMEM((width, row_count, BLK), BF)
        wbuf = pltpu.VMEM((width, BLK, BLK), BF)
        wsem = pltpu.SemaphoreType.DMA((n_dp,))
        parts = table_call(
            functools.partial(block_grad_kernel, groups, per_device, half, nz, ny),
            groups + 1,
            [sds((ny, half, rows, BLK), BF)] * nz + [sds((nz, width - half, rows, BLK), BF)] * ny,
            [sbuf, pltpu.VMEM((BLK, BLK), BF)] + tabs + [sem],
            in_specs=[ANY] * groups + [VMEM],
        )(*tables, *pieces, low)
        z_first, y_first = list(parts[:nz]), list(parts[nz:])
        hop_z = lambda term: lax.ppermute(term, "z", ring_hop(nz))
        add = lambda a, b: (a.astype(F32) + b.astype(F32)).astype(BF)
        z_carried = hop_z(z_first[1])
        y_first[1] = after(y_first[1], shards[-1])
        y_carried = lax.ppermute(y_first[1], "y", ring_hop(ny))

        low_late = after(low, bias, z_first[1], *dense_parts)
        back = sds((nx, per_device, row_count, BLK), BF)
        back_same, back_other = table_call(
            functools.partial(back_kernel, groups, per_device, nx, nz, ny),
            1 + n_dp,
            [back, back],
            [wbuf, pltpu.VMEM((groups * per_device, row_count, BLK), F32)] + tabs + [wsem],
            in_specs=[VMEM] + [ANY] * n_dp,
        )(*tables, low_late, *shards)
        across = lax.ppermute(back_other, "core", flip)

        start_late = after(start, back_other)
        cross_out, base = table_call(
            functools.partial(forward_kernel, groups, per_device, nz, ny),
            groups + 3 + n_dp,
            [sds((row_count, local_width), BF), wide],
            [wbuf, sbuf] + tabs + [sem, wsem],
            in_specs=[ANY] * groups + [VMEM] * 3 + [ANY] * n_dp,
        )(*tables, *pieces, start_late, cotangent, cross_bias.reshape(per_device, 1, BLK), *shards)

        across = after(across, base)
        z_carried = after(z_carried, base)
        if nz > 2:
            z_carried = hop_z(add(z_first[2], z_carried))

        chunks = 4 if per_device % 4 == 0 else 1
        span = per_device // chunks
        plain = pl.BlockSpec((1, row_count, BLK), lambda i: (i, 0, 0))
        x_parts = []
        for c in range(chunks):
            sl = slice(c * span, (c + 1) * span)
            carried = None
            for sx in range(1, nx):
                term = back_same[sx, sl].astype(F32) + across[sx, sl].astype(F32)
                if carried is not None:
                    term = term + carried.astype(F32)
                term = term.astype(BF)
                if c == 0 and sx == 1:
                    z_carried, y_carried = after(z_carried, term), after(y_carried, term)
                carried = lax.ppermute(term, "x", ring_hop(nx))
            x_parts.append(carried)

        for s in range(3, nz):
            z_carried = hop_z(add(z_first[s], z_carried))
        for s in range(2, ny):
            y_carried = lax.ppermute(add(y_first[s], y_carried), "y", ring_hop(ny))
        y_sum = add(y_first[0], y_carried)
        second = ring_sum(y_sum, "z", nz)
        first = ring_sum(add(z_first[0], z_carried), "y", ny)

        owns, fars, ends = [], [], []
        for c in range(chunks):
            first_block = c * span
            carried = x_parts[c]
            shifted = pl.BlockSpec((1, row_count, BLK), lambda i, f=first_block: (i + f, 0, 0))
            own_spec = pl.BlockSpec((1, 1, row_count, BLK), lambda i, f=first_block: (0, i + f, 0, 0))
            grad_low = pl.pallas_call(
                pre_kernel,
                grid=(span,),
                in_specs=[shifted, own_spec, own_spec, plain, shifted],
                out_specs=plain,
                out_shape=sds((span, row_count, BLK), BF),
                compiler_params=params(("arbitrary",)),
            )(base, back_same, across, carried, slope)
            if c >= 2:
                grad_low = after(grad_low, ends[c - 2][-1])
            gathered = ring_gather(grad_low, "z", nz)
            ends.append(gathered)
        for c in range(chunks):
            own, send = pl.pallas_call(
                functools.partial(weight_grad_kernel, nz, ny, out_rows),
                grid=(span,),
                in_specs=[plain] * nz + [pl.BlockSpec((row_count, plane), lambda i: (0, 0))] * nz,
                out_specs=[
                    pl.BlockSpec((out_rows + EXTRA, BLK), lambda i: (0, i)),
                    pl.BlockSpec((ny - 1, out_rows + EXTRA, BLK), lambda i: (0, 0, i)),
                ],
                out_shape=[
                    sds((out_rows + EXTRA, span * BLK), F32),
                    sds((ny - 1, out_rows + EXTRA, span * BLK), BF),
                ],
                compiler_params=params(("arbitrary",)),
            )(*ends[c], *dense_parts)
            carried = None
            for sy in range(1, ny):
                term = send[sy - 1 : sy]
                if carried is not None:
                    term = (term.astype(F32) + carried.astype(F32)).astype(BF)
                carried = lax.ppermute(term, "y", ring_hop(ny))
            owns.append(own)
            fars.append(carried)

        size = span * BLK
        outs = [sds((out_rows, local_width), F32), sds((1, local_width), F32)]
        done = None
        groups_of = [range(chunks)] if chunks == 1 else [range(chunks // 2), range(chunks // 2, chunks)]
        for place, group in enumerate(groups_of):
            parts_in = [owns[c] for c in group] + [fars[c] for c in group]
            total = len(group) * size
            done = pl.pallas_call(
                functools.partial(final_kernel, out_rows, len(group)),
                grid=(1,),
                in_specs=[pl.BlockSpec(p.shape, lambda i, n=p.ndim: (0,) * n) for p in parts_in]
                + ([ANY, ANY] if done else []),
                out_specs=[
                    pl.BlockSpec((out_rows, total), lambda i, place=place: (0, place)),
                    pl.BlockSpec((1, total), lambda i, place=place: (0, place)),
                ],
                out_shape=outs,
                input_output_aliases={len(parts_in): 0, len(parts_in) + 1: 1} if done else {},
                compiler_params=params(("arbitrary",)),
            )(*parts_in, *(done or ()))
        grad_bottom, bias_pre = done

        returned = table_call(
            functools.partial(expand_kernel, groups, per_device, half),
            2,
            [sds((capacity, rows, BLK), BF)] * groups,
        )(*tables, first, second)
        returned = [returned[0]] + [swap(returned[kk], kk) for kk in range(1, groups)]
        grad_blocks = table_call(
            functools.partial(return_kernel, groups, per_device),
            groups,
            sds((SLOTS, rows, BLK), F32),
            [smem((groups,), jnp.int32)],
        )(*tables, *returned)

        return cross_out, grad_bottom, bias_pre.reshape(-1), grad_blocks, bias.reshape(-1)

    most_slots = groups * capacity
    widths = sorted({-(-most_slots * 2 // 3), -(-most_slots * 5 // 6), most_slots})
    which = sum((most[0] > w).astype(jnp.int32) for w in widths[:-1])
    return lax.switch(
        which,
        [functools.partial(rest, w) for w in widths],
        dense,
        start,
        low,
        slope,
        bias_mixed,
        cotangent,
        cross_bias,
        *tables,
        *moved,
    )


def solution(mesh):
    n_dp, groups = mesh.devices.shape
    nx = groups // 2
    ny = nx if n_dp % nx == 0 else 1
    nz = n_dp // ny
    fine = Mesh(mesh.devices.reshape(nz, ny, nx, 2), ("z", "y", "x", "core"))
    dp, tensor = ("z", "y"), ("x", "core")
    return jax.shard_map(
        functools.partial(on_device, (nz, ny, nx)),
        mesh=fine,
        in_specs=(
            P(dp, None),
            P(None, tensor),
            P(tensor),
            P(tensor, dp, None),
            P(tensor),
            P(dp, tensor),
            P(),
            P(),
            P(),
        ),
        out_specs=(
            P(dp, tensor),
            P(dp, tensor),
            P(tensor),
            P(tensor, dp, None),
            P(tensor),
        ),
        check_vma=False,
    )
```

```python
import functools

import jax
import jax.numpy as jnp
import numpy as np
from jax import lax
from jax.experimental import pallas as pl
from jax.experimental.pallas import tpu as pltpu
from jax.sharding import Mesh, PartitionSpec as P

BLK = 512
SLOTS = 10
EXTRA = 16
BF = jnp.bfloat16
F32 = jnp.float32
ANY = pl.BlockSpec(memory_space=pl.ANY)
VMEM = pl.BlockSpec(memory_space=pltpu.VMEM)
LIMIT = 56 * 1024 * 1024


def params(semantics=None):
    return pltpu.CompilerParams(vmem_limit_bytes=LIMIT, dimension_semantics=semantics)


def dot(a, b, dims):
    return lax.dot_general(a, b, (dims, ((), ())), preferred_element_type=F32)


def ring_order(n):
    return list(range(0, n, 2)) + list(range(n - 1 - (n % 2), 0, -2))


def ring_hop(n):
    order = ring_order(n)
    return [(order[p], order[(p + 1) % n]) for p in range(n)]


def ring_from(axis, n, step):
    order = ring_order(n)
    me = lax.axis_index(axis)
    behind = [0] * n
    for p in range(n):
        behind[order[p]] = order[(p - step) % n]
    result = jnp.int32(behind[0])
    for i in range(1, n):
        result = jnp.where(me == i, behind[i], result)
    return result


def after(value, *others):
    return lax.optimization_barrier((value,) + others)[0]


def ring_gather(value, axis, n):
    pieces = [value]
    for _ in range(n - 1):
        pieces.append(lax.ppermute(pieces[-1], axis, ring_hop(n)))
    return pieces


def ring_sum(terms, axis, n):
    carried = None
    for s in range(1, n):
        term = terms[s]
        if carried is not None:
            term = (term.astype(F32) + carried.astype(F32)).astype(BF)
        carried = lax.ppermute(term, axis, ring_hop(n))
    return (terms[0].astype(F32) + carried.astype(F32)).astype(BF)


def local_of(block, per_device):
    return lax.div(block, jnp.int32(per_device))


def owner_walk(me, ref, live, groups, per_device, visit):
    total = jnp.int32(0)
    for kk in range(groups):
        source = me ^ kk
        alive = live[source]
        rank = jnp.int32(0)
        for k in range(SLOTS):
            hit = (k < alive) & (local_of(ref[source, k], per_device) == me)

            @pl.when(hit)
            def _(source=source, k=k, total=total, rank=rank, kk=kk):
                visit(kk, source, k, total, rank)

            step = hit.astype(jnp.int32)
            total = total + step
            rank = rank + step
    return total


def tensor_index():
    return lax.axis_index("x") * lax.axis_size("core") + lax.axis_index("core")


def pack_kernel(groups, per_device, inb, outb, live, w, *refs):
    packed, most, count = refs[:groups], refs[groups], refs[groups + 1]
    me = tensor_index()
    for g in range(groups):
        count[g] = 0
    for t in range(groups):
        alive = live[t]

        def tally(k, carry, t=t, alive=alive):
            @pl.when(k < alive)
            def _():
                owner = local_of(outb[t, k], per_device)
                count[owner] = count[owner] + 1

            return carry

        lax.fori_loop(0, SLOTS, tally, 0)
    largest = count[0]
    for g in range(1, groups):
        largest = jnp.maximum(largest, count[g])
    most[0] = largest
    for g in range(groups):
        count[g] = 0
    alive = live[me]

    def body(k, carry):
        to = me ^ local_of(outb[me, k], per_device)

        @pl.when(k < alive)
        def _():
            for g in range(groups):

                @pl.when(to == g)
                def _(g=g):
                    packed[g][count[g]] = w[k]

            count[to] = count[to] + 1

        return carry

    lax.fori_loop(0, SLOTS, body, 0)


def compact_kernel(groups, per_device, inb, outb, live, *refs):
    pieces, out = refs[:groups], refs[groups]
    me = tensor_index()

    def visit(kk, source, k, total, rank):
        out[total] = pieces[kk][rank]

    owner_walk(me, outb, live, groups, per_device, visit)


def expand_kernel(groups, per_device, half, inb, outb, live, first, second, *packed):
    me = tensor_index()

    def visit(kk, source, k, total, rank):
        @pl.when(total < half)
        def _():
            packed[kk][rank] = first[total]

        @pl.when(total >= half)
        def _():
            packed[kk][rank] = second[total - half]

    owner_walk(me, outb, live, groups, per_device, visit)


def return_kernel(groups, per_device, inb, outb, live, *refs):
    pieces, out, count = refs[:groups], refs[groups], refs[groups + 1]
    me = tensor_index()
    for g in range(groups):
        count[g] = 0
    alive = live[me]

    def body(k, carry):
        to = me ^ local_of(outb[me, k], per_device)

        @pl.when(k < alive)
        def _():
            for g in range(groups):

                @pl.when(to == g)
                def _(g=g):
                    out[k] = pieces[g][count[g]].astype(F32)

            count[to] = count[to] + 1

        @pl.when(k >= alive)
        def _():
            out[k] = jnp.zeros(out.shape[1:], F32)

        return carry

    lax.fori_loop(0, SLOTS, body, 0)


def bottom_kernel(dense, weight, bias, cot, start, low, slope, bias_sum):
    pre = jnp.dot(dense[...], weight[...], preferred_element_type=F32) + bias[...]
    sigma = 1.0 / (1.0 + jnp.exp(-pre))
    begin = (pre * sigma).astype(BF)
    start[0] = begin
    grad = cot[...].astype(F32) * begin.astype(F32)
    low[0] = grad.astype(BF)
    slope[0] = sigma * (1.0 + pre * (1.0 - sigma))
    bias_sum[...] = jnp.sum(grad, axis=0, keepdims=True)


def list_slots(groups, per_device, inb, outb, live, tin, tout):
    me = tensor_index()

    def visit(kk, source, k, total, rank):
        block = inb[source, k]
        owner = local_of(block, per_device)
        tin[total] = block + ((me ^ owner) - owner) * per_device
        tout[total] = outb[source, k] - me * per_device

    return owner_walk(me, outb, live, groups, per_device, visit)


def fetch_inputs(groups, per_device, inb, outb, live, pieces, sbuf, tin, tout, sem):
    total = list_slots(groups, per_device, inb, outb, live, tin, tout)

    def issue(j, carry):
        which = local_of(tin[j], per_device)
        col = tin[j] - which * per_device
        for g in range(groups):

            @pl.when(which == g)
            def _(g=g):
                pltpu.make_async_copy(pieces[g].at[col], sbuf.at[j], sem.at[j]).start()

        return carry

    lax.fori_loop(0, total, issue, 0)
    return total


def wait_input(pieces, sbuf, sem, j):
    pltpu.make_async_copy(pieces[0].at[0], sbuf.at[j], sem.at[j]).wait()


def block_grad_kernel(groups, per_device, half, nz, ny, inb, outb, live, *refs):
    pieces = refs[:groups]
    low, first, second = refs[groups], refs[groups + 1 : groups + 1 + nz], refs[groups + 1 + nz : groups + 1 + nz + ny]
    sbuf, tmp, tin, tout, sem = refs[groups + 1 + nz + ny :]
    total = fetch_inputs(groups, per_device, inb, outb, live, pieces, sbuf, tin, tout, sem)
    rows = first[0].shape[2]

    def body(j, carry):
        wait_input(pieces, sbuf, sem, j)
        tmp[...] = dot(sbuf[j], low[tout[j]], ((0,), (0,))).astype(BF)
        for sz in range(nz):
            for sy in range(ny):
                d = ring_from("z", nz, sz) * ny + ring_from("y", ny, sy)
                part = tmp[pl.ds(pl.multiple_of(d * rows, rows), rows), :]

                @pl.when(j < half)
                def _(sz=sz, sy=sy, part=part):
                    first[sz][sy, j] = part

                @pl.when(j >= half)
                def _(sz=sz, sy=sy, part=part):
                    second[sy][sz, j - half] = part

        return carry

    lax.fori_loop(0, total, body, 0)


def load_shards(nz, ny, shards, wbuf, wsem):
    rows = shards[0].shape[1]
    copies = []
    for sz in range(nz):
        for sy in range(ny):
            d = ring_from("z", nz, sz) * ny + ring_from("y", ny, sy)
            place = pl.ds(pl.multiple_of(d * rows, rows), rows)
            i = sz * ny + sy
            copies.append(pltpu.make_async_copy(shards[i], wbuf.at[:, place, :], wsem.at[i]))
    for copy in copies:
        copy.start()
    return copies


def back_kernel(groups, per_device, nx, nz, ny, inb, outb, live, *refs):
    low, shards = refs[0], refs[1 : 1 + nz * ny]
    back_same, back_other, wbuf, acc, tin, tout, wsem = refs[1 + nz * ny :]
    copies = load_shards(nz, ny, shards, wbuf, wsem)
    total = list_slots(groups, per_device, inb, outb, live, tin, tout)

    def clear(i, carry):
        acc[i] = jnp.zeros(acc.shape[1:], F32)
        return carry

    lax.fori_loop(0, acc.shape[0], clear, 0)
    for copy in copies:
        copy.wait()

    def body(j, carry):
        back = dot(low[tout[j]], wbuf[j], ((1,), (1,))).astype(BF).astype(F32)
        acc[tin[j]] = acc[tin[j]] + back
        return carry

    lax.fori_loop(0, total, body, 0)

    mx = lax.axis_index("x")
    for sx in range(nx):
        rel = (mx ^ ring_from("x", nx, sx)) * 2

        def spill(b, carry, sx=sx, rel=rel):
            back_same[sx, b] = acc[rel * per_device + b].astype(BF)
            back_other[sx, b] = acc[(rel + 1) * per_device + b].astype(BF)
            return carry

        lax.fori_loop(0, per_device, spill, 0)


def forward_kernel(groups, per_device, nz, ny, inb, outb, live, *refs):
    pieces = refs[:groups]
    start, cot, bias = refs[groups : groups + 3]
    shards = refs[groups + 3 : groups + 3 + nz * ny]
    cross, base, wbuf, sbuf, tin, tout, sem, wsem = refs[groups + 3 + nz * ny :]
    copies = load_shards(nz, ny, shards, wbuf, wsem)
    total = fetch_inputs(groups, per_device, inb, outb, live, pieces, sbuf, tin, tout, sem)

    def begin(b, carry):
        base[b] = jnp.broadcast_to(bias[b], base.shape[1:])
        return carry

    lax.fori_loop(0, per_device, begin, 0)
    for copy in copies:
        copy.wait()

    def body(j, carry):
        wait_input(pieces, sbuf, sem, j)
        part = dot(sbuf[j], wbuf[j], ((1,), (0,))).astype(BF).astype(F32)
        base[tout[j]] = base[tout[j]] + part
        return carry

    lax.fori_loop(0, total, body, 0)
    for b in range(per_device):
        wide = start[b].astype(F32)
        mix = base[b]
        c = cot[:, b * BLK : (b + 1) * BLK].astype(F32)
        cross[:, b * BLK : (b + 1) * BLK] = (wide * mix + wide).astype(BF)
        base[b] = c * mix + c


def pre_kernel(base, own, here, far, slope, low):
    grad = base[0] + own[0, 0].astype(F32) + here[0, 0].astype(F32) + far[0].astype(F32)
    grad = grad * slope[0]
    low[0] = grad.astype(BF)


def weight_grad_kernel(nz, ny, rows, *refs):
    grads, (near, others, own, send) = refs[:nz], refs[nz:]
    column = grads[0][0].astype(F32)
    for s in range(1, nz):
        column = column + grads[s][0].astype(F32)
    column = jnp.sum(column, axis=0, keepdims=True)
    high = column.astype(BF).astype(F32)
    place = lax.broadcasted_iota(jnp.int32, (EXTRA, BLK), 0)
    own[rows:, :] = jnp.where(place == 0, column, 0.0)
    extra = jnp.where(place == 0, high, jnp.where(place == 1, column - high, 0.0)).astype(BF)
    for sy in range(ny):
        y = ring_from("y", ny, sy)
        cols = pl.ds(pl.multiple_of(y * rows, rows), rows)
        total = None
        for s in range(nz):
            dense = near[:, cols] if s == 0 else others[s - 1, :, cols]
            term = dot(dense, grads[s][0], ((0,), (0,)))
            total = term if total is None else total + term
        if sy == 0:
            own[:rows, :] = total
        else:
            send[sy - 1, :rows, :] = total.astype(BF)
            send[sy - 1, rows:, :] = extra


def final_kernel(rows, parts, *refs):
    own, far = refs[:parts], refs[parts : 2 * parts]
    out, bias = refs[-2:]
    size = out.shape[1] // parts
    for c in range(parts):
        cols = slice(c * size, (c + 1) * size)
        out[:, cols] = own[c][:rows, :] + far[c][0, :rows, :].astype(F32)
        low = jnp.sum(far[c][0, rows:, :].astype(F32), axis=0, keepdims=True)
        bias[:, cols] = own[c][rows : rows + 1, :] + low


def on_device(sizes, *args):
    dense, bottom_weight, bottom_bias, cross_blocks, cross_bias, cotangent, inb, outb, live = args
    nz, ny, nx = sizes
    groups = nx * 2
    row_count, depth = dense.shape
    local_width = bottom_weight.shape[1]
    per_device = local_width // BLK
    capacity = -(-SLOTS // groups)
    rows = cross_blocks.shape[1]
    n_dp = nz * ny
    out_rows = depth // n_dp
    plane = ny * out_rows
    smem = pltpu.SMEM
    tables = (inb, outb, live)
    sds = jax.ShapeDtypeStruct
    flip = [(0, 1), (1, 0)]

    def table_call(kernel, n_in, out_shape, scratch=(), in_specs=None, out_specs=None):
        single = not isinstance(out_shape, (tuple, list))
        return pl.pallas_call(
            kernel,
            out_shape=out_shape,
            grid_spec=pltpu.PrefetchScalarGridSpec(
                num_scalar_prefetch=3,
                grid=(),
                in_specs=in_specs or [VMEM] * n_in,
                out_specs=out_specs or (VMEM if single else [VMEM] * len(out_shape)),
                scratch_shapes=list(scratch),
            ),
            compiler_params=params(),
        )

    def swap(value, kk):
        return lax.ppermute(value, ("x", "core"), [(i, i ^ kk) for i in range(groups)])

    *packed, most = table_call(
        functools.partial(pack_kernel, groups, per_device),
        1,
        [sds((capacity, rows, BLK), BF)] * groups + [sds((1,), jnp.int32)],
        [smem((groups,), jnp.int32)],
        out_specs=[VMEM] * groups + [pl.BlockSpec(memory_space=smem)],
    )(*tables, cross_blocks)
    moved = [packed[0]] + [swap(packed[kk], kk) for kk in range(1, groups)]

    order = ring_order(nz)

    dense_tied = after(dense, packed[0])
    block = lambda dtype: pl.BlockSpec((1, row_count, BLK), lambda i: (i, 0, 0))
    line = pl.BlockSpec((1, BLK), lambda i: (0, i))
    wide = sds((per_device, row_count, BLK), F32)
    narrow = sds((per_device, row_count, BLK), BF)
    start, low, slope, bias_mixed = pl.pallas_call(
        bottom_kernel,
        grid=(per_device,),
        in_specs=[
            pl.BlockSpec((row_count, depth), lambda i: (0, 0)),
            pl.BlockSpec((depth, BLK), lambda i: (0, i)),
            line,
            pl.BlockSpec((row_count, BLK), lambda i: (0, i)),
        ],
        out_specs=[block(BF), block(BF), block(F32), line],
        out_shape=[narrow, narrow, wide, sds((1, local_width), F32)],
        compiler_params=params(("arbitrary",)),
    )(dense_tied, bottom_weight, bottom_bias.reshape(1, -1), cotangent)

    def rest(width, *operands):
        dense, start, low, slope, bias_mixed, cotangent, cross_bias = operands[:7]
        tables = operands[7:10]
        moved = operands[10:]
        half = width // 2
        shard = table_call(
            functools.partial(compact_kernel, groups, per_device),
            groups,
            sds((width, rows, BLK), BF),
        )(*tables, *moved)

        far = lax.ppermute(start, "x", flip) if nx == 2 else None

        def gather_start(gate):
            if nx != 2:
                return [start] + [swap(start, kk) for kk in range(1, groups)]
            late = after(far, gate)
            return [start, lax.ppermute(start, "core", flip), far, lax.ppermute(late, "core", flip)]

        tabs = [smem((width,), jnp.int32), smem((width,), jnp.int32)]
        sem = pltpu.SemaphoreType.DMA((width,))
        sbuf = pltpu.VMEM((width, row_count, BLK), BF)
        wbuf = pltpu.VMEM((width, BLK, BLK), BF)
        wsem = pltpu.SemaphoreType.DMA((n_dp,))
        def block_gradients(pieces):
            parts = table_call(
                functools.partial(block_grad_kernel, groups, per_device, half, nz, ny),
                groups + 1,
                [sds((ny, half, rows, BLK), BF)] * nz + [sds((nz, width - half, rows, BLK), BF)] * ny,
                [sbuf, pltpu.VMEM((BLK, BLK), BF)] + tabs + [sem],
                in_specs=[ANY] * groups + [VMEM],
            )(*tables, *pieces, low)
            return list(parts[:nz]), list(parts[nz:])

        shards, z_pieces = [], []
        for i in range(nz):
            if i == 0:
                piece = shard
            else:
                source = z_pieces[-1]
                if i >= 2:
                    source = after(source, shards[(i - 1) * ny - 1])
                piece = lax.ppermute(source, "z", ring_hop(nz))
            z_pieces.append(piece)
            if i == nz - 1:
                pieces = gather_start(shards[-1])
                z_first, y_first = block_gradients(pieces)
            if i >= 2:
                piece = after(piece, shards[-1])
            shards += ring_gather(piece, "y", ny)

        dense_late = after(dense, z_pieces[-1], z_first[1])
        bias_late = after(bias_mixed, z_pieces[-1], z_first[1])
        share = plane // groups
        dense_parts, bias = [], bias_late
        for s in range(1, nz):
            hop = [(order[p], order[(p + s) % nz]) for p in range(nz)]
            place = ring_from("z", nz, -s) * plane + tensor_index() * share
            cut = lax.dynamic_slice_in_dim(dense_late, place, share, 1)
            dense_parts.append(lax.ppermute(cut, "z", hop))
            bias = bias + lax.ppermute(bias_late, "z", hop)
        dense_near = lax.dynamic_slice_in_dim(dense_late, lax.axis_index("z") * plane, plane, 1)
        dense_far = lax.all_gather(jnp.stack(dense_parts), ("x", "core"), axis=2, tiled=True)
        for piece in ring_gather(bias, "y", ny)[1:]:
            bias = bias + piece

        hop_z = lambda term: lax.ppermute(term, "z", ring_hop(nz))
        add = lambda a, b: (a.astype(F32) + b.astype(F32)).astype(BF)
        z_carried = hop_z(z_first[1])
        if nz > 2:
            z_term = add(z_first[2], z_carried)
            z_carried = hop_z(z_term)
        y_first[1] = after(y_first[1], shards[-1])
        y_carried = lax.ppermute(y_first[1], "y", ring_hop(ny))

        low_late = after(low, bias, z_term, *dense_parts) if nz > 2 else low
        back = sds((nx, per_device, row_count, BLK), BF)
        back_same, back_other = table_call(
            functools.partial(back_kernel, groups, per_device, nx, nz, ny),
            1 + n_dp,
            [back, back],
            [wbuf, pltpu.VMEM((groups * per_device, row_count, BLK), F32)] + tabs + [wsem],
            in_specs=[VMEM] + [ANY] * n_dp,
        )(*tables, low_late, *shards)
        across = lax.ppermute(back_other, "core", flip)

        start_late = after(start, back_other)
        cross_out, base = table_call(
            functools.partial(forward_kernel, groups, per_device, nz, ny),
            groups + 3 + n_dp,
            [sds((row_count, local_width), BF), wide],
            [wbuf, sbuf] + tabs + [sem, wsem],
            in_specs=[ANY] * groups + [VMEM] * 3 + [ANY] * n_dp,
        )(*tables, *pieces, start_late, cotangent, cross_bias.reshape(per_device, 1, BLK), *shards)

        across = after(across, base)
        z_carried = after(z_carried, base)
        for s in range(3, nz):
            z_carried = hop_z(add(z_first[s], z_carried))

        chunks = 4 if per_device % 4 == 0 else 1
        span = per_device // chunks
        plain = pl.BlockSpec((1, row_count, BLK), lambda i: (i, 0, 0))
        x_parts = []
        for c in range(chunks):
            sl = slice(c * span, (c + 1) * span)
            carried = None
            for sx in range(1, nx):
                term = back_same[sx, sl].astype(F32) + across[sx, sl].astype(F32)
                if carried is not None:
                    term = term + carried.astype(F32)
                term = term.astype(BF)
                carried = lax.ppermute(term, "x", ring_hop(nx))
            x_parts.append(carried)

        grad_lows = []
        for c in range(chunks):
            first_block = c * span
            carried = x_parts[c]
            shifted = pl.BlockSpec((1, row_count, BLK), lambda i, f=first_block: (i + f, 0, 0))
            own_spec = pl.BlockSpec((1, 1, row_count, BLK), lambda i, f=first_block: (0, i + f, 0, 0))
            grad_low = pl.pallas_call(
                pre_kernel,
                grid=(span,),
                in_specs=[shifted, own_spec, own_spec, plain, shifted],
                out_specs=plain,
                out_shape=sds((span, row_count, BLK), BF),
                compiler_params=params(("arbitrary",)),
            )(base, back_same, across, carried, slope)
            grad_lows.append(grad_low)

        first_hops = [lax.ppermute(g, "z", ring_hop(nz)) for g in grad_lows[:2]]
        y_carried = after(y_carried, first_hops[0])
        z_carried = after(z_carried, first_hops[0])
        for s in range(2, ny):
            y_carried = lax.ppermute(add(y_first[s], y_carried), "y", ring_hop(ny))
        y_sum = add(y_first[0], y_carried)
        second = ring_sum(y_sum, "z", nz)
        first = ring_sum(add(z_first[0], z_carried), "y", ny)

        returned = table_call(
            functools.partial(expand_kernel, groups, per_device, half),
            2,
            [sds((capacity, rows, BLK), BF)] * groups,
        )(*tables, first, second)
        returned = [returned[0]] + [swap(returned[kk], kk) for kk in range(1, groups)]
        grad_blocks = table_call(
            functools.partial(return_kernel, groups, per_device),
            groups,
            sds((SLOTS, rows, BLK), F32),
            [smem((groups,), jnp.int32)],
        )(*tables, *returned)

        owns, fars, ends = [], [], []
        for c in range(chunks):
            gathered = [grad_lows[c]]
            for s in range(1, nz):
                source = gathered[-1]
                if c >= 2:
                    source = after(source, (ends, owns, fars)[min(s - 1, 2)][c - 2])
                if c == chunks - 1 and s == nz - 1:
                    source = after(source, grad_blocks)
                if s == 1 and c < len(first_hops):
                    gathered.append(first_hops[c])
                else:
                    gathered.append(lax.ppermute(source, "z", ring_hop(nz)))
            ends.append(gathered[-1])
            own, send = pl.pallas_call(
                functools.partial(weight_grad_kernel, nz, ny, out_rows),
                grid=(span,),
                in_specs=[plain] * nz
                + [
                    pl.BlockSpec((row_count, plane), lambda i: (0, 0)),
                    pl.BlockSpec((nz - 1, row_count, plane), lambda i: (0, 0, 0)),
                ],
                out_specs=[
                    pl.BlockSpec((out_rows + EXTRA, BLK), lambda i: (0, i)),
                    pl.BlockSpec((ny - 1, out_rows + EXTRA, BLK), lambda i: (0, 0, i)),
                ],
                out_shape=[
                    sds((out_rows + EXTRA, span * BLK), F32),
                    sds((ny - 1, out_rows + EXTRA, span * BLK), BF),
                ],
                compiler_params=params(("arbitrary",)),
            )(*gathered, dense_near, dense_far)
            carried = None
            for sy in range(1, ny):
                term = send[sy - 1 : sy]
                if carried is not None:
                    term = (term.astype(F32) + carried.astype(F32)).astype(BF)
                carried = lax.ppermute(term, "y", ring_hop(ny))
            owns.append(own)
            fars.append(carried)

        size = span * BLK
        outs = [sds((out_rows, local_width), F32), sds((1, local_width), F32)]
        done = None
        groups_of = [range(chunks)] if chunks == 1 else [range(chunks // 2), range(chunks // 2, chunks)]
        for place, group in enumerate(groups_of):
            parts_in = [owns[c] for c in group] + [fars[c] for c in group]
            total = len(group) * size
            done = pl.pallas_call(
                functools.partial(final_kernel, out_rows, len(group)),
                grid=(1,),
                in_specs=[pl.BlockSpec(p.shape, lambda i, n=p.ndim: (0,) * n) for p in parts_in]
                + ([ANY, ANY] if done else []),
                out_specs=[
                    pl.BlockSpec((out_rows, total), lambda i, place=place: (0, place)),
                    pl.BlockSpec((1, total), lambda i, place=place: (0, place)),
                ],
                out_shape=outs,
                input_output_aliases={len(parts_in): 0, len(parts_in) + 1: 1} if done else {},
                compiler_params=params(("arbitrary",)),
            )(*parts_in, *(done or ()))
        grad_bottom, bias_pre = done

        return cross_out, grad_bottom, bias_pre.reshape(-1), grad_blocks, bias.reshape(-1)

    most_slots = groups * capacity
    widths = sorted({-(-most_slots * 2 // 3), -(-most_slots * 5 // 6), most_slots})
    which = sum((most[0] > w).astype(jnp.int32) for w in widths[:-1])
    return lax.switch(
        which,
        [functools.partial(rest, w) for w in widths],
        dense,
        start,
        low,
        slope,
        bias_mixed,
        cotangent,
        cross_bias,
        *tables,
        *moved,
    )


def solution(mesh):
    n_dp, groups = mesh.devices.shape
    nx = groups // 2
    ny = nx if n_dp % nx == 0 else 1
    nz = n_dp // ny
    fine = Mesh(mesh.devices.reshape(nz, ny, nx, 2), ("z", "y", "x", "core"))
    dp, tensor = ("z", "y"), ("x", "core")
    return jax.shard_map(
        functools.partial(on_device, (nz, ny, nx)),
        mesh=fine,
        in_specs=(
            P(dp, None),
            P(None, tensor),
            P(tensor),
            P(tensor, dp, None),
            P(tensor),
            P(dp, tensor),
            P(),
            P(),
            P(),
        ),
        out_specs=(
            P(dp, tensor),
            P(dp, tensor),
            P(tensor),
            P(tensor, dp, None),
            P(tensor),
        ),
        check_vma=False,
    )
```

```python
import functools

import jax
import jax.numpy as jnp
import numpy as np
from jax import lax
from jax.experimental import pallas as pl
from jax.experimental.pallas import tpu as pltpu
from jax.sharding import Mesh, PartitionSpec as P

BLK = 512
SLOTS = 10
EXTRA = 16
BF = jnp.bfloat16
F32 = jnp.float32
ANY = pl.BlockSpec(memory_space=pl.ANY)
VMEM = pl.BlockSpec(memory_space=pltpu.VMEM)
LIMIT = 56 * 1024 * 1024


def params(semantics=None):
    return pltpu.CompilerParams(vmem_limit_bytes=LIMIT, dimension_semantics=semantics)


def dot(a, b, dims):
    return lax.dot_general(a, b, (dims, ((), ())), preferred_element_type=F32)


def ring_order(n):
    return list(range(0, n, 2)) + list(range(n - 1 - (n % 2), 0, -2))


def ring_hop(n):
    order = ring_order(n)
    return [(order[p], order[(p + 1) % n]) for p in range(n)]


def ring_from(axis, n, step):
    order = ring_order(n)
    me = lax.axis_index(axis)
    behind = [0] * n
    for p in range(n):
        behind[order[p]] = order[(p - step) % n]
    result = jnp.int32(behind[0])
    for i in range(1, n):
        result = jnp.where(me == i, behind[i], result)
    return result


def after(value, *others):
    return lax.optimization_barrier((value,) + others)[0]


def ring_gather(value, axis, n):
    pieces = [value]
    for _ in range(n - 1):
        pieces.append(lax.ppermute(pieces[-1], axis, ring_hop(n)))
    return pieces


def ring_sum(terms, axis, n):
    carried = None
    for s in range(1, n):
        term = terms[s]
        if carried is not None:
            term = (term.astype(F32) + carried.astype(F32)).astype(BF)
        carried = lax.ppermute(term, axis, ring_hop(n))
    return (terms[0].astype(F32) + carried.astype(F32)).astype(BF)


def local_of(block, per_device):
    return lax.div(block, jnp.int32(per_device))


def owner_walk(me, ref, live, groups, per_device, visit):
    total = jnp.int32(0)
    for kk in range(groups):
        source = me ^ kk
        alive = live[source]
        rank = jnp.int32(0)
        for k in range(SLOTS):
            hit = (k < alive) & (local_of(ref[source, k], per_device) == me)

            @pl.when(hit)
            def _(source=source, k=k, total=total, rank=rank, kk=kk):
                visit(kk, source, k, total, rank)

            step = hit.astype(jnp.int32)
            total = total + step
            rank = rank + step
    return total


def tensor_index():
    return lax.axis_index("x") * lax.axis_size("core") + lax.axis_index("core")


def pack_kernel(groups, per_device, inb, outb, live, w, *refs):
    packed, most, count = refs[:groups], refs[groups], refs[groups + 1]
    me = tensor_index()
    for g in range(groups):
        count[g] = 0
    for t in range(groups):
        alive = live[t]

        def tally(k, carry, t=t, alive=alive):
            @pl.when(k < alive)
            def _():
                owner = local_of(outb[t, k], per_device)
                count[owner] = count[owner] + 1

            return carry

        lax.fori_loop(0, SLOTS, tally, 0)
    largest = count[0]
    for g in range(1, groups):
        largest = jnp.maximum(largest, count[g])
    most[0] = largest
    for g in range(groups):
        count[g] = 0
    alive = live[me]

    def body(k, carry):
        to = me ^ local_of(outb[me, k], per_device)

        @pl.when(k < alive)
        def _():
            for g in range(groups):

                @pl.when(to == g)
                def _(g=g):
                    packed[g][count[g]] = w[k]

            count[to] = count[to] + 1

        return carry

    lax.fori_loop(0, SLOTS, body, 0)


def compact_kernel(groups, per_device, inb, outb, live, *refs):
    pieces, out = refs[:groups], refs[groups]
    me = tensor_index()

    def visit(kk, source, k, total, rank):
        out[total] = pieces[kk][rank]

    owner_walk(me, outb, live, groups, per_device, visit)


def expand_kernel(groups, per_device, half, inb, outb, live, first, second, *packed):
    me = tensor_index()

    def visit(kk, source, k, total, rank):
        @pl.when(total < half)
        def _():
            packed[kk][rank] = first[total]

        @pl.when(total >= half)
        def _():
            packed[kk][rank] = second[total - half]

    owner_walk(me, outb, live, groups, per_device, visit)


def return_kernel(groups, per_device, inb, outb, live, *refs):
    pieces, out, count = refs[:groups], refs[groups], refs[groups + 1]
    me = tensor_index()
    for g in range(groups):
        count[g] = 0
    alive = live[me]

    def body(k, carry):
        to = me ^ local_of(outb[me, k], per_device)

        @pl.when(k < alive)
        def _():
            for g in range(groups):

                @pl.when(to == g)
                def _(g=g):
                    out[k] = pieces[g][count[g]].astype(F32)

            count[to] = count[to] + 1

        @pl.when(k >= alive)
        def _():
            out[k] = jnp.zeros(out.shape[1:], F32)

        return carry

    lax.fori_loop(0, SLOTS, body, 0)


def bottom_kernel(dense, weight, bias, cot, start, low, slope, bias_sum):
    pre = jnp.dot(dense[...], weight[...], preferred_element_type=F32) + bias[...]
    sigma = 1.0 / (1.0 + jnp.exp(-pre))
    begin = (pre * sigma).astype(BF)
    start[0] = begin
    grad = cot[...].astype(F32) * begin.astype(F32)
    low[0] = grad.astype(BF)
    slope[0] = sigma * (1.0 + pre * (1.0 - sigma))
    bias_sum[...] = jnp.sum(grad, axis=0, keepdims=True)


def list_slots(groups, per_device, inb, outb, live, tin, tout):
    me = tensor_index()

    def visit(kk, source, k, total, rank):
        block = inb[source, k]
        owner = local_of(block, per_device)
        tin[total] = block + ((me ^ owner) - owner) * per_device
        tout[total] = outb[source, k] - me * per_device

    return owner_walk(me, outb, live, groups, per_device, visit)


def fetch_inputs(groups, per_device, inb, outb, live, pieces, sbuf, tin, tout, sem):
    total = list_slots(groups, per_device, inb, outb, live, tin, tout)

    def issue(j, carry):
        which = local_of(tin[j], per_device)
        col = tin[j] - which * per_device
        for g in range(groups):

            @pl.when(which == g)
            def _(g=g):
                pltpu.make_async_copy(pieces[g].at[col], sbuf.at[j], sem.at[j]).start()

        return carry

    lax.fori_loop(0, total, issue, 0)
    return total


def wait_input(pieces, sbuf, sem, j):
    pltpu.make_async_copy(pieces[0].at[0], sbuf.at[j], sem.at[j]).wait()


def block_grad_kernel(groups, per_device, half, nz, ny, inb, outb, live, *refs):
    pieces = refs[:groups]
    low, first, second = refs[groups], refs[groups + 1 : groups + 1 + nz], refs[groups + 1 + nz : groups + 1 + nz + ny]
    sbuf, tmp, tin, tout, sem = refs[groups + 1 + nz + ny :]
    total = fetch_inputs(groups, per_device, inb, outb, live, pieces, sbuf, tin, tout, sem)
    rows = first[0].shape[2]

    def body(j, carry):
        wait_input(pieces, sbuf, sem, j)
        tmp[...] = dot(sbuf[j], low[tout[j]], ((0,), (0,))).astype(BF)
        for sz in range(nz):
            for sy in range(ny):
                d = ring_from("z", nz, sz) * ny + ring_from("y", ny, sy)
                part = tmp[pl.ds(pl.multiple_of(d * rows, rows), rows), :]

                @pl.when(j < half)
                def _(sz=sz, sy=sy, part=part):
                    first[sz][sy, j] = part

                @pl.when(j >= half)
                def _(sz=sz, sy=sy, part=part):
                    second[sy][sz, j - half] = part

        return carry

    lax.fori_loop(0, total, body, 0)


def load_shards(nz, ny, shards, wbuf, wsem):
    rows = shards[0].shape[1]
    copies = []
    for sz in range(nz):
        for sy in range(ny):
            d = ring_from("z", nz, sz) * ny + ring_from("y", ny, sy)
            place = pl.ds(pl.multiple_of(d * rows, rows), rows)
            i = sz * ny + sy
            copies.append(pltpu.make_async_copy(shards[i], wbuf.at[:, place, :], wsem.at[i]))
    for copy in copies:
        copy.start()
    return copies


def back_kernel(groups, per_device, nx, nz, ny, inb, outb, live, *refs):
    low, shards = refs[0], refs[1 : 1 + nz * ny]
    back_same, back_other, wbuf, acc, tin, tout, wsem = refs[1 + nz * ny :]
    copies = load_shards(nz, ny, shards, wbuf, wsem)
    total = list_slots(groups, per_device, inb, outb, live, tin, tout)

    def clear(i, carry):
        acc[i] = jnp.zeros(acc.shape[1:], F32)
        return carry

    lax.fori_loop(0, acc.shape[0], clear, 0)
    for copy in copies:
        copy.wait()

    def body(j, carry):
        back = dot(low[tout[j]], wbuf[j], ((1,), (1,))).astype(BF).astype(F32)
        acc[tin[j]] = acc[tin[j]] + back
        return carry

    lax.fori_loop(0, total, body, 0)

    mx = lax.axis_index("x")
    for sx in range(nx):
        rel = (mx ^ ring_from("x", nx, sx)) * 2

        def spill(b, carry, sx=sx, rel=rel):
            back_same[sx, b] = acc[rel * per_device + b].astype(BF)
            back_other[sx, b] = acc[(rel + 1) * per_device + b].astype(BF)
            return carry

        lax.fori_loop(0, per_device, spill, 0)


def forward_kernel(groups, per_device, nz, ny, inb, outb, live, *refs):
    pieces = refs[:groups]
    start, cot, bias = refs[groups : groups + 3]
    shards = refs[groups + 3 : groups + 3 + nz * ny]
    cross, base, wbuf, sbuf, tin, tout, sem, wsem = refs[groups + 3 + nz * ny :]
    copies = load_shards(nz, ny, shards, wbuf, wsem)
    total = fetch_inputs(groups, per_device, inb, outb, live, pieces, sbuf, tin, tout, sem)

    def begin(b, carry):
        base[b] = jnp.broadcast_to(bias[b], base.shape[1:])
        return carry

    lax.fori_loop(0, per_device, begin, 0)
    for copy in copies:
        copy.wait()

    def body(j, carry):
        wait_input(pieces, sbuf, sem, j)
        part = dot(sbuf[j], wbuf[j], ((1,), (0,))).astype(BF).astype(F32)
        base[tout[j]] = base[tout[j]] + part
        return carry

    lax.fori_loop(0, total, body, 0)
    for b in range(per_device):
        wide = start[b].astype(F32)
        mix = base[b]
        c = cot[:, b * BLK : (b + 1) * BLK].astype(F32)
        cross[:, b * BLK : (b + 1) * BLK] = (wide * mix + wide).astype(BF)
        base[b] = c * mix + c


def pre_kernel(base, own, here, far, slope, low):
    grad = base[0] + own[0, 0].astype(F32) + here[0, 0].astype(F32) + far[0].astype(F32)
    grad = grad * slope[0]
    low[0] = grad.astype(BF)


def weight_grad_kernel(nz, ny, rows, *refs):
    grads, (near, others, own, send) = refs[:nz], refs[nz:]
    column = grads[0][0].astype(F32)
    for s in range(1, nz):
        column = column + grads[s][0].astype(F32)
    column = jnp.sum(column, axis=0, keepdims=True)
    high = column.astype(BF).astype(F32)
    place = lax.broadcasted_iota(jnp.int32, (EXTRA, BLK), 0)
    own[rows:, :] = jnp.where(place == 0, column, 0.0)
    extra = jnp.where(place == 0, high, jnp.where(place == 1, column - high, 0.0)).astype(BF)
    for sy in range(ny):
        y = ring_from("y", ny, sy)
        cols = pl.ds(pl.multiple_of(y * rows, rows), rows)
        total = None
        for s in range(nz):
            dense = near[:, cols] if s == 0 else others[s - 1, :, cols]
            term = dot(dense, grads[s][0], ((0,), (0,)))
            total = term if total is None else total + term
        if sy == 0:
            own[:rows, :] = total
        else:
            send[sy - 1, :rows, :] = total.astype(BF)
            send[sy - 1, rows:, :] = extra


def final_kernel(rows, parts, *refs):
    own, far = refs[:parts], refs[parts : 2 * parts]
    out, bias = refs[-2:]
    size = out.shape[1] // parts
    for c in range(parts):
        cols = slice(c * size, (c + 1) * size)
        out[:, cols] = own[c][:rows, :] + far[c][0, :rows, :].astype(F32)
        low = jnp.sum(far[c][0, rows:, :].astype(F32), axis=0, keepdims=True)
        bias[:, cols] = own[c][rows : rows + 1, :] + low


def on_device(sizes, *args):
    dense, bottom_weight, bottom_bias, cross_blocks, cross_bias, cotangent, inb, outb, live = args
    nz, ny, nx = sizes
    groups = nx * 2
    row_count, depth = dense.shape
    local_width = bottom_weight.shape[1]
    per_device = local_width // BLK
    capacity = -(-SLOTS // groups)
    rows = cross_blocks.shape[1]
    n_dp = nz * ny
    out_rows = depth // n_dp
    plane = ny * out_rows
    smem = pltpu.SMEM
    tables = (inb, outb, live)
    sds = jax.ShapeDtypeStruct
    flip = [(0, 1), (1, 0)]

    def table_call(kernel, n_in, out_shape, scratch=(), in_specs=None, out_specs=None):
        single = not isinstance(out_shape, (tuple, list))
        return pl.pallas_call(
            kernel,
            out_shape=out_shape,
            grid_spec=pltpu.PrefetchScalarGridSpec(
                num_scalar_prefetch=3,
                grid=(),
                in_specs=in_specs or [VMEM] * n_in,
                out_specs=out_specs or (VMEM if single else [VMEM] * len(out_shape)),
                scratch_shapes=list(scratch),
            ),
            compiler_params=params(),
        )

    def swap(value, kk):
        return lax.ppermute(value, ("x", "core"), [(i, i ^ kk) for i in range(groups)])

    *packed, most = table_call(
        functools.partial(pack_kernel, groups, per_device),
        1,
        [sds((capacity, rows, BLK), BF)] * groups + [sds((1,), jnp.int32)],
        [smem((groups,), jnp.int32)],
        out_specs=[VMEM] * groups + [pl.BlockSpec(memory_space=smem)],
    )(*tables, cross_blocks)
    moved = [packed[0]] + [swap(packed[kk], kk) for kk in range(1, groups)]

    order = ring_order(nz)

    dense_tied = after(dense, packed[0])
    block = lambda dtype: pl.BlockSpec((1, row_count, BLK), lambda i: (i, 0, 0))
    line = pl.BlockSpec((1, BLK), lambda i: (0, i))
    wide = sds((per_device, row_count, BLK), F32)
    narrow = sds((per_device, row_count, BLK), BF)
    start, low, slope, bias_mixed = pl.pallas_call(
        bottom_kernel,
        grid=(per_device,),
        in_specs=[
            pl.BlockSpec((row_count, depth), lambda i: (0, 0)),
            pl.BlockSpec((depth, BLK), lambda i: (0, i)),
            line,
            pl.BlockSpec((row_count, BLK), lambda i: (0, i)),
        ],
        out_specs=[block(BF), block(BF), block(F32), line],
        out_shape=[narrow, narrow, wide, sds((1, local_width), F32)],
        compiler_params=params(("arbitrary",)),
    )(dense_tied, bottom_weight, bottom_bias.reshape(1, -1), cotangent)

    def rest(width, *operands):
        dense, start, low, slope, bias_mixed, cotangent, cross_bias = operands[:7]
        tables = operands[7:10]
        moved = operands[10:]
        half = width // 2
        shard = table_call(
            functools.partial(compact_kernel, groups, per_device),
            groups,
            sds((width, rows, BLK), BF),
        )(*tables, *moved)

        far = lax.ppermute(start, "x", flip) if nx == 2 else None

        def gather_start(gate):
            if nx != 2:
                return [start] + [swap(start, kk) for kk in range(1, groups)]
            late = after(far, gate)
            return [start, lax.ppermute(start, "core", flip), far, lax.ppermute(late, "core", flip)]

        shards, z_pieces = [], []
        for i in range(nz):
            if i == 0:
                piece = shard
            else:
                source = z_pieces[-1] if i < 2 else after(z_pieces[-1], shards[(i - 1) * ny - 1])
                piece = lax.ppermute(source, "z", ring_hop(nz))
            z_pieces.append(piece)
            shards += ring_gather(after(piece, shards[-1]) if i >= 2 else piece, "y", ny)

        pieces = gather_start(z_pieces[min(2, nz - 1)])
        tabs = [smem((width,), jnp.int32), smem((width,), jnp.int32)]
        sem = pltpu.SemaphoreType.DMA((width,))
        sbuf = pltpu.VMEM((width, row_count, BLK), BF)
        wbuf = pltpu.VMEM((width, BLK, BLK), BF)
        wsem = pltpu.SemaphoreType.DMA((n_dp,))
        grads = table_call(
            functools.partial(block_grad_kernel, groups, per_device, half, nz, ny),
            groups + 1,
            [sds((ny, half, rows, BLK), BF)] * nz + [sds((nz, width - half, rows, BLK), BF)] * ny,
            [sbuf, pltpu.VMEM((BLK, BLK), BF)] + tabs + [sem],
            in_specs=[ANY] * groups + [VMEM],
        )(*tables, *pieces, low)
        z_first, y_first = list(grads[:nz]), list(grads[nz:])
        hop_z = lambda term: lax.ppermute(term, "z", ring_hop(nz))
        hop_y = lambda term: lax.ppermute(term, "y", ring_hop(ny))
        add = lambda a, b: (a.astype(F32) + b.astype(F32)).astype(BF)
        z_carried = hop_z(z_first[1])
        y_carried = hop_y(after(y_first[1], shards[-1]))

        low_late = after(low, z_first[1])
        back = sds((nx, per_device, row_count, BLK), BF)
        back_same, back_other = table_call(
            functools.partial(back_kernel, groups, per_device, nx, nz, ny),
            1 + n_dp,
            [back, back],
            [wbuf, pltpu.VMEM((groups * per_device, row_count, BLK), F32)] + tabs + [wsem],
            in_specs=[VMEM] + [ANY] * n_dp,
        )(*tables, low_late, *shards)
        across = lax.ppermute(back_other, "core", flip)

        start_late = after(start, back_other)
        cross_out, base = table_call(
            functools.partial(forward_kernel, groups, per_device, nz, ny),
            groups + 3 + n_dp,
            [sds((row_count, local_width), BF), wide],
            [wbuf, sbuf] + tabs + [sem, wsem],
            in_specs=[ANY] * groups + [VMEM] * 3 + [ANY] * n_dp,
        )(*tables, *pieces, start_late, cotangent, cross_bias.reshape(per_device, 1, BLK), *shards)

        across = after(across, base)
        if nz > 2:
            z_carried = hop_z(add(z_first[2], after(z_carried, base)))

        chunks = 4 if per_device % 4 == 0 else 1
        span = per_device // chunks
        plain = pl.BlockSpec((1, row_count, BLK), lambda i: (i, 0, 0))
        x_parts = []
        for c in range(chunks):
            sl = slice(c * span, (c + 1) * span)
            carried = None
            for sx in range(1, nx):
                term = back_same[sx, sl].astype(F32) + across[sx, sl].astype(F32)
                if carried is not None:
                    term = term + carried.astype(F32)
                term = term.astype(BF)
                carried = lax.ppermute(term, "x", ring_hop(nx))
            x_parts.append(carried)
            if c == min(1, chunks - 1):
                x_sent = term

        for s in range(3, nz):
            z_carried = hop_z(add(z_first[s], after(z_carried, x_sent)))
        for s in range(2, ny):
            y_carried = hop_y(add(y_first[s], y_carried))
        y_sum = add(y_first[0], after(y_carried, x_sent))
        second = hop_z(y_sum[1])

        grad_lows = []
        for c in range(chunks):
            first_block = c * span
            carried = x_parts[c]
            shifted = pl.BlockSpec((1, row_count, BLK), lambda i, f=first_block: (i + f, 0, 0))
            own_spec = pl.BlockSpec((1, 1, row_count, BLK), lambda i, f=first_block: (0, i + f, 0, 0))
            grad_low = pl.pallas_call(
                pre_kernel,
                grid=(span,),
                in_specs=[shifted, own_spec, own_spec, plain, shifted],
                out_specs=plain,
                out_shape=sds((span, row_count, BLK), BF),
                compiler_params=params(("arbitrary",)),
            )(base, back_same, across, carried, slope)
            grad_lows.append(grad_low)

        first_hops = [hop_z(g) for g in grad_lows[:2]]
        if nz > 2:
            second = hop_z(add(y_sum[2], after(second, first_hops[-1])))
        first = add(z_first[0], after(z_carried, first_hops[-1]))
        first_far = hop_y(first[1])
        for s in range(2, ny):
            first_far = hop_y(add(first[s], first_far))

        dense_late = after(dense, first_hops[0])
        bias_high = bias_mixed.astype(BF).astype(F32)
        bias_rows = jnp.concatenate([bias_high, bias_mixed - bias_high]).astype(BF)
        share = plane // groups
        bias_rows = bias_rows.reshape(-1, share)
        mail = []
        for s in range(1, nz):
            place = ring_from("z", nz, -s) * plane + tensor_index() * share
            cut = lax.dynamic_slice_in_dim(dense_late, place, share, 1)
            hop = [(order[p], order[(p + s) % nz]) for p in range(nz)]
            mail.append(lax.ppermute(jnp.concatenate([cut, bias_rows]), "z", hop))
        dense_near = lax.dynamic_slice_in_dim(dense_late, lax.axis_index("z") * plane, plane, 1)
        dense_far = lax.all_gather(
            jnp.stack([m[:row_count] for m in mail]), ("x", "core"), axis=2, tiled=True
        )
        bias = bias_mixed
        for m in mail:
            terms = m[row_count:].reshape(2, local_width).astype(F32)
            bias = bias + (terms[0:1] + terms[1:2])
        bias_ys = ring_gather(bias, "y", ny)[1:]


        owns, fars, ends = [], [], []
        for c in range(chunks):
            gathered = [grad_lows[c]]
            for s in range(1, nz):
                source = gathered[-1]
                if c >= 2:
                    source = after(source, (ends, owns, fars)[min(s - 1, 2)][c - 2])
                hop = first_hops[c] if s == 1 and c < len(first_hops) else hop_z(source)
                gathered.append(hop)
                if c == 0 and s == nz - 1:
                    for q in range(3, nz):
                        second = hop_z(add(y_sum[q], after(second, hop)))
            ends.append(gathered[-1])
            near = after(dense_near, *bias_ys) if c == 0 else dense_near
            if c == max(chunks - 2, 0):
                second = add(y_sum[0], after(second, *owns[:2]))
                first = add(first[0], after(first_far, *owns[:2]))
                returned = table_call(
                    functools.partial(expand_kernel, groups, per_device, half),
                    2,
                    [sds((capacity, rows, BLK), BF)] * groups,
                )(*tables, first, second)
                near = after(dense_near, returned[0])
                returned = [returned[0]] + [swap(returned[kk], kk) for kk in range(1, groups)]
            own, send = pl.pallas_call(
                functools.partial(weight_grad_kernel, nz, ny, out_rows),
                grid=(span,),
                in_specs=[plain] * nz
                + [
                    pl.BlockSpec((row_count, plane), lambda i: (0, 0)),
                    pl.BlockSpec((nz - 1, row_count, plane), lambda i: (0, 0, 0)),
                ],
                out_specs=[
                    pl.BlockSpec((out_rows + EXTRA, BLK), lambda i: (0, i)),
                    pl.BlockSpec((ny - 1, out_rows + EXTRA, BLK), lambda i: (0, 0, i)),
                ],
                out_shape=[
                    sds((out_rows + EXTRA, span * BLK), F32),
                    sds((ny - 1, out_rows + EXTRA, span * BLK), BF),
                ],
                compiler_params=params(("arbitrary",)),
            )(*gathered, near, dense_far)
            carried = None
            for sy in range(1, ny):
                term = send[sy - 1 : sy]
                if carried is not None:
                    term = (term.astype(F32) + carried.astype(F32)).astype(BF)
                carried = lax.ppermute(term, "y", ring_hop(ny))
            owns.append(own)
            fars.append(carried)

        grad_blocks = table_call(
            functools.partial(return_kernel, groups, per_device),
            groups,
            sds((SLOTS, rows, BLK), F32),
            [smem((groups,), jnp.int32)],
        )(*tables, returned[0], *[after(r, owns[-1]) for r in returned[1:]])

        size = span * BLK
        outs = [sds((out_rows, local_width), F32), sds((1, local_width), F32)]
        done = None
        groups_of = [range(chunks)] if chunks == 1 else [range(chunks // 2), range(chunks // 2, chunks)]
        for place, group in enumerate(groups_of):
            parts_in = [owns[c] for c in group] + [fars[c] for c in group]
            total = len(group) * size
            done = pl.pallas_call(
                functools.partial(final_kernel, out_rows, len(group)),
                grid=(1,),
                in_specs=[pl.BlockSpec(p.shape, lambda i, n=p.ndim: (0,) * n) for p in parts_in]
                + ([ANY, ANY] if done else []),
                out_specs=[
                    pl.BlockSpec((out_rows, total), lambda i, place=place: (0, place)),
                    pl.BlockSpec((1, total), lambda i, place=place: (0, place)),
                ],
                out_shape=outs,
                input_output_aliases={len(parts_in): 0, len(parts_in) + 1: 1} if done else {},
                compiler_params=params(("arbitrary",)),
            )(*parts_in, *(done or ()))
        grad_bottom, bias_pre = done

        for piece in bias_ys:
            bias = bias + piece
        return cross_out, grad_bottom, bias_pre.reshape(-1), grad_blocks, bias.reshape(-1)

    most_slots = groups * capacity
    widths = sorted({-(-most_slots * 2 // 3), -(-most_slots * 5 // 6), most_slots})
    which = sum((most[0] > w).astype(jnp.int32) for w in widths[:-1])
    return lax.switch(
        which,
        [functools.partial(rest, w) for w in widths],
        dense,
        start,
        low,
        slope,
        bias_mixed,
        cotangent,
        cross_bias,
        *tables,
        *moved,
    )


def solution(mesh):
    n_dp, groups = mesh.devices.shape
    nx = groups // 2
    ny = nx if n_dp % nx == 0 else 1
    nz = n_dp // ny
    fine = Mesh(mesh.devices.reshape(nz, ny, nx, 2), ("z", "y", "x", "core"))
    dp, tensor = ("z", "y"), ("x", "core")
    return jax.shard_map(
        functools.partial(on_device, (nz, ny, nx)),
        mesh=fine,
        in_specs=(
            P(dp, None),
            P(None, tensor),
            P(tensor),
            P(tensor, dp, None),
            P(tensor),
            P(dp, tensor),
            P(),
            P(),
            P(),
        ),
        out_specs=(
            P(dp, tensor),
            P(dp, tensor),
            P(tensor),
            P(tensor, dp, None),
            P(tensor),
        ),
        check_vma=False,
    )
```

```python
import functools

import jax
import jax.numpy as jnp
import numpy as np
from jax import lax
from jax.experimental import pallas as pl
from jax.experimental.pallas import tpu as pltpu
from jax.sharding import Mesh, PartitionSpec as P

BLK = 512
SLOTS = 10
EXTRA = 16
BF = jnp.bfloat16
F32 = jnp.float32
ANY = pl.BlockSpec(memory_space=pl.ANY)
VMEM = pl.BlockSpec(memory_space=pltpu.VMEM)
LIMIT = 56 * 1024 * 1024


def params(semantics=None):
    return pltpu.CompilerParams(vmem_limit_bytes=LIMIT, dimension_semantics=semantics)


def dot(a, b, dims):
    return lax.dot_general(a, b, (dims, ((), ())), preferred_element_type=F32)


def ring_order(n):
    return list(range(0, n, 2)) + list(range(n - 1 - (n % 2), 0, -2))


def ring_hop(n):
    order = ring_order(n)
    return [(order[p], order[(p + 1) % n]) for p in range(n)]


def ring_from(axis, n, step):
    order = ring_order(n)
    me = lax.axis_index(axis)
    behind = [0] * n
    for p in range(n):
        behind[order[p]] = order[(p - step) % n]
    result = jnp.int32(behind[0])
    for i in range(1, n):
        result = jnp.where(me == i, behind[i], result)
    return result


def after(value, *others):
    return lax.optimization_barrier((value,) + others)[0]


def ring_gather(value, axis, n):
    pieces = [value]
    for _ in range(n - 1):
        pieces.append(lax.ppermute(pieces[-1], axis, ring_hop(n)))
    return pieces


def ring_sum(terms, axis, n):
    carried = None
    for s in range(1, n):
        term = terms[s]
        if carried is not None:
            term = (term.astype(F32) + carried.astype(F32)).astype(BF)
        carried = lax.ppermute(term, axis, ring_hop(n))
    return (terms[0].astype(F32) + carried.astype(F32)).astype(BF)


def local_of(block, per_device):
    return lax.div(block, jnp.int32(per_device))


def owner_walk(me, ref, live, groups, per_device, visit):
    total = jnp.int32(0)
    for kk in range(groups):
        source = me ^ kk
        alive = live[source]
        rank = jnp.int32(0)
        for k in range(SLOTS):
            hit = (k < alive) & (local_of(ref[source, k], per_device) == me)

            @pl.when(hit)
            def _(source=source, k=k, total=total, rank=rank, kk=kk):
                visit(kk, source, k, total, rank)

            step = hit.astype(jnp.int32)
            total = total + step
            rank = rank + step
    return total


def tensor_index():
    return lax.axis_index("x") * lax.axis_size("core") + lax.axis_index("core")


def pack_kernel(groups, per_device, inb, outb, live, w, *refs):
    packed, most, count = refs[:groups], refs[groups], refs[groups + 1]
    me = tensor_index()
    for g in range(groups):
        count[g] = 0
    for t in range(groups):
        alive = live[t]

        def tally(k, carry, t=t, alive=alive):
            @pl.when(k < alive)
            def _():
                owner = local_of(outb[t, k], per_device)
                count[owner] = count[owner] + 1

            return carry

        lax.fori_loop(0, SLOTS, tally, 0)
    largest = count[0]
    for g in range(1, groups):
        largest = jnp.maximum(largest, count[g])
    most[0] = largest
    for g in range(groups):
        count[g] = 0
    alive = live[me]

    def body(k, carry):
        to = me ^ local_of(outb[me, k], per_device)

        @pl.when(k < alive)
        def _():
            for g in range(groups):

                @pl.when(to == g)
                def _(g=g):
                    packed[g][count[g]] = w[k]

            count[to] = count[to] + 1

        return carry

    lax.fori_loop(0, SLOTS, body, 0)


def compact_kernel(groups, per_device, inb, outb, live, *refs):
    pieces, out = refs[:groups], refs[groups]
    me = tensor_index()

    def visit(kk, source, k, total, rank):
        out[total] = pieces[kk][rank]

    owner_walk(me, outb, live, groups, per_device, visit)


def expand_kernel(groups, per_device, half, inb, outb, live, first, second, *packed):
    me = tensor_index()

    def visit(kk, source, k, total, rank):
        @pl.when(total < half)
        def _():
            packed[kk][rank] = first[total]

        @pl.when(total >= half)
        def _():
            packed[kk][rank] = second[total - half]

    owner_walk(me, outb, live, groups, per_device, visit)


def return_kernel(groups, per_device, inb, outb, live, *refs):
    pieces, out, count = refs[:groups], refs[groups], refs[groups + 1]
    me = tensor_index()
    for g in range(groups):
        count[g] = 0
    alive = live[me]

    def body(k, carry):
        to = me ^ local_of(outb[me, k], per_device)

        @pl.when(k < alive)
        def _():
            for g in range(groups):

                @pl.when(to == g)
                def _(g=g):
                    out[k] = pieces[g][count[g]].astype(F32)

            count[to] = count[to] + 1

        @pl.when(k >= alive)
        def _():
            out[k] = jnp.zeros(out.shape[1:], F32)

        return carry

    lax.fori_loop(0, SLOTS, body, 0)


def bottom_kernel(dense, weight, bias, cot, start, low, slope, bias_sum):
    pre = jnp.dot(dense[...], weight[...], preferred_element_type=F32) + bias[...]
    sigma = 1.0 / (1.0 + jnp.exp(-pre))
    begin = (pre * sigma).astype(BF)
    start[0] = begin
    grad = cot[...].astype(F32) * begin.astype(F32)
    low[0] = grad.astype(BF)
    slope[0] = sigma * (1.0 + pre * (1.0 - sigma))
    bias_sum[...] = jnp.sum(grad, axis=0, keepdims=True)


def list_slots(groups, per_device, inb, outb, live, tin, tout):
    me = tensor_index()

    def visit(kk, source, k, total, rank):
        block = inb[source, k]
        owner = local_of(block, per_device)
        tin[total] = block + ((me ^ owner) - owner) * per_device
        tout[total] = outb[source, k] - me * per_device

    return owner_walk(me, outb, live, groups, per_device, visit)


def fetch_inputs(groups, per_device, inb, outb, live, pieces, sbuf, tin, tout, sem):
    total = list_slots(groups, per_device, inb, outb, live, tin, tout)

    def issue(j, carry):
        which = local_of(tin[j], per_device)
        col = tin[j] - which * per_device
        for g in range(groups):

            @pl.when(which == g)
            def _(g=g):
                pltpu.make_async_copy(pieces[g].at[col], sbuf.at[j], sem.at[j]).start()

        return carry

    lax.fori_loop(0, total, issue, 0)
    return total


def wait_input(pieces, sbuf, sem, j):
    pltpu.make_async_copy(pieces[0].at[0], sbuf.at[j], sem.at[j]).wait()


def block_grad_kernel(groups, per_device, half, nz, ny, inb, outb, live, *refs):
    pieces = refs[:groups]
    low, first, second = refs[groups], refs[groups + 1 : groups + 1 + nz], refs[groups + 1 + nz : groups + 1 + nz + ny]
    sbuf, tmp, tin, tout, sem = refs[groups + 1 + nz + ny :]
    total = fetch_inputs(groups, per_device, inb, outb, live, pieces, sbuf, tin, tout, sem)
    rows = first[0].shape[2]

    def body(j, carry):
        wait_input(pieces, sbuf, sem, j)
        tmp[...] = dot(sbuf[j], low[tout[j]], ((0,), (0,))).astype(BF)
        for sz in range(nz):
            for sy in range(ny):
                d = ring_from("z", nz, sz) * ny + ring_from("y", ny, sy)
                part = tmp[pl.ds(pl.multiple_of(d * rows, rows), rows), :]

                @pl.when(j < half)
                def _(sz=sz, sy=sy, part=part):
                    first[sz][sy, j] = part

                @pl.when(j >= half)
                def _(sz=sz, sy=sy, part=part):
                    second[sy][sz, j - half] = part

        return carry

    lax.fori_loop(0, total, body, 0)


def load_shards(nz, ny, shards, wbuf, wsem):
    rows = shards[0].shape[1]
    copies = []
    for sz in range(nz):
        for sy in range(ny):
            d = ring_from("z", nz, sz) * ny + ring_from("y", ny, sy)
            place = pl.ds(pl.multiple_of(d * rows, rows), rows)
            i = sz * ny + sy
            copies.append(pltpu.make_async_copy(shards[i], wbuf.at[:, place, :], wsem.at[i]))
    for copy in copies:
        copy.start()
    return copies


def back_kernel(groups, per_device, nx, nz, ny, inb, outb, live, *refs):
    low, shards = refs[0], refs[1 : 1 + nz * ny]
    back_same, back_other, wbuf, acc, tin, tout, wsem = refs[1 + nz * ny :]
    copies = load_shards(nz, ny, shards, wbuf, wsem)
    total = list_slots(groups, per_device, inb, outb, live, tin, tout)

    def clear(i, carry):
        acc[i] = jnp.zeros(acc.shape[1:], F32)
        return carry

    lax.fori_loop(0, acc.shape[0], clear, 0)
    for copy in copies:
        copy.wait()

    def body(j, carry):
        back = dot(low[tout[j]], wbuf[j], ((1,), (1,))).astype(BF).astype(F32)
        acc[tin[j]] = acc[tin[j]] + back
        return carry

    lax.fori_loop(0, total, body, 0)

    mx = lax.axis_index("x")
    for sx in range(nx):
        rel = (mx ^ ring_from("x", nx, sx)) * 2

        def spill(b, carry, sx=sx, rel=rel):
            back_same[sx, b] = acc[rel * per_device + b].astype(BF)
            back_other[sx, b] = acc[(rel + 1) * per_device + b].astype(BF)
            return carry

        lax.fori_loop(0, per_device, spill, 0)


def forward_kernel(groups, per_device, nz, ny, inb, outb, live, *refs):
    pieces = refs[:groups]
    start, cot, bias = refs[groups : groups + 3]
    shards = refs[groups + 3 : groups + 3 + nz * ny]
    cross, base, wbuf, sbuf, tin, tout, sem, wsem = refs[groups + 3 + nz * ny :]
    copies = load_shards(nz, ny, shards, wbuf, wsem)
    total = fetch_inputs(groups, per_device, inb, outb, live, pieces, sbuf, tin, tout, sem)

    def begin(b, carry):
        base[b] = jnp.broadcast_to(bias[b], base.shape[1:])
        return carry

    lax.fori_loop(0, per_device, begin, 0)
    for copy in copies:
        copy.wait()

    def body(j, carry):
        wait_input(pieces, sbuf, sem, j)
        part = dot(sbuf[j], wbuf[j], ((1,), (0,))).astype(BF).astype(F32)
        base[tout[j]] = base[tout[j]] + part
        return carry

    lax.fori_loop(0, total, body, 0)
    for b in range(per_device):
        wide = start[b].astype(F32)
        mix = base[b]
        c = cot[:, b * BLK : (b + 1) * BLK].astype(F32)
        cross[:, b * BLK : (b + 1) * BLK] = (wide * mix + wide).astype(BF)
        base[b] = c * mix + c


def pre_kernel(base, own, here, far, slope, low):
    grad = base[0] + own[0, 0].astype(F32) + here[0, 0].astype(F32) + far[0].astype(F32)
    grad = grad * slope[0]
    low[0] = grad.astype(BF)


def weight_grad_kernel(nz, ny, rows, *refs):
    grads, (near, others, own, send, turned, joined) = refs[:nz], refs[nz:]
    count = near.shape[0]

    @pl.when(pl.program_id(0) == 0)
    def _():
        for s in range(nz):
            dense = near[...] if s == 0 else others[s - 1]
            turned[:, s * count : (s + 1) * count] = dense.astype(F32).T.astype(BF)

    for s in range(nz):
        joined[s * count : (s + 1) * count, :] = grads[s][0]
    column = jnp.sum(joined[...].astype(F32), axis=0, keepdims=True)
    high = column.astype(BF).astype(F32)
    place = lax.broadcasted_iota(jnp.int32, (EXTRA, BLK), 0)
    own[rows:, :] = jnp.where(place == 0, column, 0.0)
    extra = jnp.where(place == 0, high, jnp.where(place == 1, column - high, 0.0)).astype(BF)
    for sy in range(ny):
        place = pl.ds(pl.multiple_of(ring_from("y", ny, sy) * rows, rows), rows)
        total = dot(turned[place, :], joined[...], ((1,), (0,)))
        if sy == 0:
            own[:rows, :] = total
        else:
            send[sy - 1, :rows, :] = total.astype(BF)
            send[sy - 1, rows:, :] = extra


def final_kernel(rows, parts, *refs):
    own, far = refs[:parts], refs[parts : 2 * parts]
    out, bias = refs[-2:]
    size = out.shape[1] // parts
    for c in range(parts):
        cols = slice(c * size, (c + 1) * size)
        out[:, cols] = own[c][:rows, :] + far[c][0, :rows, :].astype(F32)
        low = jnp.sum(far[c][0, rows:, :].astype(F32), axis=0, keepdims=True)
        bias[:, cols] = own[c][rows : rows + 1, :] + low


def on_device(sizes, *args):
    dense, bottom_weight, bottom_bias, cross_blocks, cross_bias, cotangent, inb, outb, live = args
    nz, ny, nx = sizes
    groups = nx * 2
    row_count, depth = dense.shape
    local_width = bottom_weight.shape[1]
    per_device = local_width // BLK
    capacity = -(-SLOTS // groups)
    rows = cross_blocks.shape[1]
    n_dp = nz * ny
    out_rows = depth // n_dp
    plane = ny * out_rows
    smem = pltpu.SMEM
    tables = (inb, outb, live)
    sds = jax.ShapeDtypeStruct
    flip = [(0, 1), (1, 0)]

    def table_call(kernel, n_in, out_shape, scratch=(), in_specs=None, out_specs=None):
        single = not isinstance(out_shape, (tuple, list))
        return pl.pallas_call(
            kernel,
            out_shape=out_shape,
            grid_spec=pltpu.PrefetchScalarGridSpec(
                num_scalar_prefetch=3,
                grid=(),
                in_specs=in_specs or [VMEM] * n_in,
                out_specs=out_specs or (VMEM if single else [VMEM] * len(out_shape)),
                scratch_shapes=list(scratch),
            ),
            compiler_params=params(),
        )

    def swap(value, kk):
        return lax.ppermute(value, ("x", "core"), [(i, i ^ kk) for i in range(groups)])

    *packed, most = table_call(
        functools.partial(pack_kernel, groups, per_device),
        1,
        [sds((capacity, rows, BLK), BF)] * groups + [sds((1,), jnp.int32)],
        [smem((groups,), jnp.int32)],
        out_specs=[VMEM] * groups + [pl.BlockSpec(memory_space=smem)],
    )(*tables, cross_blocks)
    moved = [packed[0]] + [swap(packed[kk], kk) for kk in range(1, groups)]

    order = ring_order(nz)

    dense_tied = after(dense, packed[0])
    block = lambda dtype: pl.BlockSpec((1, row_count, BLK), lambda i: (i, 0, 0))
    line = pl.BlockSpec((1, BLK), lambda i: (0, i))
    wide = sds((per_device, row_count, BLK), F32)
    narrow = sds((per_device, row_count, BLK), BF)
    start, low, slope, bias_mixed = pl.pallas_call(
        bottom_kernel,
        grid=(per_device,),
        in_specs=[
            pl.BlockSpec((row_count, depth), lambda i: (0, 0)),
            pl.BlockSpec((depth, BLK), lambda i: (0, i)),
            line,
            pl.BlockSpec((row_count, BLK), lambda i: (0, i)),
        ],
        out_specs=[block(BF), block(BF), block(F32), line],
        out_shape=[narrow, narrow, wide, sds((1, local_width), F32)],
        compiler_params=params(("arbitrary",)),
    )(dense_tied, bottom_weight, bottom_bias.reshape(1, -1), cotangent)

    def rest(width, *operands):
        dense, start, low, slope, bias_mixed, cotangent, cross_bias = operands[:7]
        tables = operands[7:10]
        moved = operands[10:]
        half = width // 2
        shard = table_call(
            functools.partial(compact_kernel, groups, per_device),
            groups,
            sds((width, rows, BLK), BF),
        )(*tables, *moved)

        far = lax.ppermute(start, "x", flip) if nx == 2 else None

        def gather_start(gate):
            if nx != 2:
                return [start] + [swap(start, kk) for kk in range(1, groups)]
            late = after(far, gate)
            return [start, lax.ppermute(start, "core", flip), far, lax.ppermute(late, "core", flip)]

        shards, z_pieces = [], []
        for i in range(nz):
            if i == 0:
                piece = shard
            else:
                source = z_pieces[-1] if i < 2 else after(z_pieces[-1], shards[(i - 1) * ny - 1])
                piece = lax.ppermute(source, "z", ring_hop(nz))
            z_pieces.append(piece)
            shards += ring_gather(after(piece, shards[-1]) if i >= 2 else piece, "y", ny)

        dense_late = after(dense, shards[2 * ny - 1])
        bias_high = bias_mixed.astype(BF).astype(F32)
        bias_rows = jnp.concatenate([bias_high, bias_mixed - bias_high]).astype(BF)
        share = plane // groups
        bias_rows = bias_rows.reshape(-1, share)
        mail = []
        for s in range(1, nz):
            place = ring_from("z", nz, -s) * plane + tensor_index() * share
            cut = lax.dynamic_slice_in_dim(dense_late, place, share, 1)
            hop = [(order[p], order[(p + s) % nz]) for p in range(nz)]
            mail.append(lax.ppermute(jnp.concatenate([cut, bias_rows]), "z", hop))
        dense_near = lax.dynamic_slice_in_dim(dense_late, lax.axis_index("z") * plane, plane, 1)
        shares = jnp.stack([m[:row_count] for m in mail])
        dense_far = lax.all_gather(shares, ("x", "core"), axis=2, tiled=True)
        bias = bias_mixed
        for m in mail:
            terms = m[row_count:].reshape(2, local_width).astype(F32)
            bias = bias + (terms[0:1] + terms[1:2])
        bias_ys = ring_gather(bias, "y", ny)[1:]


        pieces = gather_start(z_pieces[min(2, nz - 1)])
        tabs = [smem((width,), jnp.int32), smem((width,), jnp.int32)]
        sem = pltpu.SemaphoreType.DMA((width,))
        sbuf = pltpu.VMEM((width, row_count, BLK), BF)
        wbuf = pltpu.VMEM((width, BLK, BLK), BF)
        wsem = pltpu.SemaphoreType.DMA((n_dp,))
        grads = table_call(
            functools.partial(block_grad_kernel, groups, per_device, half, nz, ny),
            groups + 1,
            [sds((ny, half, rows, BLK), BF)] * nz + [sds((nz, width - half, rows, BLK), BF)] * ny,
            [sbuf, pltpu.VMEM((BLK, BLK), BF)] + tabs + [sem],
            in_specs=[ANY] * groups + [VMEM],
        )(*tables, *pieces, low)
        z_first, y_first = list(grads[:nz]), list(grads[nz:])
        hop_z = lambda term: lax.ppermute(term, "z", ring_hop(nz))
        hop_y = lambda term: lax.ppermute(term, "y", ring_hop(ny))
        add = lambda a, b: (a.astype(F32) + b.astype(F32)).astype(BF)
        z_carried = hop_z(z_first[1])
        y_carried = hop_y(after(y_first[1], shards[-1]))

        low_late = after(low, z_first[1], shares)
        back = sds((nx, per_device, row_count, BLK), BF)
        back_same, back_other = table_call(
            functools.partial(back_kernel, groups, per_device, nx, nz, ny),
            1 + n_dp,
            [back, back],
            [wbuf, pltpu.VMEM((groups * per_device, row_count, BLK), F32)] + tabs + [wsem],
            in_specs=[VMEM] + [ANY] * n_dp,
        )(*tables, low_late, *shards)
        across = lax.ppermute(back_other, "core", flip)

        start_late = after(start, back_other)
        cross_out, base = table_call(
            functools.partial(forward_kernel, groups, per_device, nz, ny),
            groups + 3 + n_dp,
            [sds((row_count, local_width), BF), wide],
            [wbuf, sbuf] + tabs + [sem, wsem],
            in_specs=[ANY] * groups + [VMEM] * 3 + [ANY] * n_dp,
        )(*tables, *pieces, start_late, cotangent, cross_bias.reshape(per_device, 1, BLK), *shards)

        across = after(across, base)
        if nz > 2:
            z_carried = hop_z(add(z_first[2], after(z_carried, base)))

        chunks = 4 if per_device % 4 == 0 else 1
        span = per_device // chunks
        plain = pl.BlockSpec((1, row_count, BLK), lambda i: (i, 0, 0))
        x_parts = []
        for c in range(chunks):
            sl = slice(c * span, (c + 1) * span)
            carried = None
            for sx in range(1, nx):
                term = back_same[sx, sl].astype(F32) + across[sx, sl].astype(F32)
                if carried is not None:
                    term = term + carried.astype(F32)
                term = term.astype(BF)
                carried = lax.ppermute(term, "x", ring_hop(nx))
            x_parts.append(carried)
            if c == min(1, chunks - 1):
                x_sent = term

        for s in range(3, nz):
            z_carried = hop_z(add(z_first[s], after(z_carried, x_sent)))
        for s in range(2, ny):
            y_carried = hop_y(add(y_first[s], y_carried))
        y_sum = add(y_first[0], after(y_carried, x_sent))
        second = hop_z(y_sum[1])

        grad_lows = []
        for c in range(chunks):
            first_block = c * span
            carried = x_parts[c]
            shifted = pl.BlockSpec((1, row_count, BLK), lambda i, f=first_block: (i + f, 0, 0))
            own_spec = pl.BlockSpec((1, 1, row_count, BLK), lambda i, f=first_block: (0, i + f, 0, 0))
            grad_low = pl.pallas_call(
                pre_kernel,
                grid=(span,),
                in_specs=[shifted, own_spec, own_spec, plain, shifted],
                out_specs=plain,
                out_shape=sds((span, row_count, BLK), BF),
                compiler_params=params(("arbitrary",)),
            )(base, back_same, across, carried, slope)
            grad_lows.append(grad_low)

        first_hops = [hop_z(g) for g in grad_lows[:2]]
        if nz > 2:
            second = hop_z(add(y_sum[2], second))
        first = add(z_first[0], after(z_carried, first_hops[-1]))
        first_far = hop_y(first[1])
        for s in range(2, ny):
            first_far = hop_y(add(first[s], first_far))

        owns, fars, ends = [], [], []
        for c in range(chunks):
            gathered = [grad_lows[c]]
            for s in range(1, nz):
                source = gathered[-1]
                if c >= 2:
                    source = after(source, (ends, owns, fars)[min(s - 1, 2)][c - 2])
                hop = first_hops[c] if s == 1 and c < len(first_hops) else hop_z(source)
                gathered.append(hop)
            ends.append(gathered[-1])
            near = after(dense_near, *bias_ys) if c == 0 else dense_near
            if c == chunks - 1:
                second = add(y_sum[0], after(second, *owns[:2], *gathered[2:3]))
                first = add(first[0], after(first_far, *owns[:2]))
                returned = table_call(
                    functools.partial(expand_kernel, groups, per_device, half),
                    2,
                    [sds((capacity, rows, BLK), BF)] * groups,
                )(*tables, first, second)
                near = after(dense_near, returned[0])
                returned = [returned[0]] + [swap(returned[kk], kk) for kk in range(1, groups)]
            own, send = pl.pallas_call(
                functools.partial(weight_grad_kernel, nz, ny, out_rows),
                grid=(span,),
                in_specs=[plain] * nz
                + [
                    pl.BlockSpec((row_count, plane), lambda i: (0, 0)),
                    pl.BlockSpec((nz - 1, row_count, plane), lambda i: (0, 0, 0)),
                ],
                out_specs=[
                    pl.BlockSpec((out_rows + EXTRA, BLK), lambda i: (0, i)),
                    pl.BlockSpec((ny - 1, out_rows + EXTRA, BLK), lambda i: (0, 0, i)),
                ],
                out_shape=[
                    sds((out_rows + EXTRA, span * BLK), F32),
                    sds((ny - 1, out_rows + EXTRA, span * BLK), BF),
                ],
                scratch_shapes=[
                    pltpu.VMEM((plane, nz * row_count), BF),
                    pltpu.VMEM((nz * row_count, BLK), BF),
                ],
                compiler_params=params(("arbitrary",)),
            )(*gathered, near, dense_far)
            carried = None
            for sy in range(1, ny):
                term = send[sy - 1 : sy]
                if carried is not None:
                    term = (term.astype(F32) + carried.astype(F32)).astype(BF)
                carried = lax.ppermute(term, "y", ring_hop(ny))
            owns.append(own)
            fars.append(carried)
            if c == min(1, chunks - 1):
                for q in range(3, nz):
                    second = hop_z(add(y_sum[q], after(second, own)))

        grad_blocks = table_call(
            functools.partial(return_kernel, groups, per_device),
            groups,
            sds((SLOTS, rows, BLK), F32),
            [smem((groups,), jnp.int32)],
        )(*tables, returned[0], *[after(r, owns[-1]) for r in returned[1:]])

        size = span * BLK
        outs = [sds((out_rows, local_width), F32), sds((1, local_width), F32)]
        done = None
        groups_of = [range(chunks)] if chunks == 1 else [range(chunks // 2), range(chunks // 2, chunks)]
        for place, group in enumerate(groups_of):
            parts_in = [owns[c] for c in group] + [fars[c] for c in group]
            total = len(group) * size
            done = pl.pallas_call(
                functools.partial(final_kernel, out_rows, len(group)),
                grid=(1,),
                in_specs=[pl.BlockSpec(p.shape, lambda i, n=p.ndim: (0,) * n) for p in parts_in]
                + ([ANY, ANY] if done else []),
                out_specs=[
                    pl.BlockSpec((out_rows, total), lambda i, place=place: (0, place)),
                    pl.BlockSpec((1, total), lambda i, place=place: (0, place)),
                ],
                out_shape=outs,
                input_output_aliases={len(parts_in): 0, len(parts_in) + 1: 1} if done else {},
                compiler_params=params(("arbitrary",)),
            )(*parts_in, *(done or ()))
        grad_bottom, bias_pre = done

        for piece in bias_ys:
            bias = bias + piece
        return cross_out, grad_bottom, bias_pre.reshape(-1), grad_blocks, bias.reshape(-1)

    most_slots = groups * capacity
    widths = sorted({-(-most_slots * 2 // 3), -(-most_slots * 5 // 6), most_slots})
    which = sum((most[0] > w).astype(jnp.int32) for w in widths[:-1])
    return lax.switch(
        which,
        [functools.partial(rest, w) for w in widths],
        dense,
        start,
        low,
        slope,
        bias_mixed,
        cotangent,
        cross_bias,
        *tables,
        *moved,
    )


def solution(mesh):
    n_dp, groups = mesh.devices.shape
    nx = groups // 2
    ny = nx if n_dp % nx == 0 else 1
    nz = n_dp // ny
    fine = Mesh(mesh.devices.reshape(nz, ny, nx, 2), ("z", "y", "x", "core"))
    dp, tensor = ("z", "y"), ("x", "core")
    return jax.shard_map(
        functools.partial(on_device, (nz, ny, nx)),
        mesh=fine,
        in_specs=(
            P(dp, None),
            P(None, tensor),
            P(tensor),
            P(tensor, dp, None),
            P(tensor),
            P(dp, tensor),
            P(),
            P(),
            P(),
        ),
        out_specs=(
            P(dp, tensor),
            P(dp, tensor),
            P(tensor),
            P(tensor, dp, None),
            P(tensor),
        ),
        check_vma=False,
    )
```

```python
import functools

import jax
import jax.numpy as jnp
import numpy as np
from jax import lax
from jax.experimental import pallas as pl
from jax.experimental.pallas import tpu as pltpu
from jax.sharding import Mesh, PartitionSpec as P

BLK = 512
SLOTS = 10
EXTRA = 16
BF = jnp.bfloat16
F32 = jnp.float32
ANY = pl.BlockSpec(memory_space=pl.ANY)
VMEM = pl.BlockSpec(memory_space=pltpu.VMEM)
LIMIT = 56 * 1024 * 1024


def params(semantics=None):
    return pltpu.CompilerParams(vmem_limit_bytes=LIMIT, dimension_semantics=semantics)


def dot(a, b, dims):
    return lax.dot_general(a, b, (dims, ((), ())), preferred_element_type=F32)


def ring_order(n):
    return list(range(0, n, 2)) + list(range(n - 1 - (n % 2), 0, -2))


def ring_hop(n):
    order = ring_order(n)
    return [(order[p], order[(p + 1) % n]) for p in range(n)]


def ring_from(axis, n, step):
    order = ring_order(n)
    me = lax.axis_index(axis)
    behind = [0] * n
    for p in range(n):
        behind[order[p]] = order[(p - step) % n]
    result = jnp.int32(behind[0])
    for i in range(1, n):
        result = jnp.where(me == i, behind[i], result)
    return result


def after(value, *others):
    return lax.optimization_barrier((value,) + others)[0]


def ring_gather(value, axis, n):
    pieces = [value]
    for _ in range(n - 1):
        pieces.append(lax.ppermute(pieces[-1], axis, ring_hop(n)))
    return pieces


def ring_sum(terms, axis, n):
    carried = None
    for s in range(1, n):
        term = terms[s]
        if carried is not None:
            term = (term.astype(F32) + carried.astype(F32)).astype(BF)
        carried = lax.ppermute(term, axis, ring_hop(n))
    return (terms[0].astype(F32) + carried.astype(F32)).astype(BF)


def local_of(block, per_device):
    return lax.div(block, jnp.int32(per_device))


def owner_walk(me, ref, live, groups, per_device, visit):
    total = jnp.int32(0)
    for kk in range(groups):
        source = me ^ kk
        alive = live[source]
        rank = jnp.int32(0)
        for k in range(SLOTS):
            hit = (k < alive) & (local_of(ref[source, k], per_device) == me)

            @pl.when(hit)
            def _(source=source, k=k, total=total, rank=rank, kk=kk):
                visit(kk, source, k, total, rank)

            step = hit.astype(jnp.int32)
            total = total + step
            rank = rank + step
    return total


def tensor_index():
    return lax.axis_index("x") * lax.axis_size("core") + lax.axis_index("core")


def pack_kernel(groups, per_device, inb, outb, live, w, *refs):
    packed, most, count = refs[:groups], refs[groups], refs[groups + 1]
    me = tensor_index()
    for g in range(groups):
        count[g] = 0
    for t in range(groups):
        alive = live[t]

        def tally(k, carry, t=t, alive=alive):
            @pl.when(k < alive)
            def _():
                owner = local_of(outb[t, k], per_device)
                count[owner] = count[owner] + 1

            return carry

        lax.fori_loop(0, SLOTS, tally, 0)
    largest = count[0]
    for g in range(1, groups):
        largest = jnp.maximum(largest, count[g])
    most[0] = largest
    for g in range(groups):
        count[g] = 0
    alive = live[me]

    def body(k, carry):
        to = me ^ local_of(outb[me, k], per_device)

        @pl.when(k < alive)
        def _():
            for g in range(groups):

                @pl.when(to == g)
                def _(g=g):
                    packed[g][count[g]] = w[k]

            count[to] = count[to] + 1

        return carry

    lax.fori_loop(0, SLOTS, body, 0)


def compact_kernel(groups, per_device, inb, outb, live, *refs):
    pieces, out = refs[:groups], refs[groups]
    me = tensor_index()

    def visit(kk, source, k, total, rank):
        out[total] = pieces[kk][rank]

    owner_walk(me, outb, live, groups, per_device, visit)


def expand_kernel(groups, per_device, half, inb, outb, live, first, second, *packed):
    me = tensor_index()

    def visit(kk, source, k, total, rank):
        @pl.when(total < half)
        def _():
            packed[kk][rank] = first[total]

        @pl.when(total >= half)
        def _():
            packed[kk][rank] = second[total - half]

    owner_walk(me, outb, live, groups, per_device, visit)


def return_kernel(groups, per_device, inb, outb, live, *refs):
    pieces, out, count = refs[:groups], refs[groups], refs[groups + 1]
    me = tensor_index()
    for g in range(groups):
        count[g] = 0
    alive = live[me]

    def body(k, carry):
        to = me ^ local_of(outb[me, k], per_device)

        @pl.when(k < alive)
        def _():
            for g in range(groups):

                @pl.when(to == g)
                def _(g=g):
                    out[k] = pieces[g][count[g]].astype(F32)

            count[to] = count[to] + 1

        @pl.when(k >= alive)
        def _():
            out[k] = jnp.zeros(out.shape[1:], F32)

        return carry

    lax.fori_loop(0, SLOTS, body, 0)


def bottom_kernel(dense, weight, bias, cot, start, low, slope, bias_sum):
    pre = jnp.dot(dense[...], weight[...], preferred_element_type=F32) + bias[...]
    sigma = 1.0 / (1.0 + jnp.exp(-pre))
    begin = (pre * sigma).astype(BF)
    start[0] = begin
    grad = cot[...].astype(F32) * begin.astype(F32)
    low[0] = grad.astype(BF)
    slope[0] = sigma * (1.0 + pre * (1.0 - sigma))
    bias_sum[...] = jnp.sum(grad, axis=0, keepdims=True)


def list_slots(groups, per_device, inb, outb, live, tin, tout):
    me = tensor_index()

    def visit(kk, source, k, total, rank):
        block = inb[source, k]
        owner = local_of(block, per_device)
        tin[total] = block + ((me ^ owner) - owner) * per_device
        tout[total] = outb[source, k] - me * per_device

    return owner_walk(me, outb, live, groups, per_device, visit)


def fetch_inputs(groups, per_device, inb, outb, live, pieces, sbuf, tin, tout, sem):
    total = list_slots(groups, per_device, inb, outb, live, tin, tout)

    def issue(j, carry):
        which = local_of(tin[j], per_device)
        col = tin[j] - which * per_device
        for g in range(groups):

            @pl.when(which == g)
            def _(g=g):
                pltpu.make_async_copy(pieces[g].at[col], sbuf.at[j], sem.at[j]).start()

        return carry

    lax.fori_loop(0, total, issue, 0)
    return total


def wait_input(pieces, sbuf, sem, j):
    pltpu.make_async_copy(pieces[0].at[0], sbuf.at[j], sem.at[j]).wait()


def block_grad_kernel(groups, per_device, half, nz, ny, inb, outb, live, *refs):
    pieces = refs[:groups]
    low, first, second = refs[groups], refs[groups + 1 : groups + 1 + nz], refs[groups + 1 + nz : groups + 1 + nz + ny]
    sbuf, tmp, tin, tout, sem = refs[groups + 1 + nz + ny :]
    total = fetch_inputs(groups, per_device, inb, outb, live, pieces, sbuf, tin, tout, sem)
    rows = first[0].shape[2]

    def body(j, carry):
        wait_input(pieces, sbuf, sem, j)
        tmp[...] = dot(sbuf[j], low[tout[j]], ((0,), (0,))).astype(BF)
        for sz in range(nz):
            for sy in range(ny):
                d = ring_from("z", nz, sz) * ny + ring_from("y", ny, sy)
                part = tmp[pl.ds(pl.multiple_of(d * rows, rows), rows), :]

                @pl.when(j < half)
                def _(sz=sz, sy=sy, part=part):
                    first[sz][sy, j] = part

                @pl.when(j >= half)
                def _(sz=sz, sy=sy, part=part):
                    second[sy][sz, j - half] = part

        return carry

    lax.fori_loop(0, total, body, 0)


def load_shards(nz, ny, shards, wbuf, wsem):
    rows = shards[0].shape[1]
    copies = []
    for sz in range(nz):
        for sy in range(ny):
            d = ring_from("z", nz, sz) * ny + ring_from("y", ny, sy)
            place = pl.ds(pl.multiple_of(d * rows, rows), rows)
            i = sz * ny + sy
            copies.append(pltpu.make_async_copy(shards[i], wbuf.at[:, place, :], wsem.at[i]))
    for copy in copies:
        copy.start()
    return copies


def back_kernel(groups, per_device, nx, nz, ny, inb, outb, live, *refs):
    low, shards = refs[0], refs[1 : 1 + nz * ny]
    back_same, back_other, wbuf, acc, tin, tout, wsem = refs[1 + nz * ny :]
    copies = load_shards(nz, ny, shards, wbuf, wsem)
    total = list_slots(groups, per_device, inb, outb, live, tin, tout)

    def clear(i, carry):
        acc[i] = jnp.zeros(acc.shape[1:], F32)
        return carry

    lax.fori_loop(0, acc.shape[0], clear, 0)
    for copy in copies:
        copy.wait()

    def body(j, carry):
        back = dot(low[tout[j]], wbuf[j], ((1,), (1,))).astype(BF).astype(F32)
        acc[tin[j]] = acc[tin[j]] + back
        return carry

    lax.fori_loop(0, total, body, 0)

    mx = lax.axis_index("x")
    for sx in range(nx):
        rel = (mx ^ ring_from("x", nx, sx)) * 2

        def spill(b, carry, sx=sx, rel=rel):
            back_same[sx, b] = acc[rel * per_device + b].astype(BF)
            back_other[sx, b] = acc[(rel + 1) * per_device + b].astype(BF)
            return carry

        lax.fori_loop(0, per_device, spill, 0)


def forward_kernel(groups, per_device, nz, ny, inb, outb, live, *refs):
    pieces = refs[:groups]
    start, cot, bias = refs[groups : groups + 3]
    shards = refs[groups + 3 : groups + 3 + nz * ny]
    cross, base, wbuf, sbuf, tin, tout, sem, wsem = refs[groups + 3 + nz * ny :]
    copies = load_shards(nz, ny, shards, wbuf, wsem)
    total = fetch_inputs(groups, per_device, inb, outb, live, pieces, sbuf, tin, tout, sem)

    def begin(b, carry):
        base[b] = jnp.broadcast_to(bias[b], base.shape[1:])
        return carry

    lax.fori_loop(0, per_device, begin, 0)
    for copy in copies:
        copy.wait()

    def body(j, carry):
        wait_input(pieces, sbuf, sem, j)
        part = dot(sbuf[j], wbuf[j], ((1,), (0,))).astype(BF).astype(F32)
        base[tout[j]] = base[tout[j]] + part
        return carry

    lax.fori_loop(0, total, body, 0)
    for b in range(per_device):
        wide = start[b].astype(F32)
        mix = base[b]
        c = cot[:, b * BLK : (b + 1) * BLK].astype(F32)
        cross[:, b * BLK : (b + 1) * BLK] = (wide * mix + wide).astype(BF)
        base[b] = c * mix + c


def pre_kernel(base, own, here, far, slope, low):
    grad = base[0] + own[0, 0].astype(F32) + here[0, 0].astype(F32) + far[0].astype(F32)
    grad = grad * slope[0]
    low[0] = grad.astype(BF)


def turn_kernel(nz, near, others, turned):
    count = near.shape[0]
    for s in range(nz):
        dense = near[...] if s == 0 else others[s - 1]
        turned[:, s * count : (s + 1) * count] = dense.astype(F32).T.astype(BF)


def weight_grad_kernel(nz, ny, rows, *refs):
    grads, (turned, own, send, joined) = refs[:nz], refs[nz:]
    count = grads[0].shape[1]
    for s in range(nz):
        joined[s * count : (s + 1) * count, :] = grads[s][0]
    column = jnp.sum(joined[...].astype(F32), axis=0, keepdims=True)
    high = column.astype(BF).astype(F32)
    place = lax.broadcasted_iota(jnp.int32, (EXTRA, BLK), 0)
    own[rows:, :] = jnp.where(place == 0, column, 0.0)
    extra = jnp.where(place == 0, high, jnp.where(place == 1, column - high, 0.0)).astype(BF)
    for sy in range(ny):
        place = pl.ds(pl.multiple_of(ring_from("y", ny, sy) * rows, rows), rows)
        total = dot(turned[place, :], joined[...], ((1,), (0,)))
        if sy == 0:
            own[:rows, :] = total
        else:
            send[sy - 1, :rows, :] = total.astype(BF)
            send[sy - 1, rows:, :] = extra


def final_kernel(rows, parts, *refs):
    own, far = refs[:parts], refs[parts : 2 * parts]
    out, bias = refs[-2:]
    size = out.shape[1] // parts
    for c in range(parts):
        cols = slice(c * size, (c + 1) * size)
        out[:, cols] = own[c][:rows, :] + far[c][0, :rows, :].astype(F32)
        low = jnp.sum(far[c][0, rows:, :].astype(F32), axis=0, keepdims=True)
        bias[:, cols] = own[c][rows : rows + 1, :] + low


def on_device(sizes, *args):
    dense, bottom_weight, bottom_bias, cross_blocks, cross_bias, cotangent, inb, outb, live = args
    nz, ny, nx = sizes
    groups = nx * 2
    row_count, depth = dense.shape
    local_width = bottom_weight.shape[1]
    per_device = local_width // BLK
    capacity = -(-SLOTS // groups)
    rows = cross_blocks.shape[1]
    n_dp = nz * ny
    out_rows = depth // n_dp
    plane = ny * out_rows
    smem = pltpu.SMEM
    tables = (inb, outb, live)
    sds = jax.ShapeDtypeStruct
    flip = [(0, 1), (1, 0)]

    def table_call(kernel, n_in, out_shape, scratch=(), in_specs=None, out_specs=None):
        single = not isinstance(out_shape, (tuple, list))
        return pl.pallas_call(
            kernel,
            out_shape=out_shape,
            grid_spec=pltpu.PrefetchScalarGridSpec(
                num_scalar_prefetch=3,
                grid=(),
                in_specs=in_specs or [VMEM] * n_in,
                out_specs=out_specs or (VMEM if single else [VMEM] * len(out_shape)),
                scratch_shapes=list(scratch),
            ),
            compiler_params=params(),
        )

    def swap(value, kk):
        return lax.ppermute(value, ("x", "core"), [(i, i ^ kk) for i in range(groups)])

    *packed, most = table_call(
        functools.partial(pack_kernel, groups, per_device),
        1,
        [sds((capacity, rows, BLK), BF)] * groups + [sds((1,), jnp.int32)],
        [smem((groups,), jnp.int32)],
        out_specs=[VMEM] * groups + [pl.BlockSpec(memory_space=smem)],
    )(*tables, cross_blocks)
    moved = [packed[0]] + [swap(packed[kk], kk) for kk in range(1, groups)]

    order = ring_order(nz)

    dense_tied = after(dense, packed[0])
    block = lambda dtype: pl.BlockSpec((1, row_count, BLK), lambda i: (i, 0, 0))
    line = pl.BlockSpec((1, BLK), lambda i: (0, i))
    wide = sds((per_device, row_count, BLK), F32)
    narrow = sds((per_device, row_count, BLK), BF)
    start, low, slope, bias_mixed = pl.pallas_call(
        bottom_kernel,
        grid=(per_device,),
        in_specs=[
            pl.BlockSpec((row_count, depth), lambda i: (0, 0)),
            pl.BlockSpec((depth, BLK), lambda i: (0, i)),
            line,
            pl.BlockSpec((row_count, BLK), lambda i: (0, i)),
        ],
        out_specs=[block(BF), block(BF), block(F32), line],
        out_shape=[narrow, narrow, wide, sds((1, local_width), F32)],
        compiler_params=params(("arbitrary",)),
    )(dense_tied, bottom_weight, bottom_bias.reshape(1, -1), cotangent)

    def rest(width, *operands):
        dense, start, low, slope, bias_mixed, cotangent, cross_bias = operands[:7]
        tables = operands[7:10]
        moved = operands[10:]
        half = width // 2
        shard = table_call(
            functools.partial(compact_kernel, groups, per_device),
            groups,
            sds((width, rows, BLK), BF),
        )(*tables, *moved)

        far = lax.ppermute(start, "x", flip) if nx == 2 else None

        def gather_start(gate):
            if nx != 2:
                return [start] + [swap(start, kk) for kk in range(1, groups)]
            late = after(far, gate)
            return [start, lax.ppermute(start, "core", flip), far, lax.ppermute(late, "core", flip)]

        shards, z_pieces = [], []
        for i in range(nz):
            if i == 0:
                piece = shard
            else:
                source = z_pieces[-1] if i < 2 else after(z_pieces[-1], shards[(i - 1) * ny - 1])
                piece = lax.ppermute(source, "z", ring_hop(nz))
            z_pieces.append(piece)
            shards += ring_gather(after(piece, shards[-1]) if i >= 2 else piece, "y", ny)

        dense_late = after(dense, shards[2 * ny - 1])
        bias_high = bias_mixed.astype(BF).astype(F32)
        bias_rows = jnp.concatenate([bias_high, bias_mixed - bias_high]).astype(BF)
        share = plane // groups
        bias_rows = bias_rows.reshape(-1, share)
        mail = []
        for s in range(1, nz):
            place = ring_from("z", nz, -s) * plane + tensor_index() * share
            cut = lax.dynamic_slice_in_dim(dense_late, place, share, 1)
            hop = [(order[p], order[(p + s) % nz]) for p in range(nz)]
            mail.append(lax.ppermute(jnp.concatenate([cut, bias_rows]), "z", hop))
        dense_near = lax.dynamic_slice_in_dim(dense_late, lax.axis_index("z") * plane, plane, 1)
        shares = jnp.stack([m[:row_count] for m in mail])
        dense_far = lax.all_gather(shares, ("x", "core"), axis=2, tiled=True)
        bias = bias_mixed
        for m in mail:
            terms = m[row_count:].reshape(2, local_width).astype(F32)
            bias = bias + (terms[0:1] + terms[1:2])
        bias_ys = ring_gather(bias, "y", ny)[1:]


        pieces = gather_start(z_pieces[min(2, nz - 1)])
        tabs = [smem((width,), jnp.int32), smem((width,), jnp.int32)]
        sem = pltpu.SemaphoreType.DMA((width,))
        sbuf = pltpu.VMEM((width, row_count, BLK), BF)
        wbuf = pltpu.VMEM((width, BLK, BLK), BF)
        wsem = pltpu.SemaphoreType.DMA((n_dp,))
        grads = table_call(
            functools.partial(block_grad_kernel, groups, per_device, half, nz, ny),
            groups + 1,
            [sds((ny, half, rows, BLK), BF)] * nz + [sds((nz, width - half, rows, BLK), BF)] * ny,
            [sbuf, pltpu.VMEM((BLK, BLK), BF)] + tabs + [sem],
            in_specs=[ANY] * groups + [VMEM],
        )(*tables, *pieces, low)
        z_first, y_first = list(grads[:nz]), list(grads[nz:])
        hop_z = lambda term: lax.ppermute(term, "z", ring_hop(nz))
        hop_y = lambda term: lax.ppermute(term, "y", ring_hop(ny))
        add = lambda a, b: (a.astype(F32) + b.astype(F32)).astype(BF)
        z_carried = hop_z(z_first[1])
        y_carried = hop_y(after(y_first[1], shards[-1]))

        low_late = after(low, z_first[1], shares)
        back = sds((nx, per_device, row_count, BLK), BF)
        back_same, back_other = table_call(
            functools.partial(back_kernel, groups, per_device, nx, nz, ny),
            1 + n_dp,
            [back, back],
            [wbuf, pltpu.VMEM((groups * per_device, row_count, BLK), F32)] + tabs + [wsem],
            in_specs=[VMEM] + [ANY] * n_dp,
        )(*tables, low_late, *shards)
        across = lax.ppermute(back_other, "core", flip)

        start_late = after(start, back_other)
        cross_out, base = table_call(
            functools.partial(forward_kernel, groups, per_device, nz, ny),
            groups + 3 + n_dp,
            [sds((row_count, local_width), BF), wide],
            [wbuf, sbuf] + tabs + [sem, wsem],
            in_specs=[ANY] * groups + [VMEM] * 3 + [ANY] * n_dp,
        )(*tables, *pieces, start_late, cotangent, cross_bias.reshape(per_device, 1, BLK), *shards)

        across = after(across, base)
        if nz > 2:
            z_carried = hop_z(add(z_first[2], after(z_carried, base)))

        chunks = 4 if per_device % 4 == 0 else 1
        span = per_device // chunks
        plain = pl.BlockSpec((1, row_count, BLK), lambda i: (i, 0, 0))
        x_parts = []
        for c in range(chunks):
            sl = slice(c * span, (c + 1) * span)
            carried = None
            for sx in range(1, nx):
                term = back_same[sx, sl].astype(F32) + across[sx, sl].astype(F32)
                if carried is not None:
                    term = term + carried.astype(F32)
                term = term.astype(BF)
                carried = lax.ppermute(term, "x", ring_hop(nx))
            x_parts.append(carried)
            if c == min(1, chunks - 1):
                x_sent = term

        for s in range(3, nz):
            z_carried = hop_z(add(z_first[s], after(z_carried, x_sent)))
        for s in range(2, ny):
            y_carried = hop_y(add(y_first[s], y_carried))
        y_sum = add(y_first[0], after(y_carried, x_sent))
        second = hop_z(y_sum[1])

        grad_lows = []
        for c in range(chunks):
            first_block = c * span
            carried = x_parts[c]
            shifted = pl.BlockSpec((1, row_count, BLK), lambda i, f=first_block: (i + f, 0, 0))
            own_spec = pl.BlockSpec((1, 1, row_count, BLK), lambda i, f=first_block: (0, i + f, 0, 0))
            grad_low = pl.pallas_call(
                pre_kernel,
                grid=(span,),
                in_specs=[shifted, own_spec, own_spec, plain, shifted],
                out_specs=plain,
                out_shape=sds((span, row_count, BLK), BF),
                compiler_params=params(("arbitrary",)),
            )(base, back_same, across, carried, slope)
            grad_lows.append(grad_low)

        first_hops = [hop_z(g) for g in grad_lows[:2]]
        if nz > 2:
            second = hop_z(add(y_sum[2], second))
        first = add(z_first[0], after(z_carried, first_hops[-1]))
        first_far = hop_y(first[1])
        for s in range(2, ny):
            first_far = hop_y(add(first[s], first_far))

        turned = pl.pallas_call(
            functools.partial(turn_kernel, nz),
            in_specs=[VMEM, VMEM],
            out_specs=VMEM,
            out_shape=sds((plane, nz * row_count), BF),
            compiler_params=params(),
        )(dense_near, dense_far)
        owns, fars, ends = [], [], []
        for c in range(chunks):
            gathered = [grad_lows[c]]
            for s in range(1, nz):
                source = gathered[-1]
                if c >= 2:
                    source = after(source, (ends, owns, fars)[min(s - 1, 2)][c - 2])
                hop = first_hops[c] if s == 1 and c < len(first_hops) else hop_z(source)
                gathered.append(hop)
            ends.append(gathered[-1])
            near = after(turned, *bias_ys) if c == 0 else turned
            if c == chunks - 1:
                second = add(y_sum[0], after(second, *owns[:2], *gathered[2:3]))
                first = add(first[0], after(first_far, *owns[:2]))
                returned = table_call(
                    functools.partial(expand_kernel, groups, per_device, half),
                    2,
                    [sds((capacity, rows, BLK), BF)] * groups,
                )(*tables, first, second)
                near = after(turned, returned[0])
                returned = [returned[0]] + [swap(returned[kk], kk) for kk in range(1, groups)]
            own, send = pl.pallas_call(
                functools.partial(weight_grad_kernel, nz, ny, out_rows),
                grid=(span,),
                in_specs=[plain] * nz
                + [pl.BlockSpec((plane, nz * row_count), lambda i: (0, 0))],
                out_specs=[
                    pl.BlockSpec((out_rows + EXTRA, BLK), lambda i: (0, i)),
                    pl.BlockSpec((ny - 1, out_rows + EXTRA, BLK), lambda i: (0, 0, i)),
                ],
                out_shape=[
                    sds((out_rows + EXTRA, span * BLK), F32),
                    sds((ny - 1, out_rows + EXTRA, span * BLK), BF),
                ],
                scratch_shapes=[
                    pltpu.VMEM((nz * row_count, BLK), BF),
                ],
                compiler_params=params(("arbitrary",)),
            )(*gathered, near)
            carried = None
            for sy in range(1, ny):
                term = send[sy - 1 : sy]
                if carried is not None:
                    term = (term.astype(F32) + carried.astype(F32)).astype(BF)
                carried = lax.ppermute(term, "y", ring_hop(ny))
            owns.append(own)
            fars.append(carried)
            if c == min(1, chunks - 1):
                for q in range(3, nz):
                    second = hop_z(add(y_sum[q], after(second, own)))

        grad_blocks = table_call(
            functools.partial(return_kernel, groups, per_device),
            groups,
            sds((SLOTS, rows, BLK), F32),
            [smem((groups,), jnp.int32)],
        )(*tables, returned[0], *[after(r, owns[-1]) for r in returned[1:]])

        size = span * BLK
        outs = [sds((out_rows, local_width), F32), sds((1, local_width), F32)]
        done = None
        groups_of = [range(chunks)] if chunks == 1 else [range(chunks // 2), range(chunks // 2, chunks)]
        for place, group in enumerate(groups_of):
            parts_in = [owns[c] for c in group] + [fars[c] for c in group]
            total = len(group) * size
            done = pl.pallas_call(
                functools.partial(final_kernel, out_rows, len(group)),
                grid=(1,),
                in_specs=[pl.BlockSpec(p.shape, lambda i, n=p.ndim: (0,) * n) for p in parts_in]
                + ([ANY, ANY] if done else []),
                out_specs=[
                    pl.BlockSpec((out_rows, total), lambda i, place=place: (0, place)),
                    pl.BlockSpec((1, total), lambda i, place=place: (0, place)),
                ],
                out_shape=outs,
                input_output_aliases={len(parts_in): 0, len(parts_in) + 1: 1} if done else {},
                compiler_params=params(("arbitrary",)),
            )(*parts_in, *(done or ()))
        grad_bottom, bias_pre = done

        for piece in bias_ys:
            bias = bias + piece
        return cross_out, grad_bottom, bias_pre.reshape(-1), grad_blocks, bias.reshape(-1)

    most_slots = groups * capacity
    widths = sorted({-(-most_slots * 2 // 3), -(-most_slots * 5 // 6), most_slots})
    which = sum((most[0] > w).astype(jnp.int32) for w in widths[:-1])
    return lax.switch(
        which,
        [functools.partial(rest, w) for w in widths],
        dense,
        start,
        low,
        slope,
        bias_mixed,
        cotangent,
        cross_bias,
        *tables,
        *moved,
    )


def solution(mesh):
    n_dp, groups = mesh.devices.shape
    nx = groups // 2
    ny = nx if n_dp % nx == 0 else 1
    nz = n_dp // ny
    fine = Mesh(mesh.devices.reshape(nz, ny, nx, 2), ("z", "y", "x", "core"))
    dp, tensor = ("z", "y"), ("x", "core")
    return jax.shard_map(
        functools.partial(on_device, (nz, ny, nx)),
        mesh=fine,
        in_specs=(
            P(dp, None),
            P(None, tensor),
            P(tensor),
            P(tensor, dp, None),
            P(tensor),
            P(dp, tensor),
            P(),
            P(),
            P(),
        ),
        out_specs=(
            P(dp, tensor),
            P(dp, tensor),
            P(tensor),
            P(tensor, dp, None),
            P(tensor),
        ),
        check_vma=False,
    )
```
